128 devices in a mesh: teacher: 16 (over z, x), student: 8 (over y, core).
Axes of the slice: x: 4, y: 4, z: 4, core: 2. Of those that a mesh axis runs over, the one named last changes fastest.
Arguments:
- embeddings: bfloat16 [131072, 1024], P(('teacher', 'student')), may hold values from -6 to 6
- action_ids: int32 [131072], P(('teacher', 'student')), may hold values from 0 to 15
- segment_ids: int32 [128, 1024], P(('teacher', 'student')), may hold values from 0 to 7, never falling along the last dimension, each value on 1 to 512 neighbouring positions
- cand_pos: int32 [32768], P(('teacher', 'student')), may hold values from 0 to 1023
- owners: int32 [32768, 1], P(('teacher', 'student')), may hold values from 0 to 15; in each aligned block of 256 rows (0 to 255, 256 to 511, ...) at most 32 rows name the same one
- features: bfloat16 [32768, 512], P(('teacher', 'student')), may hold values from -6 to 6
- action_table: bfloat16 [16, 1024], replicated, may hold values from -3 to 3
- w_query: bfloat16 [1024, 2048], P('teacher'), may hold values from -0.1875 to 0.1875
- w_keys: bfloat16 [1024, 2048], P('teacher'), may hold values from -0.1875 to 0.1875
- w_out: bfloat16 [1024, 1024], P('teacher'), may hold values from -0.1875 to 0.1875
- w_head: bfloat16 [1024, 128], replicated, may hold values from -0.1875 to 0.1875
- w_cross: bfloat16 [512, 512], replicated, may hold values from -0.25 to 0.25
- b_cross: bfloat16 [512], replicated, may hold values from -3 to 3
- w_deep: bfloat16 [512, 4096], replicated, may hold values from -0.25 to 0.25
- b_deep: bfloat16 [4096], replicated, may hold values from -3 to 3
- w_score: bfloat16 [4096, 128], replicated, may hold values from -0.09375 to 0.09375
- b_score: bfloat16 [128], replicated, may hold values from -3 to 3
Outputs:
- grad_cross: float32 [512, 512], P(('teacher', 'student'))
- grad_bcross: float32 [512], P(('teacher', 'student'))
- grad_deep: float32 [512, 4096], P(('teacher', 'student'))
- grad_bdeep: float32 [4096], P(('teacher', 'student'))
- grad_score: float32 [4096, 128], P(('teacher', 'student'))
- grad_bscore: float32 [128], P(('teacher', 'student'))
- student_rows: bfloat16 [65536, 128], P(('teacher', 'student'))
The draws below stay inside these ranges and needn't reach their ends.
Inputs may be any that keep to these rules, and one draw needn't show every extreme that they name: `owners`: within the candidates of one device, no owner is named by more than 32 of them, a bound that some block reaches.
All inputs are finite; a program needn't handle non-finite values.
Results may differ from the reference program's by a relative error of at most 0.012.
Values may be sent and summed in bfloat16 or wider, within the bound.
A program may use at most 128 MiB of HBM per device.

```python
import math
import jax
import jax.numpy as jnp
import numpy as np
from jax import lax

D = 1024
HEADS = 8
ACTIONS = 16
LOGITS = 128
F_IN = 512
DEEP = 4096
ROWS_DEV = 1024
USERS_DEV = 8
MOST_LEN = 512
CAND_DEV = 256
CAP = 32
TOKENS = 131072
CANDS = 32768
SLOTS = 65536
N_TEACHER = 16
N_STUDENT = 8
DEVICES = 128


def set_ends(values, rng, least, top_value):
    place = [jax.random.randint(jax.random.fold_in(rng, axis), (), 0, length) for axis, length in enumerate(values.shape)]
    longest = values.shape.index(max(values.shape))
    beside = place[:longest] + [(place[longest] + 1) % values.shape[longest]] + place[longest + 1:]
    return values.at[tuple(place)].set(least).at[tuple(beside)].set(top_value)


def block_scale(rng, dims, shards, low, largest):
    def one(dim, parts):
        draws = jax.random.uniform(jax.random.fold_in(jax.random.fold_in(rng, 6), dim), (parts,), jnp.float32, low / len(shards), largest / len(shards))
        return jnp.repeat(jnp.exp(draws), dims[dim] // parts).reshape((-1,) + (1,) * (len(dims) - dim - 1))

    loudness = one(*shards[0])
    for cut in shards[1:]:
        loudness = loudness * one(*cut)
    return loudness


def profile(amount, total, reach, slope):
    portions = [(1 << 20) // math.isqrt(rank ** slope) + 1 for rank in range(2, amount + 1)]
    surplus, counts = total - reach - (amount - 1), [1] * (amount - 1)
    while surplus > 0:
        candidates = [i for i in range(amount - 1) if counts[i] < reach]
        whole, remaining = sum([portions[i] for i in candidates]), surplus
        for i in candidates:
            addition = min(reach - counts[i], max(1, remaining * portions[i] // whole), surplus)
            counts[i] = counts[i] + addition
            surplus = surplus - addition
    return np.array([reach] + counts)


def ragged(key, count, total, bound, skew):
    if count == 2:
        one = jax.random.randint(key, (), max(1, total - bound), min(bound, total - 1) + 1)
        return jnp.stack([one, total - one])
    sizes = jnp.asarray(profile(count, total, bound, skew), jnp.int32)
    twos = (count - 1) // 2
    source_of, sink = sizes[1:1 + 2 * twos:2], sizes[2:2 + 2 * twos:2]
    margin = jnp.minimum(source_of - 1, bound - sink)
    moved = jax.random.randint(jax.random.fold_in(key, 1), (twos,), 0, 1 << 20) % (margin + 1)
    sizes = sizes.at[1:1 + 2 * twos:2].set(source_of - moved).at[2:2 + 2 * twos:2].set(sink + moved)
    return sizes[jax.random.permutation(jax.random.fold_in(key, 2), count)]


def assign_block(own_key, own, number, rows, count, top, most, skew):
    order = jax.random.permutation(own_key, count)
    packed, usual = shares(count, rows * top, most, skew, True), shares(count, rows * top, most, skew, False)
    places = jnp.arange(count)

    def named(sizes, turn):
        used = int((sizes > 0).sum())
        fixed = max(1, used // 4)
        moved = fixed + (places - fixed + turn * (used - fixed)) % max(1, count - fixed)
        return jnp.zeros((count,), jnp.int32).at[order[jnp.where(places < fixed, places, moved)]].set(jnp.asarray(sizes, jnp.int32))

    sizes = jnp.where(number % 4 == 0, named(packed, number // 4), named(usual, number - number // 4 - 1))
    mixed = jax.random.permutation(jax.random.fold_in(own, 3), count)
    donor, sink = mixed[0:count // 2 * 2:2], mixed[1:count // 2 * 2:2]
    room = jnp.minimum(sizes[donor] - 1, most - sizes[sink]) // 2
    room = jnp.where((donor == order[0]) | (sink == order[0]) | (sizes[sink] == 0), 0, jnp.maximum(room, 0))
    moved = jax.random.randint(jax.random.fold_in(own, 4), (count // 2,), 0, 1 << 20) % (room + 1)
    sizes = sizes.at[donor].add(-moved).at[sink].add(moved)
    members = jnp.searchsorted(jnp.cumsum(sizes), jnp.arange(rows * top), side="right").astype(jnp.int32)
    listing = members.reshape(top, rows).T
    listing = listing[jax.random.permutation(jax.random.fold_in(own, 1), rows)]
    turn = jax.random.randint(jax.random.fold_in(own, 2), (rows, 1), 0, top)
    return jnp.take_along_axis(listing, (jnp.arange(top)[None, :] + turn) % top, axis=1)


def shares(count, total, limit, skew, full):
    portions = [(1 << 20) // math.isqrt(rank ** skew) + 1 for rank in range(1, count + 1)]
    largest = limit if full else min(limit, max(-(-total // count), total * portions[0] // sum(portions)))
    least = 1 if total - largest >= count - 1 else 0
    given, spare = [largest] + [least] * (count - 1), total - largest - least * (count - 1)
    while spare > 0:
        free = [i for i in range(1, count) if given[i] < largest] or [i for i in range(1, count) if given[i] < limit]
        whole, remaining = sum([portions[i] for i in free]), spare
        for i in free:
            extra = min(limit - given[i], max(1, remaining * portions[i] // whole), spare)
            given[i] = given[i] + extra
            spare = spare - extra
    return np.array(given)


def gaussian(stream_key, extent, scale, bound, split=(), kind=jnp.bfloat16):
    result = jax.random.normal(stream_key, extent, jnp.float32) * scale
    if len(split) > 0:
        result = block_scale(stream_key, extent, split, -0.22, 0.18) * result
    return jnp.clip(result, min=-bound, max=bound).astype(kind)


def setup_inputs(seed: int = 0) -> dict:
    seeds = jax.random.split(jax.random.key(seed), 18)
    embeddings = gaussian(seeds[0], (TOKENS, D), 1.0, 6.0, ((0, 128),))
    action_ids = set_ends(jax.random.randint(seeds[1], (TOKENS,), 0, ACTIONS), jax.random.fold_in(seeds[1], 1), 0, ACTIONS - 1).astype(jnp.int32)
    segment_ids = jax.vmap(lambda own: jnp.searchsorted(jnp.cumsum(ragged(own, USERS_DEV, ROWS_DEV, MOST_LEN, 2)), jnp.arange(ROWS_DEV), side="right"))(jax.random.split(seeds[2], DEVICES)).reshape((DEVICES, ROWS_DEV)).astype(jnp.int32)
    cand_pos = set_ends(jax.random.randint(seeds[3], (CANDS,), 0, ROWS_DEV), jax.random.fold_in(seeds[3], 1), 0, ROWS_DEV - 1).astype(jnp.int32)
    owners_keys = jax.random.split(jax.random.fold_in(seeds[4], 1), CANDS // CAND_DEV)
    owners_turns = jax.random.permutation(jax.random.fold_in(seeds[4], 3), CANDS // CAND_DEV)
    owners = jax.vmap(lambda own, number: assign_block(jax.random.fold_in(seeds[4], 2), own, number, CAND_DEV, N_TEACHER, 1, CAP, 2))(owners_keys, owners_turns).reshape((CANDS, 1))
    features = gaussian(seeds[5], (CANDS, F_IN), 1.0, 6.0, ((0, 128),))
    action_table = gaussian(seeds[6], (ACTIONS, D), 0.5, 3.0)
    w_query = gaussian(seeds[7], (D, 2 * D), D ** -0.5, 0.1875, ((0, 16),))
    w_keys = gaussian(seeds[8], (D, 2 * D), D ** -0.5, 0.1875, ((0, 16),))
    w_out = gaussian(seeds[9], (D, D), D ** -0.5, 0.1875, ((0, 16),))
    w_head = gaussian(seeds[10], (D, LOGITS), D ** -0.5, 0.1875)
    w_cross = gaussian(seeds[11], (F_IN, F_IN), F_IN ** -0.5, 0.25)
    b_cross = gaussian(seeds[12], (F_IN,), 0.5, 3.0)
    w_deep = gaussian(seeds[13], (F_IN, DEEP), F_IN ** -0.5, 0.25)
    b_deep = gaussian(seeds[14], (DEEP,), 0.5, 3.0)
    w_score = gaussian(seeds[15], (DEEP, LOGITS), DEEP ** -0.5, 0.09375)
    b_score = gaussian(seeds[16], (LOGITS,), 0.5, 3.0)
    return {"embeddings": embeddings, "action_ids": action_ids, "segment_ids": segment_ids, "cand_pos": cand_pos, "owners": owners, "features": features, "action_table": action_table, "w_query": w_query, "w_keys": w_keys, "w_out": w_out, "w_head": w_head, "w_cross": w_cross, "b_cross": b_cross, "w_deep": w_deep, "b_deep": b_deep, "w_score": w_score, "b_score": b_score}


EPS = 1e-05

def action_embed(embeddings, action_ids, action_table):
    kinds = jnp.arange(action_table.shape[0], dtype=jnp.int32)
    onehot = (action_ids[:, None] == kinds[None, :]).astype(jnp.bfloat16)
    added = embeddings.astype(jnp.float32) + jnp.dot(onehot, action_table, preferred_element_type=jnp.float32)
    return added.astype(jnp.bfloat16)

def candidate_attention(key_rows, query_rows, segments, positions):
    rows = key_rows.shape[0]
    picks = query_rows.shape[0]
    width = key_rows.shape[1] // 2
    head_size = width // HEADS
    values = key_rows[:, :width].reshape(rows, HEADS, head_size).astype(jnp.float32)
    keys = key_rows[:, width:].reshape(rows, HEADS, head_size).astype(jnp.float32)
    gate = query_rows[:, :width].astype(jnp.float32)
    queries = query_rows[:, width:].reshape(picks, HEADS, head_size).astype(jnp.float32)
    scores = jnp.einsum('chd,rhd->hcr', queries, keys) * head_size ** (-0.5)
    owner_seg = jnp.take(segments, positions)
    places = jnp.arange(rows, dtype=jnp.int32)
    allowed = (segments[None, :] == owner_seg[:, None]) & (places[None, :] <= positions[:, None])
    weights = jnp.where(allowed[None], jax.nn.silu(scores), 0.0).astype(jnp.bfloat16)
    mixed = jnp.einsum('hcr,rhd->chd', weights.astype(jnp.float32), values).reshape(picks, width)
    centre = lax.optimization_barrier(jnp.mean(mixed, axis=1, keepdims=True))
    spread = lax.optimization_barrier(jnp.mean(jnp.square(mixed - centre), axis=1, keepdims=True))
    normed = (mixed - centre) * lax.rsqrt(spread + EPS)
    return (normed * gate).astype(jnp.bfloat16)

def student_terms(inputs, target, valid, w_cross, b_cross, w_deep, b_deep, w_score, b_score):
    inputs32 = inputs.astype(jnp.float32)
    cross = jnp.dot(inputs, w_cross, preferred_element_type=jnp.float32) + b_cross.astype(jnp.float32)
    crossed = (inputs32 * cross + inputs32).astype(jnp.bfloat16)
    pre = jnp.dot(crossed, w_deep, preferred_element_type=jnp.float32) + b_deep.astype(jnp.float32)
    hidden = jax.nn.silu(pre).astype(jnp.bfloat16)
    scores = jnp.dot(hidden, w_score, preferred_element_type=jnp.float32) + b_score.astype(jnp.float32)
    mask = valid.astype(jnp.float32)[:, None]
    delta = (scores - target.astype(jnp.float32)) * mask
    delta16 = delta.astype(jnp.bfloat16)
    g_score = jnp.dot(hidden.T, delta16, preferred_element_type=jnp.float32)
    g_bscore = lax.optimization_barrier(jnp.sum(delta, axis=0))
    back = jnp.dot(delta16, w_score.T, preferred_element_type=jnp.float32)
    sigma = jax.nn.sigmoid(pre)
    dpre = back * (sigma + pre * sigma * (1.0 - sigma))
    dpre16 = dpre.astype(jnp.bfloat16)
    g_deep = jnp.dot(crossed.T, dpre16, preferred_element_type=jnp.float32)
    g_bdeep = lax.optimization_barrier(jnp.sum(dpre, axis=0))
    dcross = jnp.dot(dpre16, w_deep.T, preferred_element_type=jnp.float32) * inputs32
    dcross16 = dcross.astype(jnp.bfloat16)
    g_cross = jnp.dot(inputs.T, dcross16, preferred_element_type=jnp.float32)
    g_bcross = lax.optimization_barrier(jnp.sum(dcross, axis=0))
    rows_out = (scores * mask).astype(jnp.bfloat16)
    return ((g_cross, g_bcross, g_deep, g_bdeep, g_score, g_bscore), rows_out)

def reference(embeddings, action_ids, segment_ids, cand_pos, owners, features, action_table, w_query, w_keys, w_out, w_head, w_cross, b_cross, w_deep, b_deep, w_score, b_score):

    def step(carry, index):
        row_start = index * ROWS_DEV
        cand_start = index * CAND_DEV
        emb = lax.dynamic_slice_in_dim(embeddings, row_start, ROWS_DEV, 0)
        acts = lax.dynamic_slice_in_dim(action_ids, row_start, ROWS_DEV, 0)
        segs = lax.dynamic_slice_in_dim(segment_ids, index, 1, 0)[0]
        picks = lax.dynamic_slice_in_dim(cand_pos, cand_start, CAND_DEV, 0)
        feats = lax.dynamic_slice_in_dim(features, cand_start, CAND_DEV, 0)
        mine = action_embed(emb, acts, action_table)
        picked = jnp.take(mine, picks, axis=0)
        key_rows = jax.nn.silu(jnp.dot(mine, w_keys, preferred_element_type=jnp.float32)).astype(jnp.bfloat16)
        query_rows = jax.nn.silu(jnp.dot(picked, w_query, preferred_element_type=jnp.float32)).astype(jnp.bfloat16)
        mixed = candidate_attention(key_rows, query_rows, segs, picks)
        joined = (picked.astype(jnp.float32) + jnp.dot(mixed, w_out, preferred_element_type=jnp.float32)).astype(jnp.bfloat16)
        logits = jnp.dot(joined, w_head, preferred_element_type=jnp.float32).astype(jnp.bfloat16)
        valid = jnp.ones((CAND_DEV,), jnp.bfloat16)
        terms, rows_out = student_terms(feats, logits, valid, w_cross, b_cross, w_deep, b_deep, w_score, b_score)
        return (tuple((a + b for a, b in zip(carry, terms))), rows_out)
    init = (jnp.zeros((F_IN, F_IN), jnp.float32), jnp.zeros((F_IN,), jnp.float32), jnp.zeros((F_IN, DEEP), jnp.float32), jnp.zeros((DEEP,), jnp.float32), jnp.zeros((DEEP, LOGITS), jnp.float32), jnp.zeros((LOGITS,), jnp.float32))
    sums, scores = lax.scan(step, init, jnp.arange(DEVICES, dtype=jnp.int32))
    scale = 1.0 / (CAND_DEV * DEVICES)
    grads = tuple((s * scale for s in sums))
    dest = owners[:, 0].reshape(DEVICES, CAND_DEV)
    hits = (dest[:, :, None] == jnp.arange(N_TEACHER, dtype=jnp.int32)[None, None, :]).astype(jnp.int32)
    rank = lax.optimization_barrier(jnp.sum((jnp.cumsum(hits, axis=1) - hits) * hits, axis=2))
    source = jnp.arange(DEVICES, dtype=jnp.int32)
    src_teacher = source // N_STUDENT
    src_student = source % N_STUDENT
    target_row = (dest * N_STUDENT + src_student[:, None]) * (N_TEACHER * CAP) + src_teacher[:, None] * CAP + rank
    student_rows = jnp.zeros((SLOTS, LOGITS), jnp.bfloat16).at[target_row.reshape(-1)].set(scores.reshape(-1, LOGITS))
    return (grads[0], grads[1], grads[2], grads[3], grads[4], grads[5], student_rows)
```

```python
import functools

import jax
import jax.numpy as jnp
from jax import lax
from jax.experimental import pallas as pl
from jax.experimental.pallas import tpu as pltpu
from jax.sharding import PartitionSpec as P

HEADS = 8
CAP = 32
EPS = 1e-05
BF = jnp.bfloat16
F32 = jnp.float32
MESH = pl.DeviceIdType.MESH

ROUTES = ((0, 1, 2), (1, 2, 0), (2, 0, 1))


def nn(a, b):
    return lax.dot_general(a, b, (((1,), (0,)), ((), ())), preferred_element_type=F32)


def nt(a, b):
    return lax.dot_general(a, b, (((1,), (1,)), ((), ())), preferred_element_type=F32)


def silu(v):
    half = 0.5 * v
    return half + half * jnp.tanh(half)


def flip(v):
    return v.astype(F32).T.astype(BF)


def student_kernel(
    logits_ref,
    owners_ref,
    feat_ref,
    w_cross_ref,
    b_cross_ref,
    w_deep_ref,
    b_deep_ref,
    w_score_ref,
    b_score_ref,
    o_cross,
    o_deep,
    o_score,
    o_bias,
    o_rows,
    crossed,
    ct,
    ct_sib,
    ft,
    ft_sib,
    hid_t,
    slope,
    scores,
    place_out,
    rows_in,
    d_own,
    d_sib,
    gs,
    gs_sib,
    dcross,
    dc,
    dc_sib,
    bd,
    grads,
    x1,
    x2,
    x3,
    y3,
    w1,
    v1,
    v2,
    v3,
    u3,
    w2,
    last,
    fin,
    s1s,
    s1r,
    s2s,
    s2r,
    s3s,
    s3r,
    scs,
    scr,
    srs,
    srr,
):
    t = lax.axis_index("teacher")
    s = lax.axis_index("student")
    z, x = t // 4, t % 4
    y, c = s // 2, s % 2
    pos = (z, x, y)
    sibling = (t, y * 2 + 1 - c)
    sends = []

    def at_chip(axis, value, core):
        p = list(pos)
        p[axis] = value
        return (p[0] * 4 + p[1], p[2] * 2 + core)

    def push(src, dst, send_sem, recv_sem, device):
        copy = pltpu.make_async_remote_copy(
            src_ref=src,
            dst_ref=dst,
            send_sem=send_sem,
            recv_sem=recv_sem,
            device_id=device,
            device_id_type=MESH,
        )
        copy.start()
        sends.append(copy)
        return copy

    peers = [((t + k) % 16, s) for k in range(1, 16)] + [sibling]
    peers += [at_chip(2, (y + k) % 4, c) for k in range(1, 4)]
    peers += [at_chip(axis, (pos[axis] + k) % 4, 1 - c) for axis in range(3) for k in range(1, 4)]
    barrier = pltpu.get_barrier_semaphore()
    for peer in peers:
        pl.semaphore_signal(barrier, inc=1, device_id=peer, device_id_type=MESH)
    pl.semaphore_wait(barrier, len(peers))

    feats = feat_ref[...]
    feats32 = feats.astype(F32)
    cross = nn(feats, w_cross_ref[...]) + b_cross_ref[...].astype(F32)
    crossed[...] = (feats32 * cross + feats32).astype(BF)
    ct[...] = flip(crossed[...])
    ft[...] = flip(feats)
    ct_copy = push(ct, ct_sib, scs.at[0], scr.at[0], sibling)
    ft_copy = push(ft, ft_sib, scs.at[1], scr.at[1], sibling)
    scores[...] = jnp.broadcast_to(b_score_ref[...].astype(F32), scores.shape)

    def forward(j, carry):
        cols = pl.ds(pl.multiple_of(j * 512, 512), 512)
        pre = nn(crossed[...], w_deep_ref[:, cols]) + b_deep_ref[:, cols].astype(F32)
        sigma = 0.5 + 0.5 * jnp.tanh(0.5 * pre)
        hidden = (pre * sigma).astype(BF)
        slope[j] = sigma * (1.0 + pre * (1.0 - sigma))
        hid_t[cols, :] = flip(hidden)
        scores[...] += nn(hidden, w_score_ref[cols, :])
        return carry

    lax.fori_loop(0, 8, forward, 0)

    dest = owners_ref[...]
    kinds = lax.broadcasted_iota(jnp.int32, (16, 256), 0)
    hits = (kinds == dest).astype(F32)
    upper = (
        lax.broadcasted_iota(jnp.int32, (256, 256), 0)
        < lax.broadcasted_iota(jnp.int32, (256, 256), 1)
    ).astype(BF)
    before = nn(hits.astype(BF), upper)
    rank = jnp.sum(before * hits, axis=0, keepdims=True).astype(jnp.int32)
    slot = dest * CAP + rank
    place = (lax.broadcasted_iota(jnp.int32, (512, 256), 0) == slot).astype(BF)
    placed = nn(place, scores[...].astype(BF)).astype(BF).reshape(16, CAP, 128)
    place_out[...] = placed
    rows_in[t] = place_out[t]
    row_copies = []
    for k in range(1, 16):
        to = (t + k) % 16
        row_copies.append(push(place_out.at[to], rows_in.at[t], srs.at[k], srr.at[k], (to, s)))

    delta = scores[...] - logits_ref[...].astype(F32)
    delta16 = delta.astype(BF)
    bscore = jnp.sum(delta, axis=0, keepdims=True)

    def back_chunk(j):
        rows = pl.ds(pl.multiple_of(j * 512, 512), 512)
        dpre = nt(delta16, w_score_ref[rows, :]) * slope[j]
        d_own[j] = dpre.astype(BF)
        bd[j] = jnp.broadcast_to(jnp.sum(dpre, axis=0, keepdims=True), (8, 512))

    d_copies = []
    for q in range(4):
        j = (1 - c) * 4 + q
        back_chunk(j)
        d_copies.append(push(d_own.at[j], d_sib.at[q], scs.at[2 + q], scr.at[2 + q], sibling))

    def score_grads(i, carry):
        rows = pl.ds(pl.multiple_of(i * 512, 512), 512)
        g = nn(hid_t[rows, :], delta16).astype(BF).reshape(8, 2, 2, 16, 128)
        chips = pl.ds(pl.multiple_of(i * 8, 8), 8)
        for core in range(2):
            gs[core, chips, :, 0:128] = g[:, core, 0]
            gs[core, chips, :, 128:256] = g[:, core, 1]
        return carry

    lax.fori_loop(0, 8, score_grads, 0)
    gs_copy = push(gs.at[1 - c], gs_sib, scs.at[6], scr.at[6], sibling)

    def own_chunk(q, carry):
        back_chunk(c * 4 + q)
        return carry

    lax.fori_loop(0, 4, own_chunk, 0)

    def axes_of(u):
        axis = ROUTES[u // 2][0]
        rest = [a for a in range(3) if a != axis]
        return axis, rest

    def piece(u, where, half):
        axis, rest = axes_of(u)
        index = [slice(None)] * 3
        index[axis] = where
        index[rest[0]] = pl.ds(2 * half, 2)
        return (u, *index)

    def stage1_start(u):
        axis, _ = axes_of(u)
        m = pos[axis]
        right, left, opp = (m + 1) % 4, (m + 3) % 4, (m + 2) % 4
        to_right, to_left = at_chip(axis, right, c), at_chip(axis, left, c)
        return (
            push(grads.at[piece(u, opp, 0)], x1.at[u, 0], s1s.at[u, 0], s1r.at[u, 0], to_right),
            push(grads.at[piece(u, opp, 1)], x1.at[u, 1], s1s.at[u, 1], s1r.at[u, 1], to_left),
            push(grads.at[piece(u, right, 1)], x2.at[u, 0], s1s.at[u, 2], s1r.at[u, 2], to_right),
            push(grads.at[piece(u, left, 0)], x2.at[u, 1], s1s.at[u, 3], s1r.at[u, 3], to_left),
        )

    def stage1_pass(u, started):
        axis, _ = axes_of(u)
        m = pos[axis]
        right, left = (m + 1) % 4, (m + 3) % 4
        out = []
        for side, (where, device) in enumerate(
            ((right, at_chip(axis, right, c)), (left, at_chip(axis, left, c)))
        ):
            started[side].wait_recv()
            mine = grads[piece(u, where, side)].astype(F32)
            y3[u, side] = (mine + x1[u, side].astype(F32)).astype(BF)
            out.append(
                push(y3.at[u, side], x3.at[u, side], s1s.at[u, 4 + side], s1r.at[u, 4 + side], device)
            )
        return out

    def stage1_end(u, started, passed):
        axis, _ = axes_of(u)
        m = pos[axis]
        for copy in (started[2], started[3], passed[0], passed[1]):
            copy.wait_recv()
        for half in range(2):
            total = grads[piece(u, m, half)].astype(F32)
            total += x2[u, 1 - half].astype(F32) + x3[u, half].astype(F32)
            w1[u // 2, u % 2, 2 * half : 2 * half + 2] = total.astype(BF)

    started = {}

    gs_copy.wait_recv()

    def add_scores(i, carry):
        summed = gs[c, pl.ds(i * 16, 16)].astype(F32) + gs_sib[pl.ds(i * 16, 16)].astype(F32)
        grads[0, i] = summed.astype(BF).reshape(4, 4, 16, 256)
        return carry

    lax.fori_loop(0, 4, add_scores, 0)
    started[0] = stage1_start(0)

    ct_copy.wait_recv()
    for q in range(4):
        d_copies[q].wait_recv()

        def deep_grads(i, carry, q=q):
            rows = pl.ds(pl.multiple_of(i * 128, 128), 128)
            g = nn(ct[rows, :], d_own[c * 4 + q]) + nn(ct_sib[rows, :], d_sib[q])
            g = g.reshape(16, 8, 512)
            g = jnp.concatenate([g[:, :, :256], g[:, :, 256:]], axis=1)
            grads[1 + q, i] = g.astype(BF).reshape(4, 4, 16, 256)
            return carry

        lax.fori_loop(0, 4, deep_grads, 0)
        started[1 + q] = stage1_start(1 + q)

    dcross[...] = jnp.zeros_like(dcross)

    def cross_chunk(j, carry):
        cols = pl.ds(pl.multiple_of(j * 512, 512), 512)
        dcross[...] += nt(d_own[j], w_deep_ref[:, cols])
        return carry

    lax.fori_loop(0, 8, cross_chunk, 0)
    dcr = dcross[...] * feats32
    bcross = jnp.sum(dcr, axis=0, keepdims=True)
    dc[0] = dcr[:, :256].astype(BF)
    dc[1] = dcr[:, 256:].astype(BF)
    dc_copy = push(dc.at[1 - c], dc_sib, scs.at[7], scr.at[7], sibling)
    sub = lax.broadcasted_iota(jnp.int32, (16, 128), 0)
    for pair in range(32):
        deep_row = bd[pair // 4, 0:1, (pair % 4) * 128 : (pair % 4) * 128 + 128]
        cross_row = bcross[:, (pair // 8) * 128 : (pair // 8) * 128 + 128]
        tile = jnp.where(sub == 0, deep_row, jnp.where(sub == 1, cross_row, bscore))
        tile = tile.astype(BF)
        for chip in (2 * pair, 2 * pair + 1):
            grads[5, chip // 16, chip // 4 % 4, chip % 4, :, 128:256] = tile
    passed = {}
    for u in range(5):
        passed[u] = stage1_pass(u, started[u])
    ft_copy.wait_recv()
    dc_copy.wait_recv()

    def cross_grads(i, carry):
        rows = pl.ds(pl.multiple_of(i * 128, 128), 128)
        g = nn(ft[rows, :], dc[c]) + nn(ft_sib[rows, :], dc_sib[...])
        g = g.reshape(16, 8, 256)
        g = jnp.concatenate([g[:, :, :128], g[:, :, 128:]], axis=1)
        grads[5, i, :, :, :, 0:128] = g.astype(BF).reshape(4, 4, 16, 128)
        return carry

    lax.fori_loop(0, 4, cross_grads, 0)
    started[5] = stage1_start(5)
    for u in range(4):
        stage1_end(u, started[u], passed[u])

    def piece2(r, where, half):
        axis, second, _ = ROUTES[r]
        rest = [a for a in range(3) if a != axis]
        index = [None, None]
        index[rest.index(second)] = where
        index[1 - rest.index(second)] = pl.ds(2 * half, 2)
        return (r, slice(None), *index)

    def stage2_start(r):
        axis = ROUTES[r][1]
        m = pos[axis]
        right, left, opp = (m + 1) % 4, (m + 3) % 4, (m + 2) % 4
        to_right, to_left = at_chip(axis, right, c), at_chip(axis, left, c)
        return (
            push(w1.at[piece2(r, opp, 0)], v1.at[r, 0], s2s.at[r, 0], s2r.at[r, 0], to_right),
            push(w1.at[piece2(r, opp, 1)], v1.at[r, 1], s2s.at[r, 1], s2r.at[r, 1], to_left),
            push(w1.at[piece2(r, right, 1)], v2.at[r, 0], s2s.at[r, 2], s2r.at[r, 2], to_right),
            push(w1.at[piece2(r, left, 0)], v2.at[r, 1], s2s.at[r, 3], s2r.at[r, 3], to_left),
        )

    def stage2_pass(r, begun):
        axis = ROUTES[r][1]
        m = pos[axis]
        out = []
        for side, where in enumerate(((m + 1) % 4, (m + 3) % 4)):
            begun[side].wait_recv()
            mine = w1[piece2(r, where, side)].astype(F32)
            u3[r, side] = (mine + v1[r, side].astype(F32)).astype(BF)
            out.append(
                push(
                    u3.at[r, side],
                    v3.at[r, side],
                    s2s.at[r, 4 + side],
                    s2r.at[r, 4 + side],
                    at_chip(axis, where, c),
                )
            )
        return out

    def stage2_end(r, begun, handed):
        axis, _ = ROUTES[r][1], None
        m = pos[axis]
        for copy in (begun[2], begun[3], handed[0], handed[1]):
            copy.wait_recv()
        for half in range(2):
            total = w1[piece2(r, m, half)].astype(F32)
            total += v2[r, 1 - half].astype(F32) + v3[r, half].astype(F32)
            w2[r, :, 2 * half : 2 * half + 2] = total.astype(BF)

    def stage3_start(r):
        axis = ROUTES[r][2]
        m = pos[axis]
        last[r, m, c] = w2[r, :, m]
        for k in range(4):
            where = (m + k) % 4
            for other in range(2):
                if k == 0 and other == 0:
                    continue
                core = c if other == 0 else 1 - c
                push(
                    w2.at[r, :, where],
                    last.at[r, m, c],
                    s3s.at[r, k, other],
                    s3r.at[r, k, other],
                    at_chip(axis, where, core),
                )

    def stage3_end(r):
        axis = ROUTES[r][2]
        m = pos[axis]
        for k in range(4):
            where = (m + 4 - k) % 4
            for other in range(2):
                if k == 0 and other == 0:
                    continue
                core = c if other == 0 else 1 - c
                pltpu.make_async_remote_copy(
                    src_ref=last.at[r, where, core],
                    dst_ref=last.at[r, where, core],
                    send_sem=s3s.at[r, k, other],
                    recv_sem=s3r.at[r, k, other],
                    device_id=at_chip(axis, where, core),
                    device_id_type=MESH,
                ).wait_recv()
        scale = 1.0 / 32768.0
        for core in range(2):
            total = last[r, 0, core].astype(F32)
            for k in range(1, 4):
                total += last[r, k, core].astype(F32)
            fin[core, 2 * r : 2 * r + 2] = total * scale

    begun, handed = {}, {}
    for r in range(2):
        begun[r] = stage2_start(r)
    passed[5] = stage1_pass(5, started[5])
    for u in (4, 5):
        stage1_end(u, started[u], passed[u])
    begun[2] = stage2_start(2)
    for r in range(3):
        handed[r] = stage2_pass(r, begun[r])
    for r in range(3):
        stage2_end(r, begun[r], handed[r])
        stage3_start(r)
    for copy in row_copies:
        copy.wait_recv()
    o_rows[...] = rows_in[...]
    for r in range(3):
        stage3_end(r)

    def own_rows(core, unit, half, cols):
        lower = fin[core, unit, 8 * half : 8 * half + 4, cols]
        higher = fin[core, unit, 8 * half + 4 : 8 * half + 8, cols]
        return jnp.where(c == 0, lower, higher)

    for core in range(2):
        for half in range(2):
            for q in range(4):
                at = core * 2048 + q * 512 + half * 256
                o_deep[:, at : at + 256] = own_rows(core, 1 + q, half, slice(0, 256))
            at = core * 256 + half * 128
            o_cross[:, at : at + 128] = own_rows(core, 5, half, slice(0, 128))
    for half in range(2):
        cols = slice(128 * half, 128 * half + 128)
        o_score[16 * half : 16 * half + 16] = jnp.where(c == 0, fin[0, 0, :, cols], fin[1, 0, :, cols])
    chip = t * 4 + y
    bias = fin[0, 5, 0:8, 128:256] + fin[1, 5, 0:8, 128:256]
    for row, first in enumerate((chip % 2 * 64 + c * 32, chip % 16 * 8 + c * 4, chip * 2 + c)):
        o_bias[row : row + 1] = pltpu.roll(bias, (128 - first) % 128, 1)[row : row + 1]
    for copy in sends:
        copy.wait_send()


def student_call(logits, owners, features, w_cross, b_cross, w_deep, b_deep, w_score, b_score):
    dma = pltpu.SemaphoreType.DMA
    vmem = pltpu.VMEM
    whole = pl.BlockSpec(memory_space=pltpu.VMEM)
    return pl.pallas_call(
        student_kernel,
        out_shape=(
            jax.ShapeDtypeStruct((4, 512), F32),
            jax.ShapeDtypeStruct((4, 4096), F32),
            jax.ShapeDtypeStruct((32, 128), F32),
            jax.ShapeDtypeStruct((8, 128), F32),
            jax.ShapeDtypeStruct((16, CAP, 128), BF),
        ),
        in_specs=[whole] * 9,
        out_specs=(whole,) * 5,
        scratch_shapes=[
            vmem((256, 512), BF),
            vmem((512, 256), BF),
            vmem((512, 256), BF),
            vmem((512, 256), BF),
            vmem((512, 256), BF),
            vmem((4096, 256), BF),
            vmem((8, 256, 512), F32),
            vmem((256, 128), F32),
            vmem((16, CAP, 128), BF),
            vmem((16, CAP, 128), BF),
            vmem((8, 256, 512), BF),
            vmem((4, 256, 512), BF),
            vmem((2, 64, 16, 256), BF),
            vmem((64, 16, 256), BF),
            vmem((256, 512), F32),
            vmem((2, 256, 256), BF),
            vmem((256, 256), BF),
            vmem((8, 8, 512), F32),
            vmem((6, 4, 4, 4, 16, 256), BF),
            vmem((6, 2, 2, 4, 16, 256), BF),
            vmem((6, 2, 2, 4, 16, 256), BF),
            vmem((6, 2, 2, 4, 16, 256), BF),
            vmem((6, 2, 2, 4, 16, 256), BF),
            vmem((3, 2, 4, 4, 16, 256), BF),
            vmem((3, 2, 2, 2, 16, 256), BF),
            vmem((3, 2, 2, 2, 16, 256), BF),
            vmem((3, 2, 2, 2, 16, 256), BF),
            vmem((3, 2, 2, 2, 16, 256), BF),
            vmem((3, 2, 4, 16, 256), BF),
            vmem((3, 4, 2, 2, 16, 256), BF),
            vmem((2, 6, 16, 256), F32),
            dma((6, 6)),
            dma((6, 6)),
            dma((3, 6)),
            dma((3, 6)),
            dma((3, 4, 2)),
            dma((3, 4, 2)),
            dma((8,)),
            dma((8,)),
            dma((16,)),
            dma((16,)),
        ],
        compiler_params=pltpu.CompilerParams(
            collective_id=0, has_side_effects=True, vmem_limit_bytes=48 * 1024 * 1024
        ),
    )(logits, owners, features, w_cross, b_cross, w_deep, b_deep, w_score, b_score)


def action_embed(embeddings, action_ids, action_table):
    kinds = jnp.arange(action_table.shape[0], dtype=jnp.int32)
    onehot = (action_ids[:, None] == kinds[None, :]).astype(BF)
    added = embeddings.astype(F32) + nn(onehot, action_table)
    return added.astype(BF)


def candidate_attention(key_rows, query_rows, segments, positions):
    rows = key_rows.shape[0]
    picks = query_rows.shape[0]
    width = key_rows.shape[1] // 2
    head_size = width // HEADS
    values = key_rows[:, :width].reshape(rows, HEADS, head_size)
    keys = key_rows[:, width:].reshape(rows, HEADS, head_size)
    gate = query_rows[:, :width].astype(F32)
    queries = query_rows[:, width:].reshape(picks, HEADS, head_size)
    scores = (
        jnp.einsum("chd,rhd->hcr", queries, keys, preferred_element_type=F32) * head_size ** (-0.5)
    )
    owner_seg = jnp.take(segments, positions)
    places = jnp.arange(rows, dtype=jnp.int32)
    allowed = (segments[None, :] == owner_seg[:, None]) & (places[None, :] <= positions[:, None])
    weights = jnp.where(allowed[None], jax.nn.silu(scores), 0.0).astype(BF)
    mixed = jnp.einsum("hcr,rhd->chd", weights, values, preferred_element_type=F32)
    mixed = mixed.reshape(picks, width)
    centre = jnp.mean(mixed, axis=1, keepdims=True)
    spread = jnp.mean(jnp.square(mixed - centre), axis=1, keepdims=True)
    normed = (mixed - centre) * lax.rsqrt(spread + EPS)
    return (normed * gate).astype(BF)


def local(
    embeddings,
    action_ids,
    segment_ids,
    cand_pos,
    owners,
    features,
    action_table,
    w_query,
    w_keys,
    w_out,
    w_head,
    w_cross,
    b_cross,
    w_deep,
    b_deep,
    w_score,
    b_score,
):
    mine = action_embed(embeddings, action_ids, action_table)
    picked = jnp.take(mine, cand_pos, axis=0)
    query_sum = nn(picked, lax.all_gather(w_query, "teacher", axis=0, tiled=True))
    key_sum = nn(mine, lax.all_gather(w_keys, "teacher", axis=0, tiled=True))
    key_rows = jax.nn.silu(key_sum).astype(BF)
    query_rows = jax.nn.silu(query_sum).astype(BF)
    mixed = candidate_attention(key_rows, query_rows, segment_ids[0], cand_pos)
    out_head = lax.all_gather(nn(w_out, w_head).astype(BF), "teacher", axis=0, tiled=True)
    logits = (nn(picked, w_head) + nn(mixed, out_head)).astype(BF)
    g_cross, g_deep, g_score, bias, rows = student_call(
        logits,
        owners.reshape(1, -1),
        features,
        w_cross,
        b_cross.reshape(1, -1),
        w_deep,
        b_deep.reshape(1, -1),
        w_score,
        b_score.reshape(1, -1),
    )
    return (
        g_cross,
        bias[1, :4],
        g_deep,
        bias[0, :32],
        g_score,
        bias[2, :1],
        rows.reshape(512, 128),
    )


def solution(mesh):
    both = ("teacher", "student")
    return jax.shard_map(
        local,
        mesh=mesh,
        in_specs=(
            P(both, None),
            P(both),
            P(both, None),
            P(both),
            P(both, None),
            P(both, None),
            P(),
            P("teacher", None),
            P("teacher", None),
            P("teacher", None),
            P(),
            P(),
            P(),
            P(),
            P(),
            P(),
            P(),
        ),
        out_specs=(
            P(both, None),
            P(both),
            P(both, None),
            P(both),
            P(both, None),
            P(both),
            P(both, None),
        ),
        check_vma=False,
    )
```

```python
import functools

import jax
import jax.numpy as jnp
from jax import lax
from jax.experimental import pallas as pl
from jax.experimental.pallas import tpu as pltpu
from jax.sharding import PartitionSpec as P

CAP = 32
EPS = 1e-05
BF = jnp.bfloat16
F32 = jnp.float32
MESH = pl.DeviceIdType.MESH

ROUTES = ((0, 1, 2), (1, 2, 0), (2, 0, 1))


def nn(a, b):
    return lax.dot_general(a, b, (((1,), (0,)), ((), ())), preferred_element_type=F32)


def nt(a, b):
    return lax.dot_general(a, b, (((1,), (1,)), ((), ())), preferred_element_type=F32)


def silu(v):
    half = 0.5 * v
    return half + half * jnp.tanh(half)


def flip(v):
    return v.astype(F32).T.astype(BF)


def kernel(
    emb_hbm,
    ids_ref,
    segs_ref,
    cand_ref,
    owners_ref,
    feat_ref,
    table_ref,
    w_query_ref,
    w_keys_ref,
    w_out_ref,
    w_head_ref,
    w_cross_ref,
    b_cross_ref,
    w_deep_hbm,
    b_deep_ref,
    w_score_hbm,
    b_score_ref,
    o_cross,
    o_deep,
    o_score,
    o_bias,
    o_rows,
    emb,
    w_deep_ref,
    w_score_ref,
    heads,
    out_head,
    table_pad,
    hist,
    picked,
    mask,
    kv,
    queries,
    gate,
    mixed,
    joined,
    base,
    crossed,
    ct,
    ct_sib,
    ft,
    ft_sib,
    hid_t,
    slope,
    scores,
    place_out,
    rows_in,
    d_own,
    d_sib,
    gs,
    gs_sib,
    dcross,
    dc,
    dc_sib,
    bd,
    grads,
    x1,
    x2,
    x3,
    y3,
    w1,
    v1,
    v2,
    v3,
    u3,
    w2,
    last,
    fin,
    s1s,
    s1r,
    s2s,
    s2r,
    s3s,
    s3r,
    scs,
    scr,
    srs,
    srr,
    lds,
    p1s,
    p1r,
    p2s,
    p2r,
    ups,
    upr,
    sbs,
    sbr,
    ohs,
    ohr,
):
    t = lax.axis_index("teacher")
    s = lax.axis_index("student")
    z, x = t // 4, t % 4
    y, c = s // 2, s % 2
    pos = (z, x, y)
    sibling = (t, y * 2 + 1 - c)
    sends = []

    def at_chip(axis, value, core):
        p = list(pos)
        p[axis] = value
        return (p[0] * 4 + p[1], p[2] * 2 + core)

    def push(src, dst, send_sem, recv_sem, device):
        copy = pltpu.make_async_remote_copy(
            src_ref=src,
            dst_ref=dst,
            send_sem=send_sem,
            recv_sem=recv_sem,
            device_id=device,
            device_id_type=MESH,
        )
        copy.start()
        sends.append(copy)
        return copy

    peers = [((t + k) % 16, s) for k in range(1, 16)] + [sibling]
    peers += [at_chip(2, (y + k) % 4, c) for k in range(1, 4)]
    peers += [at_chip(axis, (pos[axis] + k) % 4, 1 - c) for axis in range(3) for k in range(1, 4)]
    barrier = pltpu.get_barrier_semaphore()
    for peer in peers:
        pl.semaphore_signal(barrier, inc=1, device_id=peer, device_id_type=MESH)

    loads = [
        pltpu.make_async_copy(w_deep_hbm, w_deep_ref, lds.at[0]),
        pltpu.make_async_copy(w_score_hbm, w_score_ref, lds.at[1]),
        pltpu.make_async_copy(emb_hbm, emb, lds.at[2]),
    ]
    for load in loads:
        load.start()

    odd = y % 2
    first = (1 - c) * x + c * z
    second = (1 - c) * z + c * x

    def shard(i, j):
        i, j = (first + i) % 4, (second + j) % 4
        return (1 - c) * (j * 4 + i) + c * (i * 4 + j)

    def head_of(k, core):
        return (4 + 2 * odd + core, core, 2 + core, 6 - 2 * odd + core)[k]

    for k in range(3):
        for part, (ref, start) in enumerate(
            ((w_keys_ref, 0), (w_keys_ref, 1024), (w_query_ref, 0), (w_query_ref, 1024))
        ):
            cols = pl.ds(pl.multiple_of(start + head_of(k, c) * 128, 128), 128)
            heads[2 * k + c, t, :, 128 * part : 128 * part + 128] = ref[:, cols]

    def along(k, i, j, rows, send_sem, recv_sem, device):
        ref = heads.at[2 * k + c, shard(i, j), rows]
        return push(ref, ref, send_sem, recv_sem, device)

    full, halves = slice(0, 64), (slice(0, 32), slice(32, 64))
    y_next = (t, (y + 1 + 2 * c) % 4 * 2 + c)
    p1, p2, ups_done = {}, {}, []

    def to_y(k, i, j):
        if k == 0:
            n = (i % 4) * 4 + j % 4
            up = heads.at[c, shard(i, j)]
            ups_done.append(push(up, heads.at[6 + c, shard(i, j)], ups.at[n], upr.at[n], y_next))

    def spread(k, i):
        for side, step in enumerate((1, 3)):
            device = (shard(0, step), s)
            p2[k, i, side] = along(k, i, 0, full, p2s.at[k, i, side], p2r.at[k, i, side], device)
        to_y(k, i, 0)

    def event0(k):
        for side, step in enumerate((1, 3)):
            device = (shard(step, 0), s)
            p1[k, side] = along(k, 0, 0, full, p1s.at[k, side], p1r.at[k, side], device)
        spread(k, 0)

    def event1(k):
        for side, step in enumerate((1, 3)):
            p1[k, side].wait_recv()
            device = (shard(step, 0), s)
            p1[k, 2 + side] = along(
                k, 4 - step, 0, halves[side], p1s.at[k, 2 + side], p1r.at[k, 2 + side], device
            )
        for i in (3, 1):
            spread(k, i)

    def event2(k):
        for side in range(2):
            p1[k, 2 + side].wait_recv()
        spread(k, 2)

    def event3(k):
        for i in (0, 1, 3, 2):
            side = 0 if i < 2 else 1
            step = (1, 3)[side]
            p2[k, i, side].wait_recv()
            device = (shard(0, step), s)
            p2[k, i, 2] = along(k, i, 4 - step, full, p2s.at[k, i, 2], p2r.at[k, i, 2], device)
            p2[k, i, 1 - side].wait_recv()
        for i in range(4):
            to_y(k, i, 3)
            to_y(k, i, 1)

    sib_done = {}

    def to_sibling(k):
        ref = heads.at[2 * k + c]
        sib_done[k] = push(ref, ref, sbs.at[k], sbr.at[k], sibling)

    def event4(k):
        for i in range(4):
            p2[k, i, 2].wait_recv()
            to_y(k, i, 2)
        to_sibling(k)

    own_out = nn(w_out_ref[...], w_head_ref[...]).astype(BF)
    out_head[t] = own_out
    pl.semaphore_wait(barrier, len(peers))
    for k in range(3):
        event0(k)

    feats = feat_ref[...]
    feats32 = feats.astype(F32)
    cross = nn(feats, w_cross_ref[...]) + b_cross_ref[...].astype(F32)
    crossed[...] = (feats32 * cross + feats32).astype(BF)
    ct[...] = flip(crossed[...])
    ft[...] = flip(feats)
    ct_copy = push(ct, ct_sib, scs.at[0], scr.at[0], sibling)
    ft_copy = push(ft, ft_sib, scs.at[1], scr.at[1], sibling)
    scores[...] = jnp.broadcast_to(b_score_ref[...].astype(F32), scores.shape)
    for k in range(3):
        event1(k)

    def forward(j, carry):
        cols = pl.ds(pl.multiple_of(j * 512, 512), 512)
        pre = nn(crossed[...], w_deep_ref[:, cols]) + b_deep_ref[:, cols].astype(F32)
        sigma = 0.5 + 0.5 * jnp.tanh(0.5 * pre)
        hidden = (pre * sigma).astype(BF)
        slope[j] = sigma * (1.0 + pre * (1.0 - sigma))
        hid_t[cols, :] = flip(hidden)
        scores[...] += nn(hidden, w_score_ref[cols, :])
        return carry

    loads[0].wait()
    loads[1].wait()
    lax.fori_loop(0, 3, forward, 0)
    for k in range(3):
        event2(k)
    lax.fori_loop(3, 8, forward, 0)
    event3(0)

    table_pad[...] = jnp.zeros_like(table_pad)
    table_pad[0:16] = table_ref[...]
    loads[2].wait()

    def embed(i, carry):
        rows = pl.ds(pl.multiple_of(i * 256, 256), 256)
        kinds = lax.broadcasted_iota(jnp.int32, (128, 256), 0)
        onehot = flip(kinds == ids_ref[:, rows])
        hist[rows, :] = (emb[rows, :].astype(F32) + nn(onehot, table_pad[...])).astype(BF)
        return carry

    lax.fori_loop(0, 4, embed, 0)
    event3(1)
    where_col = jnp.broadcast_to(cand_ref[...], (128, 256)).astype(F32).T[:, 0:1]
    places = lax.broadcasted_iota(jnp.int32, (256, 1024), 1).astype(F32)
    segs = segs_ref[...].astype(F32)
    chosen = (places == where_col).astype(F32)
    picked[...] = nn(chosen.astype(BF), hist[...]).astype(BF)
    seg_col = jnp.sum(chosen * segs, axis=1, keepdims=True)
    mask[...] = jnp.where((segs == seg_col) & (places <= where_col), 1.0, 0.0)
    base[...] = nn(picked[...], w_head_ref[...])
    event4(0)
    event3(2)

    def attend(k, core):
        slot = 2 * k + core
        head = head_of(k, core)
        qrows = silu(nn(picked[...], heads[slot, :, :, 256:512].reshape(1024, 256))).astype(BF)
        gate[head] = qrows[:, :128]
        queries[...] = qrows[:, 128:]
        mixed[head] = jnp.zeros((256, 128), F32)

        def rows_step(i, carry):
            rows = pl.ds(pl.multiple_of(i * 256, 256), 256)
            weights_kv = heads[slot, :, :, 0:256].reshape(1024, 256)
            kv[...] = silu(nn(hist[rows, :], weights_kv)).astype(BF)
            half = nt(queries[...], kv[:, 128:]) * (0.5 * 128 ** (-0.5))
            weights = ((half + half * jnp.tanh(half)) * mask[:, rows]).astype(BF)
            mixed[head] += nn(weights, kv[:, :128])
            return carry

        lax.fori_loop(0, 4, rows_step, 0)

    attend(0, c)
    event4(1)
    sib_done[0].wait_recv()
    attend(0, 1 - c)
    event4(2)
    oh_copies = []
    mine_rows = pl.ds(pl.multiple_of(32 * c, 32), 32)
    for k in range(1, 16):
        ref = out_head.at[t, mine_rows]
        oh_copies.append(push(ref, ref, ohs.at[k], ohr.at[k], ((t + k) % 16, s)))

    dest = owners_ref[...]
    kinds = lax.broadcasted_iota(jnp.int32, (16, 256), 0)
    hits = (kinds == dest).astype(F32)
    upper = (
        lax.broadcasted_iota(jnp.int32, (256, 256), 0)
        < lax.broadcasted_iota(jnp.int32, (256, 256), 1)
    ).astype(BF)
    before = nn(hits.astype(BF), upper)
    rank = jnp.sum(before * hits, axis=0, keepdims=True).astype(jnp.int32)
    slot = dest * CAP + rank
    place = (lax.broadcasted_iota(jnp.int32, (512, 256), 0) == slot).astype(BF)
    placed = nn(place, scores[...].astype(BF)).astype(BF).reshape(16, CAP, 128)
    place_out[...] = placed
    rows_in[t] = place_out[t]
    row_copies = []
    for k in range(1, 16):
        to = (t + k) % 16
        row_copies.append(push(place_out.at[to], rows_in.at[t], srs.at[k], srr.at[k], (to, s)))

    attend(1, c)
    sib_done[1].wait_recv()
    attend(1, 1 - c)
    for copy in oh_copies:
        copy.wait_recv()
    every = out_head.at[:, mine_rows]
    oh_sib = push(every, every, ohs.at[0], ohr.at[0], sibling)
    for copy in ups_done:
        copy.wait_recv()
    to_sibling(3)
    attend(2, c)
    sib_done[2].wait_recv()
    attend(2, 1 - c)
    attend(3, c)
    sib_done[3].wait_recv()
    attend(3, 1 - c)

    centre = jnp.sum(jnp.sum(mixed[...], axis=0), axis=1, keepdims=True) * (1.0 / 1024.0)
    spread_sum = jnp.sum(jnp.square(mixed[...] - centre[None]), axis=0)
    scale_rows = lax.rsqrt(jnp.sum(spread_sum, axis=1, keepdims=True) * (1.0 / 1024.0) + EPS)
    for head in range(8):
        normed = (mixed[head] - centre) * scale_rows
        joined[:, 128 * head : 128 * head + 128] = (normed * gate[head].astype(F32)).astype(BF)
    oh_sib.wait_recv()
    logits = base[...] + nn(joined[...], out_head[...].reshape(1024, 128))

    delta = scores[...] - logits.astype(BF).astype(F32)
    delta16 = delta.astype(BF)
    bscore = jnp.sum(delta, axis=0, keepdims=True)

    def back_chunk(j):
        rows = pl.ds(pl.multiple_of(j * 512, 512), 512)
        dpre = nt(delta16, w_score_ref[rows, :]) * slope[j]
        d_own[j] = dpre.astype(BF)
        bd[j] = jnp.broadcast_to(jnp.sum(dpre, axis=0, keepdims=True), (8, 512))

    d_copies = []
    for q in range(4):
        j = (1 - c) * 4 + q
        back_chunk(j)
        d_copies.append(push(d_own.at[j], d_sib.at[q], scs.at[2 + q], scr.at[2 + q], sibling))

    def score_grads(i, carry):
        rows = pl.ds(pl.multiple_of(i * 512, 512), 512)
        g = nn(hid_t[rows, :], delta16).astype(BF).reshape(8, 2, 2, 16, 128)
        chips = pl.ds(pl.multiple_of(i * 8, 8), 8)
        for core in range(2):
            gs[core, chips, :, 0:128] = g[:, core, 0]
            gs[core, chips, :, 128:256] = g[:, core, 1]
        return carry

    lax.fori_loop(0, 8, score_grads, 0)
    gs_copy = push(gs.at[1 - c], gs_sib, scs.at[6], scr.at[6], sibling)

    def own_chunk(q, carry):
        back_chunk(c * 4 + q)
        return carry

    lax.fori_loop(0, 4, own_chunk, 0)

    def axes_of(u):
        axis = ROUTES[u // 2][0]
        rest = [a for a in range(3) if a != axis]
        return axis, rest

    def piece(u, where, half):
        axis, rest = axes_of(u)
        index = [slice(None)] * 3
        index[axis] = where
        index[rest[0]] = pl.ds(2 * half, 2)
        return (u, *index)

    def stage1_start(u):
        axis, _ = axes_of(u)
        m = pos[axis]
        right, left, opp = (m + 1) % 4, (m + 3) % 4, (m + 2) % 4
        to_right, to_left = at_chip(axis, right, c), at_chip(axis, left, c)
        return (
            push(grads.at[piece(u, opp, 0)], x1.at[u, 0], s1s.at[u, 0], s1r.at[u, 0], to_right),
            push(grads.at[piece(u, opp, 1)], x1.at[u, 1], s1s.at[u, 1], s1r.at[u, 1], to_left),
            push(grads.at[piece(u, right, 1)], x2.at[u, 0], s1s.at[u, 2], s1r.at[u, 2], to_right),
            push(grads.at[piece(u, left, 0)], x2.at[u, 1], s1s.at[u, 3], s1r.at[u, 3], to_left),
        )

    def stage1_pass(u, started):
        axis, _ = axes_of(u)
        m = pos[axis]
        right, left = (m + 1) % 4, (m + 3) % 4
        out = []
        for side, (where, device) in enumerate(
            ((right, at_chip(axis, right, c)), (left, at_chip(axis, left, c)))
        ):
            started[side].wait_recv()
            mine = grads[piece(u, where, side)].astype(F32)
            y3[u, side] = (mine + x1[u, side].astype(F32)).astype(BF)
            out.append(
                push(y3.at[u, side], x3.at[u, side], s1s.at[u, 4 + side], s1r.at[u, 4 + side], device)
            )
        return out

    def stage1_end(u, started, passed):
        axis, _ = axes_of(u)
        m = pos[axis]
        for copy in (started[2], started[3], passed[0], passed[1]):
            copy.wait_recv()
        for half in range(2):
            total = grads[piece(u, m, half)].astype(F32)
            total += x2[u, 1 - half].astype(F32) + x3[u, half].astype(F32)
            w1[u // 2, u % 2, 2 * half : 2 * half + 2] = total.astype(BF)

    started = {}

    gs_copy.wait_recv()

    def add_scores(i, carry):
        summed = gs[c, pl.ds(i * 16, 16)].astype(F32) + gs_sib[pl.ds(i * 16, 16)].astype(F32)
        grads[0, i] = summed.astype(BF).reshape(4, 4, 16, 256)
        return carry

    lax.fori_loop(0, 4, add_scores, 0)
    started[0] = stage1_start(0)

    ct_copy.wait_recv()
    for q in range(4):
        d_copies[q].wait_recv()

        def deep_grads(i, carry, q=q):
            rows = pl.ds(pl.multiple_of(i * 128, 128), 128)
            g = nn(ct[rows, :], d_own[c * 4 + q]) + nn(ct_sib[rows, :], d_sib[q])
            g = g.reshape(16, 8, 512)
            g = jnp.concatenate([g[:, :, :256], g[:, :, 256:]], axis=1)
            grads[1 + q, i] = g.astype(BF).reshape(4, 4, 16, 256)
            return carry

        lax.fori_loop(0, 4, deep_grads, 0)
        started[1 + q] = stage1_start(1 + q)

    dcross[...] = jnp.zeros_like(dcross)

    def cross_chunk(j, carry):
        cols = pl.ds(pl.multiple_of(j * 512, 512), 512)
        dcross[...] += nt(d_own[j], w_deep_ref[:, cols])
        return carry

    lax.fori_loop(0, 8, cross_chunk, 0)
    dcr = dcross[...] * feats32
    bcross = jnp.sum(dcr, axis=0, keepdims=True)
    dc[0] = dcr[:, :256].astype(BF)
    dc[1] = dcr[:, 256:].astype(BF)
    dc_copy = push(dc.at[1 - c], dc_sib, scs.at[7], scr.at[7], sibling)
    sub = lax.broadcasted_iota(jnp.int32, (16, 128), 0)
    for pair in range(32):
        deep_row = bd[pair // 4, 0:1, (pair % 4) * 128 : (pair % 4) * 128 + 128]
        cross_row = bcross[:, (pair // 8) * 128 : (pair // 8) * 128 + 128]
        tile = jnp.where(sub == 0, deep_row, jnp.where(sub == 1, cross_row, bscore))
        tile = tile.astype(BF)
        for chip in (2 * pair, 2 * pair + 1):
            grads[5, chip // 16, chip // 4 % 4, chip % 4, :, 128:256] = tile
    passed = {}
    for u in range(5):
        passed[u] = stage1_pass(u, started[u])
    ft_copy.wait_recv()
    dc_copy.wait_recv()

    def cross_grads(i, carry):
        rows = pl.ds(pl.multiple_of(i * 128, 128), 128)
        g = nn(ft[rows, :], dc[c]) + nn(ft_sib[rows, :], dc_sib[...])
        g = g.reshape(16, 8, 256)
        g = jnp.concatenate([g[:, :, :128], g[:, :, 128:]], axis=1)
        grads[5, i, :, :, :, 0:128] = g.astype(BF).reshape(4, 4, 16, 128)
        return carry

    lax.fori_loop(0, 4, cross_grads, 0)
    started[5] = stage1_start(5)
    for u in range(4):
        stage1_end(u, started[u], passed[u])

    def piece2(r, where, half):
        axis, second, _ = ROUTES[r]
        rest = [a for a in range(3) if a != axis]
        index = [None, None]
        index[rest.index(second)] = where
        index[1 - rest.index(second)] = pl.ds(2 * half, 2)
        return (r, slice(None), *index)

    def stage2_start(r):
        axis = ROUTES[r][1]
        m = pos[axis]
        right, left, opp = (m + 1) % 4, (m + 3) % 4, (m + 2) % 4
        to_right, to_left = at_chip(axis, right, c), at_chip(axis, left, c)
        return (
            push(w1.at[piece2(r, opp, 0)], v1.at[r, 0], s2s.at[r, 0], s2r.at[r, 0], to_right),
            push(w1.at[piece2(r, opp, 1)], v1.at[r, 1], s2s.at[r, 1], s2r.at[r, 1], to_left),
            push(w1.at[piece2(r, right, 1)], v2.at[r, 0], s2s.at[r, 2], s2r.at[r, 2], to_right),
            push(w1.at[piece2(r, left, 0)], v2.at[r, 1], s2s.at[r, 3], s2r.at[r, 3], to_left),
        )

    def stage2_pass(r, begun):
        axis = ROUTES[r][1]
        m = pos[axis]
        out = []
        for side, where in enumerate(((m + 1) % 4, (m + 3) % 4)):
            begun[side].wait_recv()
            mine = w1[piece2(r, where, side)].astype(F32)
            u3[r, side] = (mine + v1[r, side].astype(F32)).astype(BF)
            out.append(
                push(
                    u3.at[r, side],
                    v3.at[r, side],
                    s2s.at[r, 4 + side],
                    s2r.at[r, 4 + side],
                    at_chip(axis, where, c),
                )
            )
        return out

    def stage2_end(r, begun, handed):
        axis, _ = ROUTES[r][1], None
        m = pos[axis]
        for copy in (begun[2], begun[3], handed[0], handed[1]):
            copy.wait_recv()
        for half in range(2):
            total = w1[piece2(r, m, half)].astype(F32)
            total += v2[r, 1 - half].astype(F32) + v3[r, half].astype(F32)
            w2[r, :, 2 * half : 2 * half + 2] = total.astype(BF)

    def stage3_start(r):
        axis = ROUTES[r][2]
        m = pos[axis]
        last[r, m, c] = w2[r, :, m]
        for k in range(4):
            where = (m + k) % 4
            for other in range(2):
                if k == 0 and other == 0:
                    continue
                core = c if other == 0 else 1 - c
                push(
                    w2.at[r, :, where],
                    last.at[r, m, c],
                    s3s.at[r, k, other],
                    s3r.at[r, k, other],
                    at_chip(axis, where, core),
                )

    def stage3_end(r):
        axis = ROUTES[r][2]
        m = pos[axis]
        for k in range(4):
            where = (m + 4 - k) % 4
            for other in range(2):
                if k == 0 and other == 0:
                    continue
                core = c if other == 0 else 1 - c
                pltpu.make_async_remote_copy(
                    src_ref=last.at[r, where, core],
                    dst_ref=last.at[r, where, core],
                    send_sem=s3s.at[r, k, other],
                    recv_sem=s3r.at[r, k, other],
                    device_id=at_chip(axis, where, core),
                    device_id_type=MESH,
                ).wait_recv()
        scale = 1.0 / 32768.0
        for core in range(2):
            total = last[r, 0, core].astype(F32)
            for k in range(1, 4):
                total += last[r, k, core].astype(F32)
            fin[core, 2 * r : 2 * r + 2] = total * scale

    begun, handed = {}, {}
    for r in range(2):
        begun[r] = stage2_start(r)
    passed[5] = stage1_pass(5, started[5])
    for u in (4, 5):
        stage1_end(u, started[u], passed[u])
    begun[2] = stage2_start(2)
    for r in range(3):
        handed[r] = stage2_pass(r, begun[r])
    for r in range(3):
        stage2_end(r, begun[r], handed[r])
        stage3_start(r)
    for copy in row_copies:
        copy.wait_recv()
    o_rows[...] = rows_in[...]
    for r in range(3):
        stage3_end(r)

    def own_rows(core, unit, half, cols):
        lower = fin[core, unit, 8 * half : 8 * half + 4, cols]
        higher = fin[core, unit, 8 * half + 4 : 8 * half + 8, cols]
        return jnp.where(c == 0, lower, higher)

    for core in range(2):
        for half in range(2):
            for q in range(4):
                at = core * 2048 + q * 512 + half * 256
                o_deep[:, at : at + 256] = own_rows(core, 1 + q, half, slice(0, 256))
            at = core * 256 + half * 128
            o_cross[:, at : at + 128] = own_rows(core, 5, half, slice(0, 128))
    for half in range(2):
        cols = slice(128 * half, 128 * half + 128)
        o_score[16 * half : 16 * half + 16] = jnp.where(c == 0, fin[0, 0, :, cols], fin[1, 0, :, cols])
    chip = t * 4 + y
    bias = fin[0, 5, 0:8, 128:256] + fin[1, 5, 0:8, 128:256]
    for row, first in enumerate((chip % 2 * 64 + c * 32, chip % 16 * 8 + c * 4, chip * 2 + c)):
        o_bias[row : row + 1] = pltpu.roll(bias, (128 - first) % 128, 1)[row : row + 1]
    for copy in sends:
        copy.wait_send()


def local(
    embeddings,
    action_ids,
    segment_ids,
    cand_pos,
    owners,
    features,
    action_table,
    w_query,
    w_keys,
    w_out,
    w_head,
    w_cross,
    b_cross,
    w_deep,
    b_deep,
    w_score,
    b_score,
):
    dma = pltpu.SemaphoreType.DMA
    vmem = pltpu.VMEM
    whole = pl.BlockSpec(memory_space=pltpu.VMEM)
    stay = pl.BlockSpec(memory_space=pl.ANY)
    g_cross, g_deep, g_score, bias, rows = pl.pallas_call(
        kernel,
        out_shape=(
            jax.ShapeDtypeStruct((4, 512), F32),
            jax.ShapeDtypeStruct((4, 4096), F32),
            jax.ShapeDtypeStruct((32, 128), F32),
            jax.ShapeDtypeStruct((8, 128), F32),
            jax.ShapeDtypeStruct((16, CAP, 128), BF),
        ),
        in_specs=[stay] + [whole] * 12 + [stay, whole, stay, whole],
        out_specs=(whole,) * 5,
        scratch_shapes=[
            vmem((1024, 1024), BF),
            vmem((512, 4096), BF),
            vmem((4096, 128), BF),
            vmem((8, 16, 64, 512), BF),
            vmem((16, 64, 128), BF),
            vmem((128, 1024), BF),
            vmem((1024, 1024), BF),
            vmem((256, 1024), BF),
            vmem((256, 1024), F32),
            vmem((256, 256), BF),
            vmem((256, 128), BF),
            vmem((8, 256, 128), BF),
            vmem((8, 256, 128), F32),
            vmem((256, 1024), BF),
            vmem((256, 128), F32),
            vmem((256, 512), BF),
            vmem((512, 256), BF),
            vmem((512, 256), BF),
            vmem((512, 256), BF),
            vmem((512, 256), BF),
            vmem((4096, 256), BF),
            vmem((8, 256, 512), F32),
            vmem((256, 128), F32),
            vmem((16, CAP, 128), BF),
            vmem((16, CAP, 128), BF),
            vmem((8, 256, 512), BF),
            vmem((4, 256, 512), BF),
            vmem((2, 64, 16, 256), BF),
            vmem((64, 16, 256), BF),
            vmem((256, 512), F32),
            vmem((2, 256, 256), BF),
            vmem((256, 256), BF),
            vmem((8, 8, 512), F32),
            vmem((6, 4, 4, 4, 16, 256), BF),
            vmem((6, 2, 2, 4, 16, 256), BF),
            vmem((6, 2, 2, 4, 16, 256), BF),
            vmem((6, 2, 2, 4, 16, 256), BF),
            vmem((6, 2, 2, 4, 16, 256), BF),
            vmem((3, 2, 4, 4, 16, 256), BF),
            vmem((3, 2, 2, 2, 16, 256), BF),
            vmem((3, 2, 2, 2, 16, 256), BF),
            vmem((3, 2, 2, 2, 16, 256), BF),
            vmem((3, 2, 2, 2, 16, 256), BF),
            vmem((3, 2, 4, 16, 256), BF),
            vmem((3, 4, 2, 2, 16, 256), BF),
            vmem((2, 6, 16, 256), F32),
            dma((6, 6)),
            dma((6, 6)),
            dma((3, 6)),
            dma((3, 6)),
            dma((3, 4, 2)),
            dma((3, 4, 2)),
            dma((8,)),
            dma((8,)),
            dma((16,)),
            dma((16,)),
            dma((3,)),
            dma((3, 4)),
            dma((3, 4)),
            dma((3, 4, 3)),
            dma((3, 4, 3)),
            dma((16,)),
            dma((16,)),
            dma((4,)),
            dma((4,)),
            dma((16,)),
            dma((16,)),
        ],
        compiler_params=pltpu.CompilerParams(
            collective_id=0, has_side_effects=True, vmem_limit_bytes=56 * 1024 * 1024
        ),
    )(
        embeddings,
        action_ids.reshape(1, -1),
        segment_ids,
        cand_pos.reshape(1, -1),
        owners.reshape(1, -1),
        features,
        action_table,
        w_query,
        w_keys,
        w_out,
        w_head,
        w_cross,
        b_cross.reshape(1, -1),
        w_deep,
        b_deep.reshape(1, -1),
        w_score,
        b_score.reshape(1, -1),
    )
    return (
        g_cross,
        bias[1, :4],
        g_deep,
        bias[0, :32],
        g_score,
        bias[2, :1],
        rows.reshape(512, 128),
    )


def solution(mesh):
    both = ("teacher", "student")
    return jax.shard_map(
        local,
        mesh=mesh,
        in_specs=(
            P(both, None),
            P(both),
            P(both, None),
            P(both),
            P(both, None),
            P(both, None),
            P(),
            P("teacher", None),
            P("teacher", None),
            P("teacher", None),
            P(),
            P(),
            P(),
            P(),
            P(),
            P(),
            P(),
        ),
        out_specs=(
            P(both, None),
            P(both),
            P(both, None),
            P(both),
            P(both, None),
            P(both),
            P(both, None),
        ),
        check_vma=False,
    )
```

```python
import functools

import jax
import jax.numpy as jnp
from jax import lax
from jax.experimental import pallas as pl
from jax.experimental.pallas import tpu as pltpu
from jax.sharding import PartitionSpec as P

CAP = 32
EPS = 1e-05
BF = jnp.bfloat16
F32 = jnp.float32
MESH = pl.DeviceIdType.MESH

ROUTES = ((0, 1, 2), (1, 2, 0), (2, 0, 1))


def nn(a, b):
    return lax.dot_general(a, b, (((1,), (0,)), ((), ())), preferred_element_type=F32)


def nt(a, b):
    return lax.dot_general(a, b, (((1,), (1,)), ((), ())), preferred_element_type=F32)


def silu(v):
    half = 0.5 * v
    return half + half * jnp.tanh(half)


def flip(v):
    return v.astype(F32).T.astype(BF)


def kernel(
    emb_hbm,
    ids_ref,
    segs_ref,
    cand_ref,
    owners_ref,
    feat_ref,
    table_ref,
    w_query_hbm,
    w_keys_hbm,
    w_out_ref,
    w_head_ref,
    w_cross_ref,
    b_cross_ref,
    w_deep_hbm,
    b_deep_ref,
    w_score_hbm,
    b_score_ref,
    o_cross,
    o_deep,
    o_score,
    o_bias,
    o_rows,
    emb,
    w_deep_ref,
    w_score_ref,
    heads,
    out_head,
    table_pad,
    hist,
    picked,
    mask,
    kv,
    gate,
    mixed,
    joined,
    base,
    crossed,
    ct,
    ct_sib,
    ft,
    ft_sib,
    hid_t,
    slope,
    scores,
    place_out,
    rows_in,
    d_own,
    d_sib,
    gs,
    gs_sib,
    dc,
    dc_sib,
    bd,
    grads,
    x1,
    x2,
    x3,
    y3,
    w1,
    v1,
    v2,
    v3,
    u3,
    w2,
    last,
    fin,
    s1s,
    s1r,
    s2s,
    s2r,
    s3s,
    s3r,
    scs,
    scr,
    srs,
    srr,
    lds,
    hds,
    p1s,
    p1r,
    p2s,
    p2r,
    ups,
    upr,
    sbs,
    sbr,
    ohs,
    ohr,
):
    t = lax.axis_index("teacher")
    s = lax.axis_index("student")
    z, x = t // 4, t % 4
    y, c = s // 2, s % 2
    pos = (z, x, y)
    sibling = (t, y * 2 + 1 - c)
    sends = []

    def at_chip(axis, value, core):
        p = list(pos)
        p[axis] = value
        return (p[0] * 4 + p[1], p[2] * 2 + core)

    def push(src, dst, send_sem, recv_sem, device):
        copy = pltpu.make_async_remote_copy(
            src_ref=src,
            dst_ref=dst,
            send_sem=send_sem,
            recv_sem=recv_sem,
            device_id=device,
            device_id_type=MESH,
        )
        copy.start()
        sends.append(copy)
        return copy

    peers = [((t + k) % 16, s) for k in range(1, 16)] + [sibling]
    peers += [at_chip(2, (y + k) % 4, c) for k in range(1, 4)]
    peers += [at_chip(axis, (pos[axis] + k) % 4, 1 - c) for axis in range(3) for k in range(1, 4)]
    barrier = pltpu.get_barrier_semaphore()
    for peer in peers:
        pl.semaphore_signal(barrier, inc=1, device_id=peer, device_id_type=MESH)

    odd = y % 2
    first = (1 - c) * x + c * z
    second = (1 - c) * z + c * x

    def shard(i, j):
        i, j = (first + i) % 4, (second + j) % 4
        return (1 - c) * (j * 4 + i) + c * (i * 4 + j)

    def head_of(k, core):
        return (4 + 2 * odd + core, core, 2 + core, 6 - 2 * odd + core)[k]

    own_cols = []
    for k in range(3):
        for part, (ref, start) in enumerate(
            ((w_keys_hbm, 0), (w_keys_hbm, 1024), (w_query_hbm, 0), (w_query_hbm, 1024))
        ):
            cols = pl.ds(pl.multiple_of(start + head_of(k, c) * 128, 128), 128)
            own_cols.append(
                pltpu.make_async_copy(
                    ref.at[:, cols],
                    heads.at[2 * k + c, t, :, 128 * part : 128 * part + 128],
                    hds.at[k, part],
                )
            )
            own_cols[-1].start()
    loads = [
        pltpu.make_async_copy(w_deep_hbm, w_deep_ref, lds.at[0]),
        pltpu.make_async_copy(w_score_hbm, w_score_ref, lds.at[1]),
        pltpu.make_async_copy(emb_hbm, emb, lds.at[2]),
    ]
    for load in loads:
        load.start()

    def along(k, i, j, rows, send_sem, recv_sem, device):
        ref = heads.at[2 * k + c, shard(i, j), rows]
        return push(ref, ref, send_sem, recv_sem, device)

    full, halves = slice(0, 64), (slice(0, 32), slice(32, 64))
    y_next = (t, (y + 1 + 2 * c) % 4 * 2 + c)
    p1, p2, ups_done = {}, {}, []

    def to_y(k, i, j):
        if k == 0:
            n = (i % 4) * 4 + j % 4
            up = heads.at[c, shard(i, j)]
            ups_done.append(push(up, heads.at[6 + c, shard(i, j)], ups.at[n], upr.at[n], y_next))

    def spread(k, i):
        for side, step in enumerate((1, 3)):
            device = (shard(0, step), s)
            p2[k, i, side] = along(k, i, 0, full, p2s.at[k, i, side], p2r.at[k, i, side], device)
        to_y(k, i, 0)

    def hop(k):
        for side, step in enumerate((1, 3)):
            device = (shard(step, 0), s)
            p1[k, side] = along(k, 0, 0, full, p1s.at[k, side], p1r.at[k, side], device)

    def hop_pass(k):
        for side, step in enumerate((1, 3)):
            p1[k, side].wait_recv()
            device = (shard(step, 0), s)
            p1[k, 2 + side] = along(
                k, 4 - step, 0, halves[side], p1s.at[k, 2 + side], p1r.at[k, 2 + side], device
            )

    def hop_end(k):
        for side in range(2):
            p1[k, 2 + side].wait_recv()

    def event3(k):
        for i in (0, 1, 3, 2):
            side = 0 if i < 2 else 1
            step = (1, 3)[side]
            p2[k, i, side].wait_recv()
            device = (shard(0, step), s)
            p2[k, i, 2] = along(k, i, 4 - step, full, p2s.at[k, i, 2], p2r.at[k, i, 2], device)
            p2[k, i, 1 - side].wait_recv()
        for i in range(4):
            to_y(k, i, 3)
            to_y(k, i, 1)

    sib_done = {}

    def to_sibling(k):
        ref = heads.at[2 * k + c]
        sib_done[k] = push(ref, ref, sbs.at[k], sbr.at[k], sibling)

    def event4(k):
        for i in range(4):
            p2[k, i, 2].wait_recv()
            to_y(k, i, 2)
        to_sibling(k)

    for copy in own_cols:
        copy.wait()
    pl.semaphore_wait(barrier, len(peers))
    hop(0)
    spread(0, 0)
    hop(1)
    hop(2)

    feats = feat_ref[...]
    feats32 = feats.astype(F32)
    cross = nn(feats, w_cross_ref[...]) + b_cross_ref[...].astype(F32).reshape(1, 512)
    crossed[...] = (feats32 * cross + feats32).astype(BF)
    ct[...] = flip(crossed[...])
    ft[...] = flip(feats)
    ct_copy = push(ct, ct_sib, scs.at[0], scr.at[0], sibling)
    ft_copy = push(ft, ft_sib, scs.at[1], scr.at[1], sibling)
    scores[...] = jnp.broadcast_to(b_score_ref[...].astype(F32), scores.shape)
    hop_pass(0)
    spread(0, 3)
    spread(0, 1)
    hop_pass(1)
    hop_pass(2)
    b_deep32 = b_deep_ref[...].astype(F32).reshape(1, 4096)

    def forward(j):
        cols = slice(j * 512, j * 512 + 512)
        pre = nn(crossed[...], w_deep_ref[:, cols]) + b_deep32[:, cols]
        sigma = 0.5 + 0.5 * jnp.tanh(0.5 * pre)
        hidden = (pre * sigma).astype(BF)
        slope[j] = sigma * (1.0 + pre * (1.0 - sigma))
        hid_t[cols, :] = hidden.T
        scores[...] += nn(hidden, w_score_ref[cols, :])

    loads[0].wait()
    loads[1].wait()
    for j in range(4):
        forward(j)
    hop_end(0)
    spread(0, 2)
    for k in (1, 2):
        hop_end(k)
    for i in range(4):
        spread(1, i)
    for j in range(4, 8):
        forward(j)

    table_pad[...] = jnp.zeros_like(table_pad)
    table_pad[0:16] = table_ref[...]
    loads[2].wait()

    def embed(i):
        rows = slice(i * 256, i * 256 + 256)
        kinds = lax.broadcasted_iota(jnp.int32, (128, 256), 0)
        onehot = flip(kinds == ids_ref[:, rows])
        hist[rows, :] = (emb[rows, :].astype(F32) + nn(onehot, table_pad[...])).astype(BF)

    for i in range(4):
        embed(i)
    event3(0)
    for i in range(4):
        spread(2, i)
    where_col = jnp.broadcast_to(cand_ref[...], (128, 256)).astype(F32).T[:, 0:1]
    places = lax.broadcasted_iota(jnp.int32, (256, 1024), 1).astype(F32)
    segs = segs_ref[...].astype(F32)
    chosen = (places == where_col).astype(F32)
    picked[...] = nn(chosen.astype(BF), hist[...]).astype(BF)
    seg_col = jnp.sum(chosen * segs, axis=1, keepdims=True)
    mask[...] = jnp.where((segs == seg_col) & (places <= where_col), 1.0, 0.0)
    base[...] = nn(picked[...], w_head_ref[...])
    event4(0)

    def attend(k):
        low, high = heads[2 * k].reshape(1024, 512), heads[2 * k + 1].reshape(1024, 512)

        def columns(part):
            cols = slice(128 * part, 128 * part + 128)
            return [low[:, cols], high[:, cols]]

        w_pair = jnp.concatenate(columns(2) + columns(3), axis=1)
        qrows = silu(nn(picked[...], w_pair)).astype(BF)
        w_pair = jnp.concatenate(columns(0) + columns(1), axis=1)
        kv[...] = silu(nn(hist[...], w_pair)).astype(BF)
        for i in range(2):
            head = head_of(k, i)
            gate[head] = qrows[:, 128 * i : 128 * i + 128]
            cols = slice(256 + 128 * i, 384 + 128 * i)
            half = nt(qrows[:, cols], kv[:, cols]) * (0.5 * 128 ** (-0.5))
            weights = ((half + half * jnp.tanh(half)) * mask[...]).astype(BF)
            mixed[head] = nn(weights, kv[:, 128 * i : 128 * i + 128])

    dest = owners_ref[...]
    kinds = lax.broadcasted_iota(jnp.int32, (16, 256), 0)
    hits = (kinds == dest).astype(F32)
    upper = (
        lax.broadcasted_iota(jnp.int32, (256, 256), 0)
        < lax.broadcasted_iota(jnp.int32, (256, 256), 1)
    ).astype(BF)
    before = nn(hits.astype(BF), upper)
    rank = jnp.sum(before * hits, axis=0, keepdims=True).astype(jnp.int32)
    slot = dest * CAP + rank
    place = (lax.broadcasted_iota(jnp.int32, (512, 256), 0) == slot).astype(BF)
    placed = nn(place, scores[...].astype(BF)).astype(BF).reshape(16, CAP, 128)
    place_out[...] = placed
    rows_in[t] = place_out[t]
    row_copies = []
    for k in range(1, 16):
        to = (t + k) % 16
        row_copies.append(push(place_out.at[to], rows_in.at[t], srs.at[k], srr.at[k], (to, s)))

    own_out = nn(w_out_ref[...], w_head_ref[...]).astype(BF)
    out_head[t] = own_out
    mine_rows = pl.ds(pl.multiple_of(32 * c, 32), 32)
    oh_copies = []
    for k in range(1, 16):
        ref = out_head.at[t, mine_rows]
        oh_copies.append(push(ref, ref, ohs.at[k], ohr.at[k], ((t + k) % 16, s)))
    event3(1)
    sib_done[0].wait_recv()
    attend(0)
    event4(1)
    event3(2)
    for copy in ups_done:
        copy.wait_recv()
    to_sibling(3)
    sib_done[1].wait_recv()
    attend(1)
    event4(2)
    for copy in oh_copies:
        copy.wait_recv()
    every = out_head.at[:, mine_rows]
    oh_sib = push(every, every, ohs.at[0], ohr.at[0], sibling)
    sib_done[3].wait_recv()
    attend(3)
    sib_done[2].wait_recv()
    attend(2)

    centre = jnp.sum(jnp.sum(mixed[...], axis=0), axis=1, keepdims=True) * (1.0 / 1024.0)
    spread_sum = jnp.sum(jnp.square(mixed[...] - centre[None]), axis=0)
    scale_rows = lax.rsqrt(jnp.sum(spread_sum, axis=1, keepdims=True) * (1.0 / 1024.0) + EPS)
    for head in range(8):
        normed = (mixed[head] - centre) * scale_rows
        joined[:, 128 * head : 128 * head + 128] = (normed * gate[head].astype(F32)).astype(BF)
    oh_sib.wait_recv()
    logits = base[...] + nn(joined[...], out_head[...].reshape(1024, 128))

    delta = scores[...] - logits.astype(BF).astype(F32)
    delta16 = delta.astype(BF)
    bscore = jnp.sum(delta, axis=0, keepdims=True)

    def back_chunk(j):
        rows = pl.ds(pl.multiple_of(j * 512, 512), 512)
        dpre = nt(delta16, w_score_ref[rows, :]) * slope[j]
        d_own[j] = dpre.astype(BF)
        bd[j] = jnp.broadcast_to(jnp.sum(dpre, axis=0, keepdims=True), (8, 512))

    d_copies = []
    for q in range(4):
        j = (1 - c) * 4 + q
        back_chunk(j)
        d_copies.append(push(d_own.at[j], d_sib.at[q], scs.at[2 + q], scr.at[2 + q], sibling))
    for i in range(8):
        g = nn(hid_t[512 * i : 512 * i + 512, :], delta16).astype(BF).reshape(8, 2, 2, 16, 128)
        for core in range(2):
            gs[core, 8 * i : 8 * i + 8, :, 0:128] = g[:, core, 0]
            gs[core, 8 * i : 8 * i + 8, :, 128:256] = g[:, core, 1]
    gs_copy = push(gs.at[1 - c], gs_sib, scs.at[6], scr.at[6], sibling)
    for q in range(4):
        back_chunk(c * 4 + q)
    every_dpre = jnp.concatenate([d_own[j] for j in range(8)], axis=1)
    dcr = nt(every_dpre, w_deep_ref[...]) * feats32
    bcross = jnp.sum(dcr, axis=0, keepdims=True)
    dc[0] = dcr[:, :256].astype(BF)
    dc[1] = dcr[:, 256:].astype(BF)
    dc_copy = push(dc.at[1 - c], dc_sib, scs.at[7], scr.at[7], sibling)

    def axes_of(u):
        axis = ROUTES[u // 2][0]
        rest = [a for a in range(3) if a != axis]
        return axis, rest

    def piece(u, where, half):
        axis, rest = axes_of(u)
        index = [slice(None)] * 3
        index[axis] = where
        index[rest[0]] = pl.ds(2 * half, 2)
        return (u, *index)

    def stage1_first(u):
        axis, _ = axes_of(u)
        m = pos[axis]
        right, left, opp = (m + 1) % 4, (m + 3) % 4, (m + 2) % 4
        to_right, to_left = at_chip(axis, right, c), at_chip(axis, left, c)
        return (
            push(grads.at[piece(u, opp, 0)], x1.at[u, 0], s1s.at[u, 0], s1r.at[u, 0], to_right),
            push(grads.at[piece(u, opp, 1)], x1.at[u, 1], s1s.at[u, 1], s1r.at[u, 1], to_left),
        )

    def stage1_second(u):
        axis, _ = axes_of(u)
        m = pos[axis]
        right, left = (m + 1) % 4, (m + 3) % 4
        to_right, to_left = at_chip(axis, right, c), at_chip(axis, left, c)
        return (
            push(grads.at[piece(u, right, 1)], x2.at[u, 0], s1s.at[u, 2], s1r.at[u, 2], to_right),
            push(grads.at[piece(u, left, 0)], x2.at[u, 1], s1s.at[u, 3], s1r.at[u, 3], to_left),
        )

    def stage1_pass(u, started):
        axis, _ = axes_of(u)
        m = pos[axis]
        right, left = (m + 1) % 4, (m + 3) % 4
        out = []
        for side, (where, device) in enumerate(
            ((right, at_chip(axis, right, c)), (left, at_chip(axis, left, c)))
        ):
            started[side].wait_recv()
            mine = grads[piece(u, where, side)].astype(F32)
            y3[u, side] = (mine + x1[u, side].astype(F32)).astype(BF)
            out.append(
                push(y3.at[u, side], x3.at[u, side], s1s.at[u, 4 + side], s1r.at[u, 4 + side], device)
            )
        return out

    def stage1_end(u, started, passed):
        axis, _ = axes_of(u)
        m = pos[axis]
        for copy in (started[2], started[3], passed[0], passed[1]):
            copy.wait_recv()
        for half in range(2):
            total = grads[piece(u, m, half)].astype(F32)
            total += x2[u, 1 - half].astype(F32) + x3[u, half].astype(F32)
            w1[u // 2, u % 2, 2 * half : 2 * half + 2] = total.astype(BF)

    started, passed = {}, {}

    gs_copy.wait_recv()
    summed = gs[c].astype(F32) + gs_sib[...].astype(F32)
    grads[0] = summed.astype(BF).reshape(4, 4, 4, 16, 256)
    started[0] = stage1_first(0)

    ct_copy.wait_recv()
    for q in (1, 3, 0, 2):
        d_copies[q].wait_recv()
        g = nn(ct[...], d_own[c * 4 + q]) + nn(ct_sib[...], d_sib[q])
        g = g.reshape(64, 8, 512)
        g = jnp.concatenate([g[:, :, :256], g[:, :, 256:]], axis=1)
        grads[1 + q] = g.astype(BF).reshape(4, 4, 4, 16, 256)
        started[1 + q] = stage1_first(1 + q)

    sub = lax.broadcasted_iota(jnp.int32, (16, 128), 0)
    for pair in range(32):
        deep_row = bd[pair // 4, 0:1, (pair % 4) * 128 : (pair % 4) * 128 + 128]
        cross_row = bcross[:, (pair // 8) * 128 : (pair // 8) * 128 + 128]
        tile = jnp.where(sub == 0, deep_row, jnp.where(sub == 1, cross_row, bscore))
        tile = tile.astype(BF)
        for chip in (2 * pair, 2 * pair + 1):
            grads[5, chip // 16, chip // 4 % 4, chip % 4, :, 128:256] = tile
    ft_copy.wait_recv()
    dc_copy.wait_recv()
    g = nn(ft[...], dc[c]) + nn(ft_sib[...], dc_sib[...])
    g = g.reshape(64, 8, 256)
    g = jnp.concatenate([g[:, :, :128], g[:, :, 128:]], axis=1)
    grads[5, :, :, :, :, 0:128] = g.astype(BF).reshape(4, 4, 4, 16, 128)
    started[5] = stage1_first(5)
    for u in (0, 2, 4, 1, 3, 5):
        started[u] += stage1_second(u)
    for u in (0, 2, 4, 1, 3, 5):
        passed[u] = stage1_pass(u, started[u])

    def piece2(r, where, half):
        axis, second, _ = ROUTES[r]
        rest = [a for a in range(3) if a != axis]
        index = [None, None]
        index[rest.index(second)] = where
        index[1 - rest.index(second)] = pl.ds(2 * half, 2)
        return (r, slice(None), *index)

    def stage2_start(r):
        axis = ROUTES[r][1]
        m = pos[axis]
        right, left, opp = (m + 1) % 4, (m + 3) % 4, (m + 2) % 4
        to_right, to_left = at_chip(axis, right, c), at_chip(axis, left, c)
        return (
            push(w1.at[piece2(r, opp, 0)], v1.at[r, 0], s2s.at[r, 0], s2r.at[r, 0], to_right),
            push(w1.at[piece2(r, opp, 1)], v1.at[r, 1], s2s.at[r, 1], s2r.at[r, 1], to_left),
            push(w1.at[piece2(r, right, 1)], v2.at[r, 0], s2s.at[r, 2], s2r.at[r, 2], to_right),
            push(w1.at[piece2(r, left, 0)], v2.at[r, 1], s2s.at[r, 3], s2r.at[r, 3], to_left),
        )

    def stage2_pass(r, begun):
        axis = ROUTES[r][1]
        m = pos[axis]
        out = []
        for side, where in enumerate(((m + 1) % 4, (m + 3) % 4)):
            begun[side].wait_recv()
            mine = w1[piece2(r, where, side)].astype(F32)
            u3[r, side] = (mine + v1[r, side].astype(F32)).astype(BF)
            out.append(
                push(
                    u3.at[r, side],
                    v3.at[r, side],
                    s2s.at[r, 4 + side],
                    s2r.at[r, 4 + side],
                    at_chip(axis, where, c),
                )
            )
        return out

    def stage2_end(r, begun, handed):
        axis, _ = ROUTES[r][1], None
        m = pos[axis]
        for copy in (begun[2], begun[3], handed[0], handed[1]):
            copy.wait_recv()
        for half in range(2):
            total = w1[piece2(r, m, half)].astype(F32)
            total += v2[r, 1 - half].astype(F32) + v3[r, half].astype(F32)
            w2[r, :, 2 * half : 2 * half + 2] = total.astype(BF)

    def stage3_start(r):
        axis = ROUTES[r][2]
        m = pos[axis]
        last[r, m, c] = w2[r, :, m]
        for k in range(4):
            where = (m + k) % 4
            for other in range(2):
                if k == 0 and other == 0:
                    continue
                core = c if other == 0 else 1 - c
                push(
                    w2.at[r, :, where],
                    last.at[r, m, c],
                    s3s.at[r, k, other],
                    s3r.at[r, k, other],
                    at_chip(axis, where, core),
                )

    def stage3_end(r):
        axis = ROUTES[r][2]
        m = pos[axis]
        for k in range(4):
            where = (m + 4 - k) % 4
            for other in range(2):
                if k == 0 and other == 0:
                    continue
                core = c if other == 0 else 1 - c
                pltpu.make_async_remote_copy(
                    src_ref=last.at[r, where, core],
                    dst_ref=last.at[r, where, core],
                    send_sem=s3s.at[r, k, other],
                    recv_sem=s3r.at[r, k, other],
                    device_id=at_chip(axis, where, core),
                    device_id_type=MESH,
                ).wait_recv()
        scale = 1.0 / 32768.0
        for core in range(2):
            total = last[r, 0, core].astype(F32)
            for k in range(1, 4):
                total += last[r, k, core].astype(F32)
            fin[core, 2 * r : 2 * r + 2] = total * scale

    begun, handed = {}, {}
    for r in range(3):
        for u in (2 * r, 2 * r + 1):
            stage1_end(u, started[u], passed[u])
        begun[r] = stage2_start(r)
    for r in range(3):
        handed[r] = stage2_pass(r, begun[r])
    for r in range(3):
        stage2_end(r, begun[r], handed[r])
        stage3_start(r)
    for copy in row_copies:
        copy.wait_recv()
    o_rows[...] = rows_in[...]
    for r in range(3):
        stage3_end(r)

    def own_rows(core, unit, half, cols):
        lower = fin[core, unit, 8 * half : 8 * half + 4, cols]
        higher = fin[core, unit, 8 * half + 4 : 8 * half + 8, cols]
        return jnp.where(c == 0, lower, higher)

    for core in range(2):
        for half in range(2):
            for q in range(4):
                at = core * 2048 + q * 512 + half * 256
                o_deep[:, at : at + 256] = own_rows(core, 1 + q, half, slice(0, 256))
            at = core * 256 + half * 128
            o_cross[:, at : at + 128] = own_rows(core, 5, half, slice(0, 128))
    for half in range(2):
        cols = slice(128 * half, 128 * half + 128)
        o_score[16 * half : 16 * half + 16] = jnp.where(c == 0, fin[0, 0, :, cols], fin[1, 0, :, cols])
    chip = t * 4 + y
    bias = fin[0, 5, 0:8, 128:256] + fin[1, 5, 0:8, 128:256]
    for row, first in enumerate((chip % 2 * 64 + c * 32, chip % 16 * 8 + c * 4, chip * 2 + c)):
        o_bias[row : row + 1] = pltpu.roll(bias, (128 - first) % 128, 1)[row : row + 1]
    for copy in sends:
        copy.wait_send()


def results(cross, deep, score, bias, rows, o_cross, o_bcross, o_deep, o_bdeep, o_score, o_bscore, o_rows):
    o_cross[...] = cross[...]
    o_deep[...] = deep[...]
    o_score[...] = score[...]
    o_rows[...] = rows[...]
    o_bdeep[...] = bias[0, 0:32]
    o_bcross[...] = bias[1, 0:4]
    o_bscore[...] = bias[2, 0:1]


def local(
    embeddings,
    action_ids,
    segment_ids,
    cand_pos,
    owners,
    features,
    action_table,
    w_query,
    w_keys,
    w_out,
    w_head,
    w_cross,
    b_cross,
    w_deep,
    b_deep,
    w_score,
    b_score,
):
    dma = pltpu.SemaphoreType.DMA
    vmem = pltpu.VMEM
    whole = pl.BlockSpec(memory_space=pltpu.VMEM)
    stay = pl.BlockSpec(memory_space=pl.ANY)
    g_cross, g_deep, g_score, bias, rows = pl.pallas_call(
        kernel,
        out_shape=(
            jax.ShapeDtypeStruct((4, 512), F32),
            jax.ShapeDtypeStruct((4, 4096), F32),
            jax.ShapeDtypeStruct((32, 128), F32),
            jax.ShapeDtypeStruct((8, 128), F32),
            jax.ShapeDtypeStruct((16, CAP, 128), BF),
        ),
        in_specs=[stay] + [whole] * 6 + [stay] * 2 + [whole] * 4 + [stay, whole, stay, whole],
        out_specs=(whole,) * 5,
        scratch_shapes=[
            vmem((1024, 1024), BF),
            vmem((512, 4096), BF),
            vmem((4096, 128), BF),
            vmem((8, 16, 64, 512), BF),
            vmem((16, 64, 128), BF),
            vmem((128, 1024), BF),
            vmem((1024, 1024), BF),
            vmem((256, 1024), BF),
            vmem((256, 1024), F32),
            vmem((1024, 512), BF),
            vmem((8, 256, 128), BF),
            vmem((8, 256, 128), F32),
            vmem((256, 1024), BF),
            vmem((256, 128), F32),
            vmem((256, 512), BF),
            vmem((512, 256), BF),
            vmem((512, 256), BF),
            vmem((512, 256), BF),
            vmem((512, 256), BF),
            vmem((4096, 256), BF),
            vmem((8, 256, 512), F32),
            vmem((256, 128), F32),
            vmem((16, CAP, 128), BF),
            vmem((16, CAP, 128), BF),
            vmem((8, 256, 512), BF),
            vmem((4, 256, 512), BF),
            vmem((2, 64, 16, 256), BF),
            vmem((64, 16, 256), BF),
            vmem((2, 256, 256), BF),
            vmem((256, 256), BF),
            vmem((8, 8, 512), F32),
            vmem((6, 4, 4, 4, 16, 256), BF),
            vmem((6, 2, 2, 4, 16, 256), BF),
            vmem((6, 2, 2, 4, 16, 256), BF),
            vmem((6, 2, 2, 4, 16, 256), BF),
            vmem((6, 2, 2, 4, 16, 256), BF),
            vmem((3, 2, 4, 4, 16, 256), BF),
            vmem((3, 2, 2, 2, 16, 256), BF),
            vmem((3, 2, 2, 2, 16, 256), BF),
            vmem((3, 2, 2, 2, 16, 256), BF),
            vmem((3, 2, 2, 2, 16, 256), BF),
            vmem((3, 2, 4, 16, 256), BF),
            vmem((3, 4, 2, 2, 16, 256), BF),
            vmem((2, 6, 16, 256), F32),
            dma((6, 6)),
            dma((6, 6)),
            dma((3, 6)),
            dma((3, 6)),
            dma((3, 4, 2)),
            dma((3, 4, 2)),
            dma((8,)),
            dma((8,)),
            dma((16,)),
            dma((16,)),
            dma((3,)),
            dma((3, 4)),
            dma((3, 4)),
            dma((3, 4)),
            dma((3, 4, 3)),
            dma((3, 4, 3)),
            dma((16,)),
            dma((16,)),
            dma((4,)),
            dma((4,)),
            dma((16,)),
            dma((16,)),
        ],
        compiler_params=pltpu.CompilerParams(
            collective_id=0, has_side_effects=True, vmem_limit_bytes=56 * 1024 * 1024
        ),
    )(
        embeddings,
        action_ids.reshape(1, -1),
        segment_ids,
        cand_pos.reshape(1, -1),
        owners.reshape(1, -1),
        features,
        action_table,
        w_query,
        w_keys,
        w_out,
        w_head,
        w_cross,
        b_cross,
        w_deep,
        b_deep,
        w_score,
        b_score.reshape(1, -1),
    )
    return pl.pallas_call(
        results,
        out_shape=(
            jax.ShapeDtypeStruct((4, 512), F32),
            jax.ShapeDtypeStruct((4,), F32),
            jax.ShapeDtypeStruct((4, 4096), F32),
            jax.ShapeDtypeStruct((32,), F32),
            jax.ShapeDtypeStruct((32, 128), F32),
            jax.ShapeDtypeStruct((1,), F32),
            jax.ShapeDtypeStruct((512, 128), BF),
        ),
        in_specs=[whole] * 5,
        out_specs=(whole,) * 7,
    )(g_cross, g_deep, g_score, bias, rows.reshape(512, 128))


def solution(mesh):
    both = ("teacher", "student")
    return jax.shard_map(
        local,
        mesh=mesh,
        in_specs=(
            P(both, None),
            P(both),
            P(both, None),
            P(both),
            P(both, None),
            P(both, None),
            P(),
            P("teacher", None),
            P("teacher", None),
            P("teacher", None),
            P(),
            P(),
            P(),
            P(),
            P(),
            P(),
            P(),
        ),
        out_specs=(
            P(both, None),
            P(both),
            P(both, None),
            P(both),
            P(both, None),
            P(both),
            P(both, None),
        ),
        check_vma=False,
    )
```

```python
import functools

import jax
import jax.numpy as jnp
from jax import lax
from jax.experimental import pallas as pl
from jax.experimental.pallas import tpu as pltpu
from jax.sharding import PartitionSpec as P

CAP = 32
EPS = 1e-05
BF = jnp.bfloat16
F32 = jnp.float32
MESH = pl.DeviceIdType.MESH

ROUTES = ((0, 1, 2), (1, 2, 0), (2, 0, 1))


def nn(a, b):
    return lax.dot_general(a, b, (((1,), (0,)), ((), ())), preferred_element_type=F32)


def nt(a, b):
    return lax.dot_general(a, b, (((1,), (1,)), ((), ())), preferred_element_type=F32)


def silu(v):
    half = 0.5 * v
    return half + half * jnp.tanh(half)


def flip(v):
    return v.astype(F32).T.astype(BF)


def kernel(
    emb_hbm,
    ids_ref,
    segs_ref,
    cand_ref,
    owners_ref,
    feat_ref,
    table_ref,
    w_query_hbm,
    w_keys_hbm,
    w_out_ref,
    w_head_ref,
    w_cross_ref,
    b_cross_ref,
    w_deep_hbm,
    b_deep_ref,
    w_score_hbm,
    b_score_ref,
    o_cross,
    o_deep,
    o_score,
    o_bias,
    o_rows,
    emb,
    w_deep_ref,
    w_score_ref,
    heads,
    out_head,
    own_half,
    table_pad,
    hist,
    picked,
    mask,
    kv,
    gate,
    gate_out,
    mixed,
    mixed_out,
    joined,
    base,
    crossed,
    ct,
    ct_sib,
    ft,
    ft_sib,
    hid_t,
    slope,
    scores,
    place_out,
    rows_in,
    d_own,
    d_sib,
    gs,
    gs_sib,
    dc,
    dc_sib,
    bd,
    grads,
    x1,
    x2,
    x3,
    y3,
    w1,
    v1,
    w2,
    last,
    fin,
    s1s,
    s1r,
    s2s,
    s2r,
    s3s,
    s3r,
    scs,
    scr,
    srs,
    srr,
    lds,
    hds,
    p1s,
    p1r,
    p2s,
    p2r,
    ups,
    upr,
    sbs,
    sbr,
    ohs,
    ohr,
):
    t = lax.axis_index("teacher")
    s = lax.axis_index("student")
    z, x = t // 4, t % 4
    y, c = s // 2, s % 2
    pos = (z, x, y)
    sibling = (t, y * 2 + 1 - c)
    sends = []

    def at_chip(axis, value, core):
        p = list(pos)
        p[axis] = value
        return (p[0] * 4 + p[1], p[2] * 2 + core)

    def push(src, dst, send_sem, recv_sem, device):
        copy = pltpu.make_async_remote_copy(
            src_ref=src,
            dst_ref=dst,
            send_sem=send_sem,
            recv_sem=recv_sem,
            device_id=device,
            device_id_type=MESH,
        )
        copy.start()
        sends.append(copy)
        return copy

    peers = [((t + k) % 16, s) for k in range(1, 16)] + [sibling]
    peers += [at_chip(2, (y + k) % 4, c) for k in range(1, 4)]
    peers += [at_chip(axis, (pos[axis] + k) % 4, 1 - c) for axis in range(3) for k in range(1, 4)]
    barrier = pltpu.get_barrier_semaphore()
    for peer in peers:
        pl.semaphore_signal(barrier, inc=1, device_id=peer, device_id_type=MESH)

    odd = y % 2
    first = (1 - c) * x + c * z
    second = (1 - c) * z + c * x

    def shard(i, j):
        i, j = (first + i) % 4, (second + j) % 4
        return (1 - c) * (j * 4 + i) + c * (i * 4 + j)

    def head_of(k, core):
        return (4 + 2 * odd + core, core, 2 + core, 6 - 2 * odd + core)[k]

    own_cols = []
    for k in range(3):
        for part, (ref, start) in enumerate(
            ((w_keys_hbm, 0), (w_keys_hbm, 1024), (w_query_hbm, 0), (w_query_hbm, 1024))
        ):
            cols = pl.ds(pl.multiple_of(start + head_of(k, c) * 128, 128), 128)
            own_cols.append(
                pltpu.make_async_copy(
                    ref.at[:, cols],
                    heads.at[k, t, :, 128 * part : 128 * part + 128],
                    hds.at[k, part],
                )
            )
            own_cols[-1].start()
    loads = [
        pltpu.make_async_copy(w_deep_hbm, w_deep_ref, lds.at[0]),
        pltpu.make_async_copy(w_score_hbm, w_score_ref, lds.at[1]),
        pltpu.make_async_copy(emb_hbm, emb, lds.at[2]),
    ]
    for load in loads:
        load.start()

    def along(k, i, j, rows, send_sem, recv_sem, device):
        ref = heads.at[k, shard(i, j), rows]
        return push(ref, ref, send_sem, recv_sem, device)

    full = slice(0, 64)
    y_next = (t, (y + 1 + 2 * c) % 4 * 2 + c)
    p1, p2, ups_done = {}, {}, []

    def to_y(k, i, j):
        if k == 0:
            n = (i % 4) * 4 + j % 4
            up = heads.at[0, shard(i, j)]
            ups_done.append(push(up, heads.at[3, shard(i, j)], ups.at[n], upr.at[n], y_next))

    def spread(k, i):
        for side, step in enumerate((1, 3, 2) if k == 0 else (1, 3)):
            device = (shard(0, step), s)
            p2[k, i, side] = along(k, i, 0, full, p2s.at[k, i, side], p2r.at[k, i, side], device)
        to_y(k, i, 0)

    def hop(k):
        for side, step in enumerate((1, 3, 2)):
            device = (shard(step, 0), s)
            p1[k, side] = along(k, 0, 0, full, p1s.at[k, side], p1r.at[k, side], device)

    def hop_end(k):
        for side in range(3):
            p1[k, side].wait_recv()

    def arrive(i):
        for side, j in enumerate((3, 1, 2)):
            p2[0, i, side].wait_recv()
            to_y(0, i, j)

    def event3(k):
        for i in (0, 1, 3, 2):
            side = 0 if i < 2 else 1
            step = (1, 3)[side]
            p2[k, i, side].wait_recv()
            device = (shard(0, step), s)
            p2[k, i, 2] = along(k, i, 4 - step, full, p2s.at[k, i, 2], p2r.at[k, i, 2], device)
            p2[k, i, 1 - side].wait_recv()

    def event4(k):
        for i in range(4):
            p2[k, i, 2].wait_recv()

    for copy in own_cols:
        copy.wait()
    pl.semaphore_wait(barrier, len(peers))
    hop(0)
    spread(0, 0)
    hop(1)
    hop(2)

    feats = feat_ref[...]
    feats32 = feats.astype(F32)
    cross = nn(feats, w_cross_ref[...]) + b_cross_ref[...].astype(F32).reshape(1, 512)
    crossed[...] = (feats32 * cross + feats32).astype(BF)
    ct[...] = flip(crossed[...])
    ft[...] = flip(feats)
    ct_copy = push(ct, ct_sib, scs.at[0], scr.at[0], sibling)
    ft_copy = push(ft, ft_sib, scs.at[1], scr.at[1], sibling)
    scores[...] = jnp.broadcast_to(b_score_ref[...].astype(F32), scores.shape)
    table_pad[...] = jnp.zeros_like(table_pad)
    table_pad[0:16] = table_ref[...]
    loads[2].wait()

    def embed(i):
        rows = slice(i * 256, i * 256 + 256)
        kinds = lax.broadcasted_iota(jnp.int32, (128, 256), 0)
        onehot = flip(kinds == ids_ref[:, rows])
        hist[0, rows, :] = (emb[rows, :].astype(F32) + nn(onehot, table_pad[...])).astype(BF)

    for i in range(4):
        embed(i)
    hist_copy = push(hist.at[0], hist.at[1], sbs.at[0], sbr.at[0], sibling)
    hop_end(0)
    for i in (3, 1, 2):
        spread(0, i)
    b_deep32 = b_deep_ref[...].astype(F32).reshape(1, 4096)

    def forward(j):
        cols = slice(j * 512, j * 512 + 512)
        pre = nn(crossed[...], w_deep_ref[:, cols]) + b_deep32[:, cols]
        sigma = 0.5 + 0.5 * jnp.tanh(0.5 * pre)
        hidden = (pre * sigma).astype(BF)
        slope[j] = sigma * (1.0 + pre * (1.0 - sigma))
        hid_t[cols, :] = hidden.T
        scores[...] += nn(hidden, w_score_ref[cols, :])

    loads[0].wait()
    loads[1].wait()
    for j in range(2):
        forward(j)
    for k in (1, 2):
        hop_end(k)
        for i in range(4):
            spread(k, i)

    where_col = jnp.broadcast_to(cand_ref[...], (128, 256)).astype(F32).T[:, 0:1]
    places = lax.broadcasted_iota(jnp.int32, (256, 1024), 1).astype(F32)
    segs = segs_ref[...].astype(F32)
    chosen = (places == where_col).astype(F32)
    picked[0:256] = nn(chosen.astype(BF), hist[0]).astype(BF)
    seg_col = jnp.sum(chosen * segs, axis=1, keepdims=True)
    mask[0] = jnp.where((segs == seg_col) & (places <= where_col), 1.0, 0.0)
    base[...] = nn(picked[0:256], w_head_ref[...])
    picked_copy = push(picked.at[0:256], picked.at[256:512], sbs.at[1], sbr.at[1], sibling)
    mask_copy = push(mask.at[0], mask.at[1], sbs.at[2], sbr.at[2], sibling)
    arrive(0)
    for j in range(2, 5):
        forward(j)
    arrive(3)
    arrive(1)
    for j in range(5, 8):
        forward(j)
    arrive(2)

    att_done = []

    def attend(k, between=None):
        head = head_of(k, c)
        columns = heads[k].reshape(1024, 512)
        qrows = silu(nn(picked[...], columns[:, 256:512])).astype(BF)
        gate[head] = qrows[:256, :128]
        gate_out[k] = qrows[256:, :128]
        for side in (1, 0):
            kv[side] = silu(nn(hist[side], columns[:, :256])).astype(BF)
        if between is not None:
            between()
        for side in (1, 0):
            half = nt(qrows[256 * side : 256 * side + 256, 128:], kv[side, :, 128:])
            half = half * (0.5 * 128 ** (-0.5))
            weights = ((half + half * jnp.tanh(half)) * mask[side]).astype(BF)
            result = nn(weights, kv[side, :, :128])
            if side == 0:
                mixed[head] = result
            else:
                mixed_out[k] = result
                for n, (src, dst) in enumerate(((mixed_out, mixed), (gate_out, gate))):
                    n += 3 + 2 * k
                    att_done.append(push(src.at[k], dst.at[head], sbs.at[n], sbr.at[n], sibling))

    dest = owners_ref[...]
    kinds = lax.broadcasted_iota(jnp.int32, (16, 256), 0)
    hits = (kinds == dest).astype(F32)
    upper = (
        lax.broadcasted_iota(jnp.int32, (256, 256), 0)
        < lax.broadcasted_iota(jnp.int32, (256, 256), 1)
    ).astype(BF)
    before = nn(hits.astype(BF), upper)
    rank = jnp.sum(before * hits, axis=0, keepdims=True).astype(jnp.int32)
    slot = dest * CAP + rank
    place = (lax.broadcasted_iota(jnp.int32, (512, 256), 0) == slot).astype(BF)
    own_out = nn(w_out_ref[...], w_head_ref[...]).astype(BF)
    own_half[...] = own_out
    mine_rows = pl.ds(pl.multiple_of(32 * c, 32), 32)
    placed = nn(place, scores[...].astype(BF)).astype(BF).reshape(16, CAP, 128)
    place_out[:, :CAP] = placed
    place_out[:, CAP:] = jnp.broadcast_to(own_half[mine_rows, :][None], (16, 32, 128))
    rows_in[t] = place_out[t]
    row_copies = []
    for k in range(1, 16):
        to = (t + k) % 16
        row_copies.append(push(place_out.at[to], rows_in.at[t], srs.at[k], srr.at[k], (to, s)))

    event3(1)
    for copy in (hist_copy, picked_copy, mask_copy):
        copy.wait_recv()
    attend(0, functools.partial(event3, 2))
    event4(1)
    attend(1, functools.partial(event4, 2))
    for copy in row_copies:
        copy.wait_recv()
    out_head[:, mine_rows] = rows_in[:, CAP:]
    every = out_head.at[:, mine_rows]
    oh_sib = push(every, every, ohs.at[0], ohr.at[0], sibling)
    attend(2)
    for copy in ups_done:
        copy.wait_recv()
    attend(3)
    for copy in att_done:
        copy.wait_recv()

    centre = jnp.sum(jnp.sum(mixed[...], axis=0), axis=1, keepdims=True) * (1.0 / 1024.0)
    spread_sum = jnp.sum(jnp.square(mixed[...] - centre[None]), axis=0)
    scale_rows = lax.rsqrt(jnp.sum(spread_sum, axis=1, keepdims=True) * (1.0 / 1024.0) + EPS)
    for head in range(8):
        normed = (mixed[head] - centre) * scale_rows
        joined[:, 128 * head : 128 * head + 128] = (normed * gate[head].astype(F32)).astype(BF)
    oh_sib.wait_recv()
    logits = base[...] + nn(joined[...], out_head[...].reshape(1024, 128))

    delta = scores[...] - logits.astype(BF).astype(F32)
    delta16 = delta.astype(BF)
    bscore = jnp.sum(delta, axis=0, keepdims=True)

    def back_chunk(j):
        rows = pl.ds(pl.multiple_of(j * 512, 512), 512)
        dpre = nt(delta16, w_score_ref[rows, :]) * slope[j]
        d_own[j] = dpre.astype(BF)
        bd[j] = jnp.broadcast_to(jnp.sum(dpre, axis=0, keepdims=True), (8, 512))

    d_copies = {}
    for q in (0, 1, 3, 2):
        j = (1 - c) * 4 + q
        back_chunk(j)
        d_copies[q] = push(d_own.at[j], d_sib.at[q], scs.at[2 + q], scr.at[2 + q], sibling)
    for q in (0, 1, 3, 2):
        back_chunk(c * 4 + q)
    for i in range(8):
        g = nn(hid_t[512 * i : 512 * i + 512, :], delta16).astype(BF).reshape(8, 2, 2, 16, 128)
        for core in range(2):
            gs[core, 8 * i : 8 * i + 8, :, 0:128] = g[:, core, 0]
            gs[core, 8 * i : 8 * i + 8, :, 128:256] = g[:, core, 1]
    gs_copy = push(gs.at[1 - c], gs_sib, scs.at[6], scr.at[6], sibling)
    every_dpre = jnp.concatenate([d_own[j] for j in range(8)], axis=1)
    dcr = nt(every_dpre, w_deep_ref[...]) * feats32
    bcross = jnp.sum(dcr, axis=0, keepdims=True)
    dc[0] = dcr[:, :256].astype(BF)
    dc[1] = dcr[:, 256:].astype(BF)
    dc_copy = push(dc.at[1 - c], dc_sib, scs.at[7], scr.at[7], sibling)

    def axes_of(u):
        axis = ROUTES[u // 2][0]
        rest = [a for a in range(3) if a != axis]
        return axis, rest

    def piece(u, where, half):
        axis, rest = axes_of(u)
        index = [slice(None)] * 3
        index[axis] = where
        index[rest[0]] = pl.ds(2 * half, 2)
        return (u, *index)

    def stage1_first(u):
        axis, _ = axes_of(u)
        m = pos[axis]
        right, left, opp = (m + 1) % 4, (m + 3) % 4, (m + 2) % 4
        to_right, to_left = at_chip(axis, right, c), at_chip(axis, left, c)
        return (
            push(grads.at[piece(u, opp, 0)], x1.at[u, 0], s1s.at[u, 0], s1r.at[u, 0], to_right),
            push(grads.at[piece(u, opp, 1)], x1.at[u, 1], s1s.at[u, 1], s1r.at[u, 1], to_left),
        )

    def stage1_second(u):
        axis, _ = axes_of(u)
        m = pos[axis]
        right, left = (m + 1) % 4, (m + 3) % 4
        to_right, to_left = at_chip(axis, right, c), at_chip(axis, left, c)
        return (
            push(grads.at[piece(u, right, 1)], x2.at[u, 0], s1s.at[u, 2], s1r.at[u, 2], to_right),
            push(grads.at[piece(u, left, 0)], x2.at[u, 1], s1s.at[u, 3], s1r.at[u, 3], to_left),
        )

    def stage1_pass(u, started):
        axis, _ = axes_of(u)
        m = pos[axis]
        right, left = (m + 1) % 4, (m + 3) % 4
        out = []
        for side, (where, device) in enumerate(
            ((right, at_chip(axis, right, c)), (left, at_chip(axis, left, c)))
        ):
            started[side].wait_recv()
            mine = grads[piece(u, where, side)].astype(F32)
            y3[u, side] = (mine + x1[u, side].astype(F32)).astype(BF)
            out.append(
                push(y3.at[u, side], x3.at[u, side], s1s.at[u, 4 + side], s1r.at[u, 4 + side], device)
            )
        return out

    def stage1_end(u, started, passed):
        axis, _ = axes_of(u)
        m = pos[axis]
        for copy in (started[2], started[3], passed[0], passed[1]):
            copy.wait_recv()
        for half in range(2):
            total = grads[piece(u, m, half)].astype(F32)
            total += x2[u, 1 - half].astype(F32) + x3[u, half].astype(F32)
            w1[u // 2, u % 2, 2 * half : 2 * half + 2] = total.astype(BF)

    started, passed = {}, {}

    ct_copy.wait_recv()
    for q in (0, 1, 3, 2):
        d_copies[q].wait_recv()
        g = nn(ct[...], d_own[c * 4 + q]) + nn(ct_sib[...], d_sib[q])
        g = g.reshape(64, 8, 512)
        g = jnp.concatenate([g[:, :, :256], g[:, :, 256:]], axis=1)
        grads[1 + q] = g.astype(BF).reshape(4, 4, 4, 16, 256)
        started[1 + q] = stage1_first(1 + q)

    gs_copy.wait_recv()
    summed = gs[c].astype(F32) + gs_sib[...].astype(F32)
    grads[0] = summed.astype(BF).reshape(4, 4, 4, 16, 256)
    started[0] = stage1_first(0)

    for u in (1, 2, 4):
        started[u] += stage1_second(u)

    sub = lax.broadcasted_iota(jnp.int32, (16, 128), 0)
    for pair in range(32):
        deep_row = bd[pair // 4, 0:1, (pair % 4) * 128 : (pair % 4) * 128 + 128]
        cross_row = bcross[:, (pair // 8) * 128 : (pair // 8) * 128 + 128]
        tile = jnp.where(sub == 0, deep_row, jnp.where(sub == 1, cross_row, bscore))
        tile = tile.astype(BF)
        for chip in (2 * pair, 2 * pair + 1):
            grads[5, chip // 16, chip // 4 % 4, chip % 4, :, 128:256] = tile
    ft_copy.wait_recv()
    dc_copy.wait_recv()
    g = nn(ft[...], dc[c]) + nn(ft_sib[...], dc_sib[...])
    g = g.reshape(64, 8, 256)
    g = jnp.concatenate([g[:, :, :128], g[:, :, 128:]], axis=1)
    grads[5, :, :, :, :, 0:128] = g.astype(BF).reshape(4, 4, 4, 16, 128)
    started[5] = stage1_first(5)
    for u in (3, 0, 5):
        started[u] += stage1_second(u)
    for u in (1, 2, 4, 3, 0, 5):
        passed[u] = stage1_pass(u, started[u])

    def piece2(u, where):
        axis, second, _ = ROUTES[u // 2]
        rest = [a for a in range(3) if a != axis]
        index = [slice(None)] * 2
        index[rest.index(second)] = where
        return (u // 2, u % 2, *index)

    def stage2_start(u):
        axis = ROUTES[u // 2][1]
        m = pos[axis]
        return [
            push(
                w1.at[piece2(u, (m + step) % 4)],
                v1.at[u, k],
                s2s.at[u, k],
                s2r.at[u, k],
                at_chip(axis, (m + step) % 4, c),
            )
            for k, step in enumerate((1, 3, 2))
        ]

    def stage2_end(u, begun):
        total = w1[piece2(u, pos[ROUTES[u // 2][1]])].astype(F32)
        for k, copy in enumerate(begun):
            copy.wait_recv()
            total += v1[u, k].astype(F32)
        w2[u // 2, u % 2] = total.astype(BF)

    def stage3_start(r):
        axis = ROUTES[r][2]
        m = pos[axis]
        last[r, m, c] = w2[r, :, m]
        for k in range(4):
            where = (m + k) % 4
            for other in range(2):
                if k == 0 and other == 0:
                    continue
                core = c if other == 0 else 1 - c
                push(
                    w2.at[r, :, where],
                    last.at[r, m, c],
                    s3s.at[r, k, other],
                    s3r.at[r, k, other],
                    at_chip(axis, where, core),
                )

    def stage3_end(r):
        axis = ROUTES[r][2]
        m = pos[axis]
        for k in range(4):
            where = (m + 4 - k) % 4
            for other in range(2):
                if k == 0 and other == 0:
                    continue
                core = c if other == 0 else 1 - c
                pltpu.make_async_remote_copy(
                    src_ref=last.at[r, where, core],
                    dst_ref=last.at[r, where, core],
                    send_sem=s3s.at[r, k, other],
                    recv_sem=s3r.at[r, k, other],
                    device_id=at_chip(axis, where, core),
                    device_id_type=MESH,
                ).wait_recv()
        scale = 1.0 / 32768.0
        for core in range(2):
            total = last[r, 0, core].astype(F32)
            for k in range(1, 4):
                total += last[r, k, core].astype(F32)
            fin[core, 2 * r : 2 * r + 2] = total * scale

    begun = {}
    for u in (1, 2, 4, 3, 0, 5):
        stage1_end(u, started[u], passed[u])
        begun[u] = stage2_start(u)
    for r in range(3):
        for u in (2 * r, 2 * r + 1):
            stage2_end(u, begun[u])
        stage3_start(r)
    o_rows[...] = rows_in[:, :CAP]
    for r in range(3):
        stage3_end(r)

    def own_rows(core, unit, half, cols):
        lower = fin[core, unit, 8 * half : 8 * half + 4, cols]
        higher = fin[core, unit, 8 * half + 4 : 8 * half + 8, cols]
        return jnp.where(c == 0, lower, higher)

    for core in range(2):
        for half in range(2):
            for q in range(4):
                at = core * 2048 + q * 512 + half * 256
                o_deep[:, at : at + 256] = own_rows(core, 1 + q, half, slice(0, 256))
            at = core * 256 + half * 128
            o_cross[:, at : at + 128] = own_rows(core, 5, half, slice(0, 128))
    for half in range(2):
        cols = slice(128 * half, 128 * half + 128)
        o_score[16 * half : 16 * half + 16] = jnp.where(c == 0, fin[0, 0, :, cols], fin[1, 0, :, cols])
    chip = t * 4 + y
    bias = fin[0, 5, 0:8, 128:256] + fin[1, 5, 0:8, 128:256]
    for row, first in enumerate((chip % 2 * 64 + c * 32, chip % 16 * 8 + c * 4, chip * 2 + c)):
        o_bias[row : row + 1] = pltpu.roll(bias, (128 - first) % 128, 1)[row : row + 1]
    for copy in sends:
        copy.wait_send()


def results(cross, deep, score, bias, rows, o_cross, o_bcross, o_deep, o_bdeep, o_score, o_bscore, o_rows):
    o_cross[...] = cross[...]
    o_deep[...] = deep[...]
    o_score[...] = score[...]
    o_rows[...] = rows[...]
    o_bdeep[...] = bias[0, 0:32]
    o_bcross[...] = bias[1, 0:4]
    o_bscore[...] = bias[2, 0:1]


def local(
    embeddings,
    action_ids,
    segment_ids,
    cand_pos,
    owners,
    features,
    action_table,
    w_query,
    w_keys,
    w_out,
    w_head,
    w_cross,
    b_cross,
    w_deep,
    b_deep,
    w_score,
    b_score,
):
    dma = pltpu.SemaphoreType.DMA
    vmem = pltpu.VMEM
    whole = pl.BlockSpec(memory_space=pltpu.VMEM)
    stay = pl.BlockSpec(memory_space=pl.ANY)
    g_cross, g_deep, g_score, bias, rows = pl.pallas_call(
        kernel,
        out_shape=(
            jax.ShapeDtypeStruct((4, 512), F32),
            jax.ShapeDtypeStruct((4, 4096), F32),
            jax.ShapeDtypeStruct((32, 128), F32),
            jax.ShapeDtypeStruct((8, 128), F32),
            jax.ShapeDtypeStruct((16, CAP, 128), BF),
        ),
        in_specs=[stay] + [whole] * 6 + [stay] * 2 + [whole] * 4 + [stay, whole, stay, whole],
        out_specs=(whole,) * 5,
        scratch_shapes=[
            vmem((1024, 1024), BF),
            vmem((512, 4096), BF),
            vmem((4096, 128), BF),
            vmem((4, 16, 64, 512), BF),
            vmem((16, 64, 128), BF),
            vmem((64, 128), BF),
            vmem((128, 1024), BF),
            vmem((2, 1024, 1024), BF),
            vmem((512, 1024), BF),
            vmem((2, 256, 1024), F32),
            vmem((2, 1024, 256), BF),
            vmem((8, 256, 128), BF),
            vmem((4, 256, 128), BF),
            vmem((8, 256, 128), F32),
            vmem((4, 256, 128), F32),
            vmem((256, 1024), BF),
            vmem((256, 128), F32),
            vmem((256, 512), BF),
            vmem((512, 256), BF),
            vmem((512, 256), BF),
            vmem((512, 256), BF),
            vmem((512, 256), BF),
            vmem((4096, 256), BF),
            vmem((8, 256, 512), F32),
            vmem((256, 128), F32),
            vmem((16, CAP + 32, 128), BF),
            vmem((16, CAP + 32, 128), BF),
            vmem((8, 256, 512), BF),
            vmem((4, 256, 512), BF),
            vmem((2, 64, 16, 256), BF),
            vmem((64, 16, 256), BF),
            vmem((2, 256, 256), BF),
            vmem((256, 256), BF),
            vmem((8, 8, 512), F32),
            vmem((6, 4, 4, 4, 16, 256), BF),
            vmem((6, 2, 2, 4, 16, 256), BF),
            vmem((6, 2, 2, 4, 16, 256), BF),
            vmem((6, 2, 2, 4, 16, 256), BF),
            vmem((6, 2, 2, 4, 16, 256), BF),
            vmem((3, 2, 4, 4, 16, 256), BF),
            vmem((6, 3, 4, 16, 256), BF),
            vmem((3, 2, 4, 16, 256), BF),
            vmem((3, 4, 2, 2, 16, 256), BF),
            vmem((2, 6, 16, 256), F32),
            dma((6, 6)),
            dma((6, 6)),
            dma((6, 3)),
            dma((6, 3)),
            dma((3, 4, 2)),
            dma((3, 4, 2)),
            dma((8,)),
            dma((8,)),
            dma((16,)),
            dma((16,)),
            dma((3,)),
            dma((3, 4)),
            dma((3, 4)),
            dma((3, 4)),
            dma((3, 4, 3)),
            dma((3, 4, 3)),
            dma((16,)),
            dma((16,)),
            dma((11,)),
            dma((11,)),
            dma((1,)),
            dma((1,)),
        ],
        compiler_params=pltpu.CompilerParams(
            collective_id=0, has_side_effects=True, vmem_limit_bytes=56 * 1024 * 1024
        ),
    )(
        embeddings,
        action_ids.reshape(1, -1),
        segment_ids,
        cand_pos.reshape(1, -1),
        owners.reshape(1, -1),
        features,
        action_table,
        w_query,
        w_keys,
        w_out,
        w_head,
        w_cross,
        b_cross,
        w_deep,
        b_deep,
        w_score,
        b_score.reshape(1, -1),
    )
    return pl.pallas_call(
        results,
        out_shape=(
            jax.ShapeDtypeStruct((4, 512), F32),
            jax.ShapeDtypeStruct((4,), F32),
            jax.ShapeDtypeStruct((4, 4096), F32),
            jax.ShapeDtypeStruct((32,), F32),
            jax.ShapeDtypeStruct((32, 128), F32),
            jax.ShapeDtypeStruct((1,), F32),
            jax.ShapeDtypeStruct((512, 128), BF),
        ),
        in_specs=[whole] * 5,
        out_specs=(whole,) * 7,
    )(g_cross, g_deep, g_score, bias, rows.reshape(512, 128))


def solution(mesh):
    both = ("teacher", "student")
    return jax.shard_map(
        local,
        mesh=mesh,
        in_specs=(
            P(both, None),
            P(both),
            P(both, None),
            P(both),
            P(both, None),
            P(both, None),
            P(),
            P("teacher", None),
            P("teacher", None),
            P("teacher", None),
            P(),
            P(),
            P(),
            P(),
            P(),
            P(),
            P(),
        ),
        out_specs=(
            P(both, None),
            P(both),
            P(both, None),
            P(both),
            P(both, None),
            P(both),
            P(both, None),
        ),
        check_vma=False,
    )
```

```python
import functools

import jax
import jax.numpy as jnp
from jax import lax
from jax.experimental import pallas as pl
from jax.experimental.pallas import tpu as pltpu
from jax.sharding import PartitionSpec as P

CAP = 32
EPS = 1e-05
BF = jnp.bfloat16
F32 = jnp.float32
MESH = pl.DeviceIdType.MESH

ROUTES = ((0, 1, 2), (1, 2, 0), (2, 0, 1))


def nn(a, b):
    return lax.dot_general(a, b, (((1,), (0,)), ((), ())), preferred_element_type=F32)


def nt(a, b):
    return lax.dot_general(a, b, (((1,), (1,)), ((), ())), preferred_element_type=F32)


def silu(v):
    half = 0.5 * v
    return half + half * jnp.tanh(half)


def flip(v):
    return v.astype(F32).T.astype(BF)


def kernel(
    emb_hbm,
    ids_hbm,
    segs_hbm,
    cand_hbm,
    owners_hbm,
    feat_hbm,
    table_hbm,
    w_query_hbm,
    w_keys_hbm,
    w_out_hbm,
    w_head_hbm,
    w_cross_hbm,
    b_cross_hbm,
    w_deep_hbm,
    b_deep_hbm,
    w_score_hbm,
    b_score_hbm,
    o_cross,
    o_deep,
    o_score,
    o_bias,
    o_rows,
    ids_ref,
    segs_ref,
    cand_ref,
    owners_ref,
    feat_ref,
    table_ref,
    w_out_ref,
    w_head_ref,
    w_cross_ref,
    b_cross_ref,
    b_deep_ref,
    b_score_ref,
    emb,
    w_deep_ref,
    w_score_ref,
    heads,
    out_head,
    own_half,
    table_pad,
    hist,
    picked,
    mask,
    kv,
    gate,
    gate_out,
    mixed,
    mixed_out,
    joined,
    base,
    crossed,
    ct,
    ct_sib,
    ft,
    ft_sib,
    hid_t,
    slope,
    scores,
    place_out,
    rows_in,
    d_own,
    d_sib,
    gs,
    gs_sib,
    dc,
    dc_sib,
    bd,
    grads,
    x1,
    x2,
    x3,
    y3,
    w1,
    v1,
    w2,
    last,
    fin,
    s1s,
    s1r,
    s2s,
    s2r,
    s3s,
    s3r,
    scs,
    scr,
    srs,
    srr,
    lds,
    hds,
    p1s,
    p1r,
    p2s,
    p2r,
    ups,
    upr,
    sbs,
    sbr,
    ohs,
    ohr,
):
    t = lax.axis_index("teacher")
    s = lax.axis_index("student")
    z, x = t // 4, t % 4
    y, c = s // 2, s % 2
    pos = (z, x, y)
    sibling = (t, y * 2 + 1 - c)
    sends = []

    def at_chip(axis, value, core):
        p = list(pos)
        p[axis] = value
        return (p[0] * 4 + p[1], p[2] * 2 + core)

    def push(src, dst, send_sem, recv_sem, device, shared=False):
        copy = pltpu.make_async_remote_copy(
            src_ref=src,
            dst_ref=dst,
            send_sem=send_sem,
            recv_sem=recv_sem,
            device_id=device,
            device_id_type=MESH,
        )
        copy.start()
        if not shared:
            sends.append(copy)
        return copy

    def whole_of(ref, send_sem, recv_sem):
        return pltpu.make_async_remote_copy(
            src_ref=ref,
            dst_ref=ref,
            send_sem=send_sem,
            recv_sem=recv_sem,
            device_id=sibling,
            device_id_type=MESH,
        )

    peers = [((t + k) % 16, s) for k in range(1, 16)] + [sibling]
    peers += [at_chip(2, (y + k) % 4, c) for k in range(1, 4)]
    peers += [at_chip(axis, (pos[axis] + k) % 4, 1 - c) for axis in range(3) for k in range(1, 4)]
    barrier = pltpu.get_barrier_semaphore()
    for peer in peers:
        pl.semaphore_signal(barrier, inc=1, device_id=peer, device_id_type=MESH)

    odd = y % 2
    first = (1 - c) * x + c * z
    second = (1 - c) * z + c * x

    def shard(i, j):
        i, j = (first + i) % 4, (second + j) % 4
        return (1 - c) * (j * 4 + i) + c * (i * 4 + j)

    def head_of(k, core):
        return (4 + 2 * odd + core, core, 2 + core, 6 - 2 * odd + core)[k]

    own_cols = []
    for k in range(3):
        for part, (ref, start) in enumerate(
            ((w_keys_hbm, 0), (w_keys_hbm, 1024), (w_query_hbm, 0), (w_query_hbm, 1024))
        ):
            cols = pl.ds(pl.multiple_of(start + head_of(k, c) * 128, 128), 128)
            own_cols.append(
                pltpu.make_async_copy(
                    ref.at[:, cols],
                    heads.at[k, t, :, 128 * part : 128 * part + 128],
                    hds.at[k, part],
                )
            )
            own_cols[-1].start()
    pairs = (
        (feat_hbm, feat_ref),
        (w_cross_hbm, w_cross_ref),
        (b_cross_hbm, b_cross_ref),
        (b_score_hbm, b_score_ref),
        (ids_hbm, ids_ref),
        (table_hbm, table_ref),
        (segs_hbm, segs_ref),
        (cand_hbm, cand_ref),
        (owners_hbm, owners_ref),
        (w_out_hbm, w_out_ref),
        (w_head_hbm, w_head_ref),
        (b_deep_hbm, b_deep_ref),
        (w_deep_hbm, w_deep_ref),
        (w_score_hbm, w_score_ref),
        (emb_hbm, emb),
    )
    loads = [pltpu.make_async_copy(src, dst, lds.at[n]) for n, (src, dst) in enumerate(pairs)]
    for load in loads:
        load.start()

    def along(k, i, j, rows, send_sem, recv_sem, device):
        ref = heads.at[k, shard(i, j), rows]
        return push(ref, ref, send_sem, recv_sem, device, True)

    full = slice(0, 64)
    y_next = (t, (y + 1 + 2 * c) % 4 * 2 + c)
    p1, p2 = {}, {}

    def to_y(k, i, j):
        if k == 0:
            up = heads.at[0, shard(i, j)]
            push(up, heads.at[3, shard(i, j)], ups.at[0], upr.at[0], y_next, True)

    def spread(k, i):
        for side, step in enumerate((1, 3, 2) if k == 0 else (1, 3)):
            device = (shard(0, step), s)
            p2[k, i, side] = along(k, i, 0, full, p2s.at[0], p2r.at[k, i, side], device)
        to_y(k, i, 0)

    def hop(k):
        for side, step in enumerate((1, 3, 2)):
            device = (shard(step, 0), s)
            p1[k, side] = along(k, 0, 0, full, p1s.at[0], p1r.at[k, side], device)

    def hop_end(k):
        for side in range(3):
            p1[k, side].wait_recv()

    def arrive(i):
        for side, j in enumerate((3, 1, 2)):
            p2[0, i, side].wait_recv()
            to_y(0, i, j)

    def event3(k):
        for i in (0, 1, 3, 2):
            side = 0 if i < 2 else 1
            step = (1, 3)[side]
            p2[k, i, side].wait_recv()
            device = (shard(0, step), s)
            p2[k, i, 2] = along(k, i, 4 - step, full, p2s.at[0], p2r.at[k, i, 2], device)
            p2[k, i, 1 - side].wait_recv()

    def event4(k):
        for i in range(4):
            p2[k, i, 2].wait_recv()

    for copy in own_cols:
        copy.wait()
    pl.semaphore_wait(barrier, len(peers))
    hop(0)
    spread(0, 0)
    hop(1)
    hop(2)

    for load in loads[:12]:
        load.wait()
    feats = feat_ref[...]
    feats32 = feats.astype(F32)
    cross = nn(feats, w_cross_ref[...]) + b_cross_ref[...].astype(F32).reshape(1, 512)
    crossed[...] = (feats32 * cross + feats32).astype(BF)
    ct[...] = flip(crossed[...])
    ft[...] = flip(feats)
    ct_copy = push(ct, ct_sib, scs.at[0], scr.at[0], sibling)
    ft_copy = push(ft, ft_sib, scs.at[1], scr.at[1], sibling)
    scores[...] = jnp.broadcast_to(b_score_ref[...].astype(F32), scores.shape)
    table_pad[...] = jnp.zeros_like(table_pad)
    table_pad[0:16] = table_ref[...]
    loads[14].wait()

    def embed(i):
        rows = slice(i * 256, i * 256 + 256)
        kinds = lax.broadcasted_iota(jnp.int32, (128, 256), 0)
        onehot = flip(kinds == ids_ref[:, rows])
        hist[0, rows, :] = (emb[rows, :].astype(F32) + nn(onehot, table_pad[...])).astype(BF)

    for i in range(4):
        embed(i)
    hist_copy = push(hist.at[0], hist.at[1], sbs.at[0], sbr.at[0], sibling)
    hop_end(0)
    for i in (3, 1, 2):
        spread(0, i)
    b_deep32 = b_deep_ref[...].astype(F32).reshape(1, 4096)

    def forward(j):
        cols = slice(j * 512, j * 512 + 512)
        pre = nn(crossed[...], w_deep_ref[:, cols]) + b_deep32[:, cols]
        sigma = 0.5 + 0.5 * jnp.tanh(0.5 * pre)
        hidden = (pre * sigma).astype(BF)
        slope[j] = sigma * (1.0 + pre * (1.0 - sigma))
        hid_t[cols, :] = hidden.T
        scores[...] += nn(hidden, w_score_ref[cols, :])

    loads[12].wait()
    loads[13].wait()
    for j in range(2):
        forward(j)
    for k in (1, 2):
        hop_end(k)
        for i in range(4):
            spread(k, i)

    where_col = jnp.broadcast_to(cand_ref[...], (128, 256)).astype(F32).T[:, 0:1]
    places = lax.broadcasted_iota(jnp.int32, (256, 1024), 1).astype(F32)
    segs = segs_ref[...].astype(F32)
    chosen = (places == where_col).astype(F32)
    picked[0:256] = nn(chosen.astype(BF), hist[0]).astype(BF)
    seg_col = jnp.sum(chosen * segs, axis=1, keepdims=True)
    mask[0] = jnp.where((segs == seg_col) & (places <= where_col), 1.0, 0.0)
    base[...] = nn(picked[0:256], w_head_ref[...])
    picked_copy = push(picked.at[0:256], picked.at[256:512], sbs.at[1], sbr.at[1], sibling)
    mask_copy = push(mask.at[0], mask.at[1], sbs.at[2], sbr.at[2], sibling)
    arrive(0)
    for j in range(2, 5):
        forward(j)
    arrive(3)
    arrive(1)
    for j in range(5, 8):
        forward(j)
    arrive(2)

    att_done = []

    def attend(k, between=None):
        head = head_of(k, c)
        columns = heads[k].reshape(1024, 512)
        qrows = silu(nn(picked[...], columns[:, 256:512])).astype(BF)
        gate[head] = qrows[:256, :128]
        gate_out[k] = qrows[256:, :128]
        for side in (1, 0):
            kv[side] = silu(nn(hist[side], columns[:, :256])).astype(BF)
        if between is not None:
            between()
        for side in (1, 0):
            half = nt(qrows[256 * side : 256 * side + 256, 128:], kv[side, :, 128:])
            half = half * (0.5 * 128 ** (-0.5))
            weights = ((half + half * jnp.tanh(half)) * mask[side]).astype(BF)
            result = nn(weights, kv[side, :, :128])
            if side == 0:
                mixed[head] = result
            else:
                mixed_out[k] = result
                for n, (src, dst) in enumerate(((mixed_out, mixed), (gate_out, gate))):
                    n += 3 + 2 * k
                    att_done.append(push(src.at[k], dst.at[head], sbs.at[n], sbr.at[n], sibling))

    dest = owners_ref[...]
    kinds = lax.broadcasted_iota(jnp.int32, (16, 256), 0)
    hits = (kinds == dest).astype(F32)
    upper = (
        lax.broadcasted_iota(jnp.int32, (256, 256), 0)
        < lax.broadcasted_iota(jnp.int32, (256, 256), 1)
    ).astype(BF)
    before = nn(hits.astype(BF), upper)
    rank = jnp.sum(before * hits, axis=0, keepdims=True).astype(jnp.int32)
    slot = dest * CAP + rank
    place = (lax.broadcasted_iota(jnp.int32, (512, 256), 0) == slot).astype(BF)
    own_out = nn(w_out_ref[...], w_head_ref[...]).astype(BF)
    own_half[...] = own_out
    mine_rows = pl.ds(pl.multiple_of(32 * c, 32), 32)
    placed = nn(place, scores[...].astype(BF)).astype(BF).reshape(16, CAP, 128)
    place_out[:, :CAP] = placed
    place_out[:, CAP:] = jnp.broadcast_to(own_half[mine_rows, :][None], (16, 32, 128))
    rows_in[t] = place_out[t]
    event3(1)
    for copy in (hist_copy, picked_copy, mask_copy):
        copy.wait_recv()
    attend(0, functools.partial(event3, 2))
    for k in range(1, 16):
        to = (t + k) % 16
        push(place_out.at[to], rows_in.at[t], srs.at[0], srr.at[0], (to, s), True)
    event4(1)
    attend(1, functools.partial(event4, 2))
    whole_of(rows_in.at[0:15], srs.at[0], srr.at[0]).wait_recv()
    out_head[:, mine_rows] = rows_in[:, CAP:]
    every = out_head.at[:, mine_rows]
    oh_sib = push(every, every, ohs.at[0], ohr.at[0], sibling)
    attend(2)
    whole_of(heads.at[3], ups.at[0], upr.at[0]).wait_recv()
    attend(3)
    for copy in att_done:
        copy.wait_recv()

    centre = jnp.sum(jnp.sum(mixed[...], axis=0), axis=1, keepdims=True) * (1.0 / 1024.0)
    spread_sum = jnp.sum(jnp.square(mixed[...] - centre[None]), axis=0)
    scale_rows = lax.rsqrt(jnp.sum(spread_sum, axis=1, keepdims=True) * (1.0 / 1024.0) + EPS)
    for head in range(8):
        normed = (mixed[head] - centre) * scale_rows
        joined[:, 128 * head : 128 * head + 128] = (normed * gate[head].astype(F32)).astype(BF)
    oh_sib.wait_recv()
    logits = base[...] + nn(joined[...], out_head[...].reshape(1024, 128))

    delta = scores[...] - logits.astype(BF).astype(F32)
    delta16 = delta.astype(BF)
    bscore = jnp.sum(delta, axis=0, keepdims=True)

    def back_chunk(j):
        rows = pl.ds(pl.multiple_of(j * 512, 512), 512)
        dpre = nt(delta16, w_score_ref[rows, :]) * slope[j]
        d_own[j] = dpre.astype(BF)
        bd[j] = jnp.broadcast_to(jnp.sum(dpre, axis=0, keepdims=True), (8, 512))

    d_copies = {}
    for q in (0, 1, 3, 2):
        j = (1 - c) * 4 + q
        back_chunk(j)
        d_copies[q] = push(d_own.at[j], d_sib.at[q], scs.at[2 + q], scr.at[2 + q], sibling)
    for q in (0, 1, 3, 2):
        back_chunk(c * 4 + q)
    for i in range(8):
        g = nn(hid_t[512 * i : 512 * i + 512, :], delta16).astype(BF).reshape(8, 2, 2, 16, 128)
        for core in range(2):
            gs[core, 8 * i : 8 * i + 8, :, 0:128] = g[:, core, 0]
            gs[core, 8 * i : 8 * i + 8, :, 128:256] = g[:, core, 1]
    gs_copy = push(gs.at[1 - c], gs_sib, scs.at[6], scr.at[6], sibling)
    every_dpre = jnp.concatenate([d_own[j] for j in range(8)], axis=1)
    dcr = nt(every_dpre, w_deep_ref[...]) * feats32
    bcross = jnp.sum(dcr, axis=0, keepdims=True)
    dc[0] = dcr[:, :256].astype(BF)
    dc[1] = dcr[:, 256:].astype(BF)
    dc_copy = push(dc.at[1 - c], dc_sib, scs.at[7], scr.at[7], sibling)

    def axes_of(u):
        axis = ROUTES[u // 2][0]
        rest = [a for a in range(3) if a != axis]
        return axis, rest

    def piece(u, where, half):
        axis, rest = axes_of(u)
        index = [slice(None)] * 3
        index[axis] = where
        index[rest[0]] = pl.ds(2 * half, 2)
        return (u, *index)

    def stage1_first(u):
        axis, _ = axes_of(u)
        m = pos[axis]
        right, left, opp = (m + 1) % 4, (m + 3) % 4, (m + 2) % 4
        to_right, to_left = at_chip(axis, right, c), at_chip(axis, left, c)
        return (
            push(grads.at[piece(u, opp, 0)], x1.at[u, 0], s1s.at[0], s1r.at[u, 0], to_right, True),
            push(grads.at[piece(u, opp, 1)], x1.at[u, 1], s1s.at[0], s1r.at[u, 1], to_left, True),
        )

    def stage1_second(u):
        axis, _ = axes_of(u)
        m = pos[axis]
        right, left = (m + 1) % 4, (m + 3) % 4
        to_right, to_left = at_chip(axis, right, c), at_chip(axis, left, c)
        return (
            push(grads.at[piece(u, right, 1)], x2.at[u, 0], s1s.at[1], s1r.at[u, 2], to_right, True),
            push(grads.at[piece(u, left, 0)], x2.at[u, 1], s1s.at[1], s1r.at[u, 3], to_left, True),
        )

    def stage1_pass(u, started):
        axis, _ = axes_of(u)
        m = pos[axis]
        right, left = (m + 1) % 4, (m + 3) % 4
        out = []
        for side, (where, device) in enumerate(
            ((right, at_chip(axis, right, c)), (left, at_chip(axis, left, c)))
        ):
            started[side].wait_recv()
            mine = grads[piece(u, where, side)].astype(F32)
            y3[u, side] = (mine + x1[u, side].astype(F32)).astype(BF)
            out.append(
                push(y3.at[u, side], x3.at[u, side], s1s.at[2], s1r.at[u, 4 + side], device, True)
            )
        return out

    def stage1_end(u, started, passed):
        axis, _ = axes_of(u)
        m = pos[axis]
        for copy in (started[2], started[3], passed[0], passed[1]):
            copy.wait_recv()
        for half in range(2):
            total = grads[piece(u, m, half)].astype(F32)
            total += x2[u, 1 - half].astype(F32) + x3[u, half].astype(F32)
            w1[u // 2, u % 2, 2 * half : 2 * half + 2] = total.astype(BF)

    started, passed = {}, {}

    ct_copy.wait_recv()
    for q in (0, 1, 3, 2):
        d_copies[q].wait_recv()
        g = nn(ct[...], d_own[c * 4 + q]) + nn(ct_sib[...], d_sib[q])
        g = g.reshape(64, 8, 512)
        g = jnp.concatenate([g[:, :, :256], g[:, :, 256:]], axis=1)
        grads[1 + q] = g.astype(BF).reshape(4, 4, 4, 16, 256)
        started[1 + q] = stage1_first(1 + q)

    gs_copy.wait_recv()
    summed = gs[c].astype(F32) + gs_sib[...].astype(F32)
    grads[0] = summed.astype(BF).reshape(4, 4, 4, 16, 256)
    started[0] = stage1_first(0)

    for u in (1, 2, 4):
        started[u] += stage1_second(u)

    sub = lax.broadcasted_iota(jnp.int32, (16, 128), 0)
    for pair in range(32):
        deep_row = bd[pair // 4, 0:1, (pair % 4) * 128 : (pair % 4) * 128 + 128]
        cross_row = bcross[:, (pair // 8) * 128 : (pair // 8) * 128 + 128]
        tile = jnp.where(sub == 0, deep_row, jnp.where(sub == 1, cross_row, bscore))
        tile = tile.astype(BF)
        for chip in (2 * pair, 2 * pair + 1):
            grads[5, chip // 16, chip // 4 % 4, chip % 4, :, 128:256] = tile
    ft_copy.wait_recv()
    dc_copy.wait_recv()
    g = nn(ft[...], dc[c]) + nn(ft_sib[...], dc_sib[...])
    g = g.reshape(64, 8, 256)
    g = jnp.concatenate([g[:, :, :128], g[:, :, 128:]], axis=1)
    grads[5, :, :, :, :, 0:128] = g.astype(BF).reshape(4, 4, 4, 16, 128)
    started[5] = stage1_first(5)
    for u in (3, 0, 5):
        started[u] += stage1_second(u)
    for u in (1, 2, 4, 3, 0, 5):
        passed[u] = stage1_pass(u, started[u])

    def piece2(u, where):
        axis, second, _ = ROUTES[u // 2]
        rest = [a for a in range(3) if a != axis]
        index = [slice(None)] * 2
        index[rest.index(second)] = where
        return (u // 2, u % 2, *index)

    def stage2_start(u):
        axis = ROUTES[u // 2][1]
        m = pos[axis]
        return [
            push(
                w1.at[piece2(u, (m + step) % 4)],
                v1.at[u, k],
                s2s.at[0],
                s2r.at[u, k],
                at_chip(axis, (m + step) % 4, c),
                True,
            )
            for k, step in enumerate((1, 3, 2))
        ]

    def stage2_end(u, begun):
        total = w1[piece2(u, pos[ROUTES[u // 2][1]])].astype(F32)
        for k, copy in enumerate(begun):
            copy.wait_recv()
            total += v1[u, k].astype(F32)
        w2[u // 2, u % 2] = total.astype(BF)

    def stage3_start(r):
        axis = ROUTES[r][2]
        m = pos[axis]
        last[r, m, c] = w2[r, :, m]
        for k in range(4):
            where = (m + k) % 4
            for other in range(2):
                if k == 0 and other == 0:
                    continue
                core = c if other == 0 else 1 - c
                push(
                    w2.at[r, :, where],
                    last.at[r, m, c],
                    s3s.at[k],
                    s3r.at[k],
                    at_chip(axis, where, core),
                    True,
                )

    def stage3_end(r):
        scale = 1.0 / 32768.0
        for core in range(2):
            total = last[r, 0, core].astype(F32)
            for k in range(1, 4):
                total += last[r, k, core].astype(F32)
            fin[core, 2 * r : 2 * r + 2] = total * scale

    begun = {}
    for u in (1, 2, 4, 3, 0, 5):
        stage1_end(u, started[u], passed[u])
        begun[u] = stage2_start(u)
    for r in range(3):
        for u in (2 * r, 2 * r + 1):
            stage2_end(u, begun[u])
        stage3_start(r)
    o_rows[...] = rows_in[:, :CAP]
    stage3_all = [whole_of(last.at[:, 0, 0], s3s.at[0], s3r.at[0])]
    stage3_all += [whole_of(last.at[:, 0], s3s.at[k], s3r.at[k]) for k in range(1, 4)]
    for copy in stage3_all:
        copy.wait_recv()
    for r in range(3):
        stage3_end(r)

    def own_rows(core, unit, half, cols):
        lower = fin[core, unit, 8 * half : 8 * half + 4, cols]
        higher = fin[core, unit, 8 * half + 4 : 8 * half + 8, cols]
        return jnp.where(c == 0, lower, higher)

    for core in range(2):
        for half in range(2):
            for q in range(4):
                at = core * 2048 + q * 512 + half * 256
                o_deep[:, at : at + 256] = own_rows(core, 1 + q, half, slice(0, 256))
            at = core * 256 + half * 128
            o_cross[:, at : at + 128] = own_rows(core, 5, half, slice(0, 128))
    for half in range(2):
        cols = slice(128 * half, 128 * half + 128)
        o_score[16 * half : 16 * half + 16] = jnp.where(c == 0, fin[0, 0, :, cols], fin[1, 0, :, cols])
    chip = t * 4 + y
    bias = fin[0, 5, 0:8, 128:256] + fin[1, 5, 0:8, 128:256]
    for row, first in enumerate((chip % 2 * 64 + c * 32, chip % 16 * 8 + c * 4, chip * 2 + c)):
        o_bias[row : row + 1] = pltpu.roll(bias, (128 - first) % 128, 1)[row : row + 1]
    sends += stage3_all
    sends.append(whole_of(heads.at[0, 0:9], p1s.at[0], upr.at[0]))
    sends.append(whole_of(heads.at[0:3, 0:12], p2s.at[0], upr.at[0]))
    sends.append(whole_of(heads.at[0], ups.at[0], upr.at[0]))
    sends.append(whole_of(place_out.at[0:15], srs.at[0], srr.at[0]))
    sends.append(whole_of(x1, s1s.at[0], upr.at[0]))
    sends.append(whole_of(x2, s1s.at[1], upr.at[0]))
    sends.append(whole_of(x3, s1s.at[2], upr.at[0]))
    sends.append(whole_of(v1, s2s.at[0], upr.at[0]))
    for copy in sends:
        copy.wait_send()


def results(cross, deep, score, bias, rows, o_cross, o_bcross, o_deep, o_bdeep, o_score, o_bscore, o_rows):
    o_cross[...] = cross[...]
    o_deep[...] = deep[...]
    o_score[...] = score[...]
    o_rows[...] = rows[...]
    o_bdeep[...] = bias[0, 0:32]
    o_bcross[...] = bias[1, 0:4]
    o_bscore[...] = bias[2, 0:1]


def local(
    embeddings,
    action_ids,
    segment_ids,
    cand_pos,
    owners,
    features,
    action_table,
    w_query,
    w_keys,
    w_out,
    w_head,
    w_cross,
    b_cross,
    w_deep,
    b_deep,
    w_score,
    b_score,
):
    dma = pltpu.SemaphoreType.DMA
    vmem = pltpu.VMEM
    whole = pl.BlockSpec(memory_space=pltpu.VMEM)
    stay = pl.BlockSpec(memory_space=pl.ANY)
    g_cross, g_deep, g_score, bias, rows = pl.pallas_call(
        kernel,
        out_shape=(
            jax.ShapeDtypeStruct((4, 512), F32),
            jax.ShapeDtypeStruct((4, 4096), F32),
            jax.ShapeDtypeStruct((32, 128), F32),
            jax.ShapeDtypeStruct((8, 128), F32),
            jax.ShapeDtypeStruct((16, CAP, 128), BF),
        ),
        in_specs=[stay] * 17,
        out_specs=(whole,) * 5,
        scratch_shapes=[
            vmem((1, 1024), jnp.int32),
            vmem((1, 1024), jnp.int32),
            vmem((1, 256), jnp.int32),
            vmem((1, 256), jnp.int32),
            vmem((256, 512), BF),
            vmem((16, 1024), BF),
            vmem((64, 1024), BF),
            vmem((1024, 128), BF),
            vmem((512, 512), BF),
            vmem((512,), BF),
            vmem((4096,), BF),
            vmem((1, 128), BF),
            vmem((1024, 1024), BF),
            vmem((512, 4096), BF),
            vmem((4096, 128), BF),
            vmem((4, 16, 64, 512), BF),
            vmem((16, 64, 128), BF),
            vmem((64, 128), BF),
            vmem((128, 1024), BF),
            vmem((2, 1024, 1024), BF),
            vmem((512, 1024), BF),
            vmem((2, 256, 1024), F32),
            vmem((2, 1024, 256), BF),
            vmem((8, 256, 128), BF),
            vmem((4, 256, 128), BF),
            vmem((8, 256, 128), F32),
            vmem((4, 256, 128), F32),
            vmem((256, 1024), BF),
            vmem((256, 128), F32),
            vmem((256, 512), BF),
            vmem((512, 256), BF),
            vmem((512, 256), BF),
            vmem((512, 256), BF),
            vmem((512, 256), BF),
            vmem((4096, 256), BF),
            vmem((8, 256, 512), F32),
            vmem((256, 128), F32),
            vmem((16, CAP + 32, 128), BF),
            vmem((16, CAP + 32, 128), BF),
            vmem((8, 256, 512), BF),
            vmem((4, 256, 512), BF),
            vmem((2, 64, 16, 256), BF),
            vmem((64, 16, 256), BF),
            vmem((2, 256, 256), BF),
            vmem((256, 256), BF),
            vmem((8, 8, 512), F32),
            vmem((6, 4, 4, 4, 16, 256), BF),
            vmem((6, 2, 2, 4, 16, 256), BF),
            vmem((6, 2, 2, 4, 16, 256), BF),
            vmem((6, 2, 2, 4, 16, 256), BF),
            vmem((6, 2, 2, 4, 16, 256), BF),
            vmem((3, 2, 4, 4, 16, 256), BF),
            vmem((6, 3, 4, 16, 256), BF),
            vmem((3, 2, 4, 16, 256), BF),
            vmem((3, 4, 2, 2, 16, 256), BF),
            vmem((2, 6, 16, 256), F32),
            dma((3,)),
            dma((6, 6)),
            dma((1,)),
            dma((6, 3)),
            dma((4,)),
            dma((4,)),
            dma((8,)),
            dma((8,)),
            dma((1,)),
            dma((1,)),
            dma((15,)),
            dma((3, 4)),
            dma((1,)),
            dma((3, 3)),
            dma((1,)),
            dma((3, 4, 3)),
            dma((1,)),
            dma((1,)),
            dma((11,)),
            dma((11,)),
            dma((1,)),
            dma((1,)),
        ],
        compiler_params=pltpu.CompilerParams(
            collective_id=0, has_side_effects=True, vmem_limit_bytes=56 * 1024 * 1024
        ),
    )(
        embeddings,
        action_ids.reshape(1, -1),
        segment_ids,
        cand_pos.reshape(1, -1),
        owners.reshape(1, -1),
        features,
        action_table,
        w_query,
        w_keys,
        w_out,
        w_head,
        w_cross,
        b_cross,
        w_deep,
        b_deep,
        w_score,
        b_score.reshape(1, -1),
    )
    return pl.pallas_call(
        results,
        out_shape=(
            jax.ShapeDtypeStruct((4, 512), F32),
            jax.ShapeDtypeStruct((4,), F32),
            jax.ShapeDtypeStruct((4, 4096), F32),
            jax.ShapeDtypeStruct((32,), F32),
            jax.ShapeDtypeStruct((32, 128), F32),
            jax.ShapeDtypeStruct((1,), F32),
            jax.ShapeDtypeStruct((512, 128), BF),
        ),
        in_specs=[whole] * 5,
        out_specs=(whole,) * 7,
    )(g_cross, g_deep, g_score, bias, rows.reshape(512, 128))


def solution(mesh):
    both = ("teacher", "student")
    return jax.shard_map(
        local,
        mesh=mesh,
        in_specs=(
            P(both, None),
            P(both),
            P(both, None),
            P(both),
            P(both, None),
            P(both, None),
            P(),
            P("teacher", None),
            P("teacher", None),
            P("teacher", None),
            P(),
            P(),
            P(),
            P(),
            P(),
            P(),
            P(),
        ),
        out_specs=(
            P(both, None),
            P(both),
            P(both, None),
            P(both),
            P(both, None),
            P(both),
            P(both, None),
        ),
        check_vma=False,
    )
```

```python
import functools

import jax
import jax.numpy as jnp
from jax import lax
from jax.experimental import pallas as pl
from jax.experimental.pallas import tpu as pltpu
from jax.sharding import PartitionSpec as P

CAP = 32
EPS = 1e-05
BF = jnp.bfloat16
F32 = jnp.float32
MESH = pl.DeviceIdType.MESH

ROUTES = ((0, 1, 2), (1, 2, 0), (2, 0, 1))


def nn(a, b):
    return lax.dot_general(a, b, (((1,), (0,)), ((), ())), preferred_element_type=F32)


def nt(a, b):
    return lax.dot_general(a, b, (((1,), (1,)), ((), ())), preferred_element_type=F32)


def silu(v):
    half = 0.5 * v
    return half + half * jnp.tanh(half)


def flip(v):
    return v.astype(F32).T.astype(BF)


def kernel(
    emb_hbm,
    ids_hbm,
    segs_hbm,
    cand_hbm,
    owners_hbm,
    feat_hbm,
    table_hbm,
    w_query_hbm,
    w_keys_hbm,
    w_out_hbm,
    w_head_hbm,
    w_cross_hbm,
    b_cross_hbm,
    w_deep_hbm,
    b_deep_hbm,
    w_score_hbm,
    b_score_hbm,
    o_cross,
    o_deep,
    o_score,
    o_bias,
    o_rows,
    ids_ref,
    segs_ref,
    cand_ref,
    owners_ref,
    feat_ref,
    table_ref,
    w_out_ref,
    w_head_ref,
    w_cross_ref,
    b_cross_ref,
    b_deep_ref,
    b_score_ref,
    emb,
    w_deep_ref,
    w_score_ref,
    heads,
    out_head,
    own_half,
    table_pad,
    hist,
    picked,
    mask,
    kv,
    gate,
    gate_out,
    mixed,
    mixed_out,
    joined,
    base,
    crossed,
    ct,
    ct_sib,
    ft,
    ft_sib,
    hid_t,
    slope,
    scores,
    place_out,
    rows_in,
    d_own,
    d_sib,
    gs,
    gs_sib,
    dc,
    dc_sib,
    bd,
    grads,
    x1,
    x2,
    x3,
    y3,
    w1,
    v1,
    w2,
    last,
    fin,
    s1s,
    s1r,
    s2s,
    s2r,
    s3s,
    s3r,
    scs,
    scr,
    srs,
    srr,
    lds,
    hds,
    p1s,
    p1r,
    p2s,
    p2r,
    ups,
    upr,
    sbs,
    sbr,
    ohs,
    ohr,
):
    t = lax.axis_index("teacher")
    s = lax.axis_index("student")
    z, x = t // 4, t % 4
    y, c = s // 2, s % 2
    pos = (z, x, y)
    sibling = (t, y * 2 + 1 - c)
    sends = []

    def at_chip(axis, value, core):
        p = list(pos)
        p[axis] = value
        return (p[0] * 4 + p[1], p[2] * 2 + core)

    def push(src, dst, send_sem, recv_sem, device, shared=False):
        copy = pltpu.make_async_remote_copy(
            src_ref=src,
            dst_ref=dst,
            send_sem=send_sem,
            recv_sem=recv_sem,
            device_id=device,
            device_id_type=MESH,
        )
        copy.start()
        if not shared:
            sends.append(copy)
        return copy

    def whole_of(ref, send_sem, recv_sem):
        return pltpu.make_async_remote_copy(
            src_ref=ref,
            dst_ref=ref,
            send_sem=send_sem,
            recv_sem=recv_sem,
            device_id=sibling,
            device_id_type=MESH,
        )

    peers = [at_chip(axis, (pos[axis] + k) % 4, c) for axis in (0, 1) for k in (1, 2, 3)]
    peers += [at_chip(2, (y + k) % 4, c) for k in (1, 3)] + [sibling]
    barrier = pltpu.get_barrier_semaphore()
    for peer in peers:
        pl.semaphore_signal(barrier, inc=1, device_id=peer, device_id_type=MESH)

    odd = y % 2
    first = (1 - c) * x + c * z
    second = (1 - c) * z + c * x

    def shard(i, j):
        i, j = (first + i) % 4, (second + j) % 4
        return (1 - c) * (j * 4 + i) + c * (i * 4 + j)

    def head_of(k, core):
        return (4 + 2 * odd + core, core, 2 + core, 6 - 2 * odd + core)[k]

    own_cols = []
    for k in range(3):
        for part, (ref, start) in enumerate(
            ((w_keys_hbm, 0), (w_keys_hbm, 1024), (w_query_hbm, 0), (w_query_hbm, 1024))
        ):
            cols = pl.ds(pl.multiple_of(start + head_of(k, c) * 128, 128), 128)
            own_cols.append(
                pltpu.make_async_copy(
                    ref.at[:, cols],
                    heads.at[k, t, :, 128 * part : 128 * part + 128],
                    hds.at[k, part],
                )
            )
            own_cols[-1].start()
    pairs = (
        (feat_hbm, feat_ref),
        (w_cross_hbm, w_cross_ref),
        (b_cross_hbm, b_cross_ref),
        (b_score_hbm, b_score_ref),
        (ids_hbm, ids_ref),
        (table_hbm, table_ref),
        (segs_hbm, segs_ref),
        (cand_hbm, cand_ref),
        (owners_hbm, owners_ref),
        (w_out_hbm, w_out_ref),
        (w_head_hbm, w_head_ref),
        (b_deep_hbm, b_deep_ref),
        (w_deep_hbm, w_deep_ref),
        (w_score_hbm, w_score_ref),
        (emb_hbm, emb),
    )
    loads = [pltpu.make_async_copy(src, dst, lds.at[n]) for n, (src, dst) in enumerate(pairs)]
    for load in loads:
        load.start()

    def along(k, i, j, rows, send_sem, recv_sem, device):
        ref = heads.at[k, shard(i, j), rows]
        return push(ref, ref, send_sem, recv_sem, device, True)

    full = slice(0, 64)
    y_next = (t, (y + 1 + 2 * c) % 4 * 2 + c)
    p1, p2 = {}, {}

    def to_y(k, i, j):
        if k == 0:
            up = heads.at[0, shard(i, j)]
            push(up, heads.at[3, shard(i, j)], ups.at[0], upr.at[0], y_next, True)

    def spread(k, i):
        for side, step in enumerate((1, 3, 2) if k == 0 else (1, 3)):
            device = (shard(0, step), s)
            p2[k, i, side] = along(k, i, 0, full, p2s.at[0], p2r.at[k, i, side], device)
        to_y(k, i, 0)

    def hop(k):
        for side, step in enumerate((1, 3, 2)):
            device = (shard(step, 0), s)
            p1[k, side] = along(k, 0, 0, full, p1s.at[0], p1r.at[k, side], device)

    def hop_end(k):
        for side in range(3):
            p1[k, side].wait_recv()

    def arrive(i):
        for side, j in enumerate((3, 1, 2)):
            p2[0, i, side].wait_recv()
            to_y(0, i, j)

    def event3(k):
        for i in (0, 1, 3, 2):
            side = 0 if i < 2 else 1
            step = (1, 3)[side]
            p2[k, i, side].wait_recv()
            device = (shard(0, step), s)
            p2[k, i, 2] = along(k, i, 4 - step, full, p2s.at[0], p2r.at[k, i, 2], device)
            p2[k, i, 1 - side].wait_recv()

    def event4(k):
        for i in range(4):
            p2[k, i, 2].wait_recv()

    for copy in own_cols:
        copy.wait()
    pl.semaphore_wait(barrier, len(peers))
    hop(0)
    spread(0, 0)
    hop(1)
    hop(2)

    for load in loads[:12]:
        load.wait()
    feats = feat_ref[...]
    feats32 = feats.astype(F32)
    cross = nn(feats, w_cross_ref[...]) + b_cross_ref[...].astype(F32).reshape(1, 512)
    crossed[...] = (feats32 * cross + feats32).astype(BF)
    ct[...] = flip(crossed[...])
    ft[...] = flip(feats)
    ct_copy = push(ct, ct_sib, scs.at[0], scr.at[0], sibling)
    ft_copy = push(ft, ft_sib, scs.at[1], scr.at[1], sibling)
    scores[...] = jnp.broadcast_to(b_score_ref[...].astype(F32), scores.shape)
    table_pad[...] = jnp.zeros_like(table_pad)
    table_pad[0:16] = table_ref[...]
    loads[14].wait()

    def embed(i):
        rows = slice(i * 256, i * 256 + 256)
        kinds = lax.broadcasted_iota(jnp.int32, (128, 256), 0)
        onehot = flip(kinds == ids_ref[:, rows])
        hist[0, rows, :] = (emb[rows, :].astype(F32) + nn(onehot, table_pad[...])).astype(BF)

    for i in range(4):
        embed(i)
    hist_copy = push(hist.at[0], hist.at[1], sbs.at[0], sbr.at[0], sibling)
    hop_end(0)
    for i in (3, 1, 2):
        spread(0, i)
    b_deep32 = b_deep_ref[...].astype(F32).reshape(1, 4096)

    def forward(j):
        cols = slice(j * 512, j * 512 + 512)
        pre = nn(crossed[...], w_deep_ref[:, cols]) + b_deep32[:, cols]
        sigma = 0.5 + 0.5 * jnp.tanh(0.5 * pre)
        hidden = (pre * sigma).astype(BF)
        slope[j] = sigma * (1.0 + pre * (1.0 - sigma))
        hid_t[cols, :] = hidden.T
        scores[...] += nn(hidden, w_score_ref[cols, :])

    loads[12].wait()
    loads[13].wait()
    for j in range(2):
        forward(j)
    for k in (1, 2):
        hop_end(k)
        for i in range(4):
            spread(k, i)

    where_col = jnp.broadcast_to(cand_ref[...], (128, 256)).astype(F32).T[:, 0:1]
    places = lax.broadcasted_iota(jnp.int32, (256, 1024), 1).astype(F32)
    segs = segs_ref[...].astype(F32)
    chosen = (places == where_col).astype(F32)
    picked[0:256] = nn(chosen.astype(BF), hist[0]).astype(BF)
    seg_col = jnp.sum(chosen * segs, axis=1, keepdims=True)
    mask[0] = jnp.where((segs == seg_col) & (places <= where_col), 1.0, 0.0)
    base[...] = nn(picked[0:256], w_head_ref[...])
    picked_copy = push(picked.at[0:256], picked.at[256:512], sbs.at[1], sbr.at[1], sibling)
    mask_copy = push(mask.at[0], mask.at[1], sbs.at[2], sbr.at[2], sibling)
    arrive(0)
    for j in range(2, 5):
        forward(j)
    arrive(3)
    arrive(1)
    for j in range(5, 8):
        forward(j)
    arrive(2)

    att_done = []

    def attend(k, between=None):
        head = head_of(k, c)
        columns = heads[k].reshape(1024, 512)
        qrows = silu(nn(picked[...], columns[:, 256:512])).astype(BF)
        gate[head] = qrows[:256, :128]
        gate_out[k] = qrows[256:, :128]
        for side in (1, 0):
            kv[side] = silu(nn(hist[side], columns[:, :256])).astype(BF)
        if between is not None:
            between()
        for side in (1, 0):
            half = nt(qrows[256 * side : 256 * side + 256, 128:], kv[side, :, 128:])
            half = half * (0.5 * 128 ** (-0.5))
            weights = ((half + half * jnp.tanh(half)) * mask[side]).astype(BF)
            result = nn(weights, kv[side, :, :128])
            if side == 0:
                mixed[head] = result
            else:
                mixed_out[k] = result
                for n, (src, dst) in enumerate(((mixed_out, mixed), (gate_out, gate))):
                    n += 3 + 2 * k
                    att_done.append(push(src.at[k], dst.at[head], sbs.at[n], sbr.at[n], sibling))

    dest = owners_ref[...]
    kinds = lax.broadcasted_iota(jnp.int32, (16, 256), 0)
    hits = (kinds == dest).astype(F32)
    upper = (
        lax.broadcasted_iota(jnp.int32, (256, 256), 0)
        < lax.broadcasted_iota(jnp.int32, (256, 256), 1)
    ).astype(BF)
    before = nn(hits.astype(BF), upper)
    rank = jnp.sum(before * hits, axis=0, keepdims=True).astype(jnp.int32)
    slot = dest * CAP + rank
    place = (lax.broadcasted_iota(jnp.int32, (512, 256), 0) == slot).astype(BF)
    own_out = nn(w_out_ref[...], w_head_ref[...]).astype(BF)
    own_half[...] = own_out
    mine_rows = pl.ds(pl.multiple_of(32 * c, 32), 32)
    placed = nn(place, scores[...].astype(BF)).astype(BF).reshape(16, CAP, 128)
    place_out[:, :CAP] = placed
    place_out[:, CAP:] = jnp.broadcast_to(own_half[mine_rows, :][None], (16, 32, 128))
    rows_in[t] = place_out[t]
    event3(1)
    for copy in (hist_copy, picked_copy, mask_copy):
        copy.wait_recv()
    attend(0, functools.partial(event3, 2))
    for k in range(1, 16):
        to = (t + k) % 16
        push(place_out.at[to], rows_in.at[t], srs.at[0], srr.at[0], (to, s), True)
    event4(1)
    attend(1, functools.partial(event4, 2))
    whole_of(rows_in.at[0:15], srs.at[0], srr.at[0]).wait_recv()
    out_head[:, mine_rows] = rows_in[:, CAP:]
    every = out_head.at[:, mine_rows]
    oh_sib = push(every, every, ohs.at[0], ohr.at[0], sibling)
    attend(2)
    whole_of(heads.at[3], ups.at[0], upr.at[0]).wait_recv()
    attend(3)
    for copy in att_done:
        copy.wait_recv()

    centre = jnp.sum(jnp.sum(mixed[...], axis=0), axis=1, keepdims=True) * (1.0 / 1024.0)
    spread_sum = jnp.sum(jnp.square(mixed[...] - centre[None]), axis=0)
    scale_rows = lax.rsqrt(jnp.sum(spread_sum, axis=1, keepdims=True) * (1.0 / 1024.0) + EPS)
    for head in range(8):
        normed = (mixed[head] - centre) * scale_rows
        joined[:, 128 * head : 128 * head + 128] = (normed * gate[head].astype(F32)).astype(BF)
    oh_sib.wait_recv()
    logits = base[...] + nn(joined[...], out_head[...].reshape(1024, 128))

    delta = scores[...] - logits.astype(BF).astype(F32)
    delta16 = delta.astype(BF)
    bscore = jnp.sum(delta, axis=0, keepdims=True)

    def back_chunk(j):
        rows = pl.ds(pl.multiple_of(j * 512, 512), 512)
        dpre = nt(delta16, w_score_ref[rows, :]) * slope[j]
        d_own[j] = dpre.astype(BF)
        bd[j] = jnp.broadcast_to(jnp.sum(dpre, axis=0, keepdims=True), (8, 512))

    d_copies = {}
    for q in (0, 1, 3, 2):
        j = (1 - c) * 4 + q
        back_chunk(j)
        d_copies[q] = push(d_own.at[j], d_sib.at[q], scs.at[2 + q], scr.at[2 + q], sibling)
    for q in (0, 1, 3, 2):
        back_chunk(c * 4 + q)
    def axes_of(u):
        axis = ROUTES[u // 2][0]
        rest = [a for a in range(3) if a != axis]
        return axis, rest

    def piece(u, where, half):
        axis, rest = axes_of(u)
        index = [slice(None)] * 3
        index[axis] = where
        index[rest[0]] = pl.ds(2 * half, 2)
        return (u, *index)

    def stage1_first(u):
        axis, _ = axes_of(u)
        m = pos[axis]
        right, left, opp = (m + 1) % 4, (m + 3) % 4, (m + 2) % 4
        to_right, to_left = at_chip(axis, right, c), at_chip(axis, left, c)
        return (
            push(grads.at[piece(u, opp, 0)], x1.at[u, 0], s1s.at[0], s1r.at[u, 0], to_right, True),
            push(grads.at[piece(u, opp, 1)], x1.at[u, 1], s1s.at[0], s1r.at[u, 1], to_left, True),
        )

    def stage1_second(u):
        axis, _ = axes_of(u)
        m = pos[axis]
        right, left = (m + 1) % 4, (m + 3) % 4
        to_right, to_left = at_chip(axis, right, c), at_chip(axis, left, c)
        return (
            push(grads.at[piece(u, right, 1)], x2.at[u, 0], s1s.at[1], s1r.at[u, 2], to_right, True),
            push(grads.at[piece(u, left, 0)], x2.at[u, 1], s1s.at[1], s1r.at[u, 3], to_left, True),
        )

    def stage1_pass(u, started):
        axis, _ = axes_of(u)
        m = pos[axis]
        right, left = (m + 1) % 4, (m + 3) % 4
        out = []
        for side, (where, device) in enumerate(
            ((right, at_chip(axis, right, c)), (left, at_chip(axis, left, c)))
        ):
            started[side].wait_recv()
            mine = grads[piece(u, where, side)].astype(F32)
            y3[u, side] = (mine + x1[u, side].astype(F32)).astype(BF)
            out.append(
                push(y3.at[u, side], x3.at[u, side], s1s.at[2], s1r.at[u, 4 + side], device, True)
            )
        return out

    def stage1_end(u, started, passed):
        axis, _ = axes_of(u)
        m = pos[axis]
        for copy in (started[2], started[3], passed[0], passed[1]):
            copy.wait_recv()
        for half in range(2):
            total = grads[piece(u, m, half)].astype(F32)
            total += x2[u, 1 - half].astype(F32) + x3[u, half].astype(F32)
            w1[u // 2, u % 2, 2 * half : 2 * half + 2] = total.astype(BF)

    started, passed = {}, {}

    ct_copy.wait_recv()

    def deep_unit(q):
        d_copies[q].wait_recv()
        g = nn(ct[...], d_own[c * 4 + q]) + nn(ct_sib[...], d_sib[q])
        g = g.reshape(64, 8, 512)
        g = jnp.concatenate([g[:, :, :256], g[:, :, 256:]], axis=1)
        grads[1 + q] = g.astype(BF).reshape(4, 4, 4, 16, 256)
        started[1 + q] = stage1_first(1 + q)

    for q in (0, 1, 3):
        deep_unit(q)
    for i in range(8):
        g = nn(hid_t[512 * i : 512 * i + 512, :], delta16).astype(BF).reshape(8, 2, 2, 16, 128)
        for core in range(2):
            gs[core, 8 * i : 8 * i + 8, :, 0:128] = g[:, core, 0]
            gs[core, 8 * i : 8 * i + 8, :, 128:256] = g[:, core, 1]
    gs_copy = push(gs.at[1 - c], gs_sib, scs.at[6], scr.at[6], sibling)
    every_dpre = jnp.concatenate([d_own[j] for j in range(8)], axis=1)
    dcr = nt(every_dpre, w_deep_ref[...]) * feats32
    bcross = jnp.sum(dcr, axis=0, keepdims=True)
    dc[0] = dcr[:, :256].astype(BF)
    dc[1] = dcr[:, 256:].astype(BF)
    dc_copy = push(dc.at[1 - c], dc_sib, scs.at[7], scr.at[7], sibling)
    deep_unit(2)

    gs_copy.wait_recv()
    summed = gs[c].astype(F32) + gs_sib[...].astype(F32)
    grads[0] = summed.astype(BF).reshape(4, 4, 4, 16, 256)
    started[0] = stage1_first(0)

    for u in (1, 2, 4):
        started[u] += stage1_second(u)

    sub = lax.broadcasted_iota(jnp.int32, (16, 128), 0)
    for pair in range(32):
        deep_row = bd[pair // 4, 0:1, (pair % 4) * 128 : (pair % 4) * 128 + 128]
        cross_row = bcross[:, (pair // 8) * 128 : (pair // 8) * 128 + 128]
        tile = jnp.where(sub == 0, deep_row, jnp.where(sub == 1, cross_row, bscore))
        tile = tile.astype(BF)
        for chip in (2 * pair, 2 * pair + 1):
            grads[5, chip // 16, chip // 4 % 4, chip % 4, :, 128:256] = tile
    ft_copy.wait_recv()
    dc_copy.wait_recv()
    g = nn(ft[...], dc[c]) + nn(ft_sib[...], dc_sib[...])
    g = g.reshape(64, 8, 256)
    g = jnp.concatenate([g[:, :, :128], g[:, :, 128:]], axis=1)
    grads[5, :, :, :, :, 0:128] = g.astype(BF).reshape(4, 4, 4, 16, 128)
    started[5] = stage1_first(5)
    for u in (3, 0, 5):
        started[u] += stage1_second(u)
    for u in (1, 2, 4, 3, 0, 5):
        passed[u] = stage1_pass(u, started[u])

    def piece2(u, where):
        axis, second, _ = ROUTES[u // 2]
        rest = [a for a in range(3) if a != axis]
        index = [slice(None)] * 2
        index[rest.index(second)] = where
        return (u // 2, u % 2, *index)

    def stage2_start(u):
        axis = ROUTES[u // 2][1]
        m = pos[axis]
        return [
            push(
                w1.at[piece2(u, (m + step) % 4)],
                v1.at[u, k],
                s2s.at[0],
                s2r.at[u, k],
                at_chip(axis, (m + step) % 4, c),
                True,
            )
            for k, step in enumerate((1, 3, 2))
        ]

    def stage2_end(u, begun):
        total = w1[piece2(u, pos[ROUTES[u // 2][1]])].astype(F32)
        for k, copy in enumerate(begun):
            copy.wait_recv()
            total += v1[u, k].astype(F32)
        w2[u // 2, u % 2] = total.astype(BF)

    def stage3_start(r):
        axis = ROUTES[r][2]
        m = pos[axis]
        last[r, m, c] = w2[r, :, m]
        for k in range(4):
            where = (m + k) % 4
            for other in range(2):
                if k == 0 and other == 0:
                    continue
                core = c if other == 0 else 1 - c
                push(
                    w2.at[r, :, where],
                    last.at[r, m, c],
                    s3s.at[k],
                    s3r.at[k],
                    at_chip(axis, where, core),
                    True,
                )

    def stage3_end(r):
        scale = 1.0 / 32768.0
        for core in range(2):
            total = last[r, 0, core].astype(F32)
            for k in range(1, 4):
                total += last[r, k, core].astype(F32)
            fin[core, 2 * r : 2 * r + 2] = total * scale

    begun = {}
    for u in (1, 2, 4, 3, 0, 5):
        stage1_end(u, started[u], passed[u])
        begun[u] = stage2_start(u)
    for r in range(3):
        for u in (2 * r, 2 * r + 1):
            stage2_end(u, begun[u])
        stage3_start(r)
    o_rows[...] = rows_in[:, :CAP]
    stage3_all = [whole_of(last.at[:, 0, 0], s3s.at[0], s3r.at[0])]
    stage3_all += [whole_of(last.at[:, 0], s3s.at[k], s3r.at[k]) for k in range(1, 4)]
    for copy in stage3_all:
        copy.wait_recv()
    for r in range(3):
        stage3_end(r)

    def own_rows(core, unit, half, cols):
        lower = fin[core, unit, 8 * half : 8 * half + 4, cols]
        higher = fin[core, unit, 8 * half + 4 : 8 * half + 8, cols]
        return jnp.where(c == 0, lower, higher)

    for core in range(2):
        for half in range(2):
            for q in range(4):
                at = core * 2048 + q * 512 + half * 256
                o_deep[:, at : at + 256] = own_rows(core, 1 + q, half, slice(0, 256))
            at = core * 256 + half * 128
            o_cross[:, at : at + 128] = own_rows(core, 5, half, slice(0, 128))
    for half in range(2):
        cols = slice(128 * half, 128 * half + 128)
        o_score[16 * half : 16 * half + 16] = jnp.where(c == 0, fin[0, 0, :, cols], fin[1, 0, :, cols])
    chip = t * 4 + y
    bias = fin[0, 5, 0:8, 128:256] + fin[1, 5, 0:8, 128:256]
    for row, first in enumerate((chip % 2 * 64 + c * 32, chip % 16 * 8 + c * 4, chip * 2 + c)):
        o_bias[row : row + 1] = pltpu.roll(bias, (128 - first) % 128, 1)[row : row + 1]
    sends += stage3_all
    sends.append(whole_of(heads.at[0, 0:9], p1s.at[0], upr.at[0]))
    sends.append(whole_of(heads.at[0:3, 0:12], p2s.at[0], upr.at[0]))
    sends.append(whole_of(heads.at[0], ups.at[0], upr.at[0]))
    sends.append(whole_of(place_out.at[0:15], srs.at[0], srr.at[0]))
    sends.append(whole_of(x1, s1s.at[0], upr.at[0]))
    sends.append(whole_of(x2, s1s.at[1], upr.at[0]))
    sends.append(whole_of(x3, s1s.at[2], upr.at[0]))
    sends.append(whole_of(v1, s2s.at[0], upr.at[0]))
    for copy in sends:
        copy.wait_send()


def results(cross, deep, score, bias, rows, o_cross, o_bcross, o_deep, o_bdeep, o_score, o_bscore, o_rows):
    o_cross[...] = cross[...]
    o_deep[...] = deep[...]
    o_score[...] = score[...]
    o_rows[...] = rows[...]
    o_bdeep[...] = bias[0, 0:32]
    o_bcross[...] = bias[1, 0:4]
    o_bscore[...] = bias[2, 0:1]


def local(
    embeddings,
    action_ids,
    segment_ids,
    cand_pos,
    owners,
    features,
    action_table,
    w_query,
    w_keys,
    w_out,
    w_head,
    w_cross,
    b_cross,
    w_deep,
    b_deep,
    w_score,
    b_score,
):
    dma = pltpu.SemaphoreType.DMA
    vmem = pltpu.VMEM
    whole = pl.BlockSpec(memory_space=pltpu.VMEM)
    stay = pl.BlockSpec(memory_space=pl.ANY)
    g_cross, g_deep, g_score, bias, rows = pl.pallas_call(
        kernel,
        out_shape=(
            jax.ShapeDtypeStruct((4, 512), F32),
            jax.ShapeDtypeStruct((4, 4096), F32),
            jax.ShapeDtypeStruct((32, 128), F32),
            jax.ShapeDtypeStruct((8, 128), F32),
            jax.ShapeDtypeStruct((16, CAP, 128), BF),
        ),
        in_specs=[stay] * 17,
        out_specs=(whole,) * 5,
        scratch_shapes=[
            vmem((1, 1024), jnp.int32),
            vmem((1, 1024), jnp.int32),
            vmem((1, 256), jnp.int32),
            vmem((1, 256), jnp.int32),
            vmem((256, 512), BF),
            vmem((16, 1024), BF),
            vmem((64, 1024), BF),
            vmem((1024, 128), BF),
            vmem((512, 512), BF),
            vmem((512,), BF),
            vmem((4096,), BF),
            vmem((1, 128), BF),
            vmem((1024, 1024), BF),
            vmem((512, 4096), BF),
            vmem((4096, 128), BF),
            vmem((4, 16, 64, 512), BF),
            vmem((16, 64, 128), BF),
            vmem((64, 128), BF),
            vmem((128, 1024), BF),
            vmem((2, 1024, 1024), BF),
            vmem((512, 1024), BF),
            vmem((2, 256, 1024), F32),
            vmem((2, 1024, 256), BF),
            vmem((8, 256, 128), BF),
            vmem((4, 256, 128), BF),
            vmem((8, 256, 128), F32),
            vmem((4, 256, 128), F32),
            vmem((256, 1024), BF),
            vmem((256, 128), F32),
            vmem((256, 512), BF),
            vmem((512, 256), BF),
            vmem((512, 256), BF),
            vmem((512, 256), BF),
            vmem((512, 256), BF),
            vmem((4096, 256), BF),
            vmem((8, 256, 512), F32),
            vmem((256, 128), F32),
            vmem((16, CAP + 32, 128), BF),
            vmem((16, CAP + 32, 128), BF),
            vmem((8, 256, 512), BF),
            vmem((4, 256, 512), BF),
            vmem((2, 64, 16, 256), BF),
            vmem((64, 16, 256), BF),
            vmem((2, 256, 256), BF),
            vmem((256, 256), BF),
            vmem((8, 8, 512), F32),
            vmem((6, 4, 4, 4, 16, 256), BF),
            vmem((6, 2, 2, 4, 16, 256), BF),
            vmem((6, 2, 2, 4, 16, 256), BF),
            vmem((6, 2, 2, 4, 16, 256), BF),
            vmem((6, 2, 2, 4, 16, 256), BF),
            vmem((3, 2, 4, 4, 16, 256), BF),
            vmem((6, 3, 4, 16, 256), BF),
            vmem((3, 2, 4, 16, 256), BF),
            vmem((3, 4, 2, 2, 16, 256), BF),
            vmem((2, 6, 16, 256), F32),
            dma((3,)),
            dma((6, 6)),
            dma((1,)),
            dma((6, 3)),
            dma((4,)),
            dma((4,)),
            dma((8,)),
            dma((8,)),
            dma((1,)),
            dma((1,)),
            dma((15,)),
            dma((3, 4)),
            dma((1,)),
            dma((3, 3)),
            dma((1,)),
            dma((3, 4, 3)),
            dma((1,)),
            dma((1,)),
            dma((11,)),
            dma((11,)),
            dma((1,)),
            dma((1,)),
        ],
        compiler_params=pltpu.CompilerParams(
            collective_id=0, has_side_effects=True, vmem_limit_bytes=56 * 1024 * 1024
        ),
    )(
        embeddings,
        action_ids.reshape(1, -1),
        segment_ids,
        cand_pos.reshape(1, -1),
        owners.reshape(1, -1),
        features,
        action_table,
        w_query,
        w_keys,
        w_out,
        w_head,
        w_cross,
        b_cross,
        w_deep,
        b_deep,
        w_score,
        b_score.reshape(1, -1),
    )
    return pl.pallas_call(
        results,
        out_shape=(
            jax.ShapeDtypeStruct((4, 512), F32),
            jax.ShapeDtypeStruct((4,), F32),
            jax.ShapeDtypeStruct((4, 4096), F32),
            jax.ShapeDtypeStruct((32,), F32),
            jax.ShapeDtypeStruct((32, 128), F32),
            jax.ShapeDtypeStruct((1,), F32),
            jax.ShapeDtypeStruct((512, 128), BF),
        ),
        in_specs=[whole] * 5,
        out_specs=(whole,) * 7,
    )(g_cross, g_deep, g_score, bias, rows.reshape(512, 128))


def solution(mesh):
    both = ("teacher", "student")
    return jax.shard_map(
        local,
        mesh=mesh,
        in_specs=(
            P(both, None),
            P(both),
            P(both, None),
            P(both),
            P(both, None),
            P(both, None),
            P(),
            P("teacher", None),
            P("teacher", None),
            P("teacher", None),
            P(),
            P(),
            P(),
            P(),
            P(),
            P(),
            P(),
        ),
        out_specs=(
            P(both, None),
            P(both),
            P(both, None),
            P(both),
            P(both, None),
            P(both),
            P(both, None),
        ),
        check_vma=False,
    )
```

```python
import functools

import jax
import jax.numpy as jnp
from jax import lax
from jax.experimental import pallas as pl
from jax.experimental.pallas import tpu as pltpu
from jax.sharding import PartitionSpec as P

CAP = 32
EPS = 1e-05
BF = jnp.bfloat16
F32 = jnp.float32
MESH = pl.DeviceIdType.MESH

ROUTES = ((0, 1, 2), (1, 2, 0), (2, 0, 1))


def nn(a, b):
    return lax.dot_general(a, b, (((1,), (0,)), ((), ())), preferred_element_type=F32)


def nt(a, b):
    return lax.dot_general(a, b, (((1,), (1,)), ((), ())), preferred_element_type=F32)


def silu(v):
    half = 0.5 * v
    return half + half * jnp.tanh(half)


def flip(v):
    return v.astype(F32).T.astype(BF)


def kernel(
    emb_hbm,
    ids_hbm,
    segs_hbm,
    cand_hbm,
    owners_hbm,
    feat_hbm,
    table_hbm,
    w_query_hbm,
    w_keys_hbm,
    w_out_hbm,
    w_head_hbm,
    w_cross_hbm,
    b_cross_hbm,
    w_deep_hbm,
    b_deep_hbm,
    w_score_hbm,
    b_score_hbm,
    o_cross,
    o_deep,
    o_score,
    o_bias,
    o_rows,
    ids_ref,
    segs_ref,
    cand_ref,
    owners_ref,
    feat_ref,
    table_ref,
    w_out_ref,
    w_head_ref,
    w_cross_ref,
    b_cross_ref,
    b_deep_ref,
    b_score_ref,
    emb,
    w_deep_ref,
    w_score_ref,
    heads,
    out_head,
    own_half,
    table_pad,
    hist,
    picked,
    mask,
    kv,
    gate,
    gate_out,
    mixed,
    mixed_out,
    joined,
    base,
    crossed,
    ct,
    ct_sib,
    ft,
    ft_sib,
    hid_t,
    slope,
    scores,
    place_out,
    rows_in,
    d_own,
    d_sib,
    gs,
    gs_sib,
    dc,
    dc_sib,
    bd,
    grads,
    x1,
    x2,
    x3,
    y3,
    w1,
    v1,
    w2,
    last,
    fin,
    s1s,
    s1r,
    s2s,
    s2r,
    s3s,
    s3r,
    scs,
    scr,
    srs,
    srr,
    lds,
    hds,
    p1s,
    p1r,
    p2s,
    p2r,
    ups,
    upr,
    sbs,
    sbr,
    ohs,
    ohr,
):
    t = lax.axis_index("teacher")
    s = lax.axis_index("student")
    z, x = t // 4, t % 4
    y, c = s // 2, s % 2
    pos = (z, x, y)
    sibling = (t, y * 2 + 1 - c)
    sends = []

    def at_chip(axis, value, core):
        p = list(pos)
        p[axis] = value
        return (p[0] * 4 + p[1], p[2] * 2 + core)

    def push(src, dst, send_sem, recv_sem, device, shared=False):
        copy = pltpu.make_async_remote_copy(
            src_ref=src,
            dst_ref=dst,
            send_sem=send_sem,
            recv_sem=recv_sem,
            device_id=device,
            device_id_type=MESH,
        )
        copy.start()
        if not shared:
            sends.append(copy)
        return copy

    def whole_of(ref, send_sem, recv_sem):
        return pltpu.make_async_remote_copy(
            src_ref=ref,
            dst_ref=ref,
            send_sem=send_sem,
            recv_sem=recv_sem,
            device_id=sibling,
            device_id_type=MESH,
        )

    peers = [at_chip(axis, (pos[axis] + k) % 4, c) for axis in (0, 1) for k in (1, 2, 3)]
    peers += [at_chip(2, (y + k) % 4, c) for k in (1, 3)] + [sibling]
    barrier = pltpu.get_barrier_semaphore()
    for peer in peers:
        pl.semaphore_signal(barrier, inc=1, device_id=peer, device_id_type=MESH)

    odd = y % 2
    first = (1 - c) * x + c * z
    second = (1 - c) * z + c * x

    def shard(i, j):
        i, j = (first + i) % 4, (second + j) % 4
        return (1 - c) * (j * 4 + i) + c * (i * 4 + j)

    def head_of(k, core):
        return (4 + 2 * odd + core, core, 2 + core, 6 - 2 * odd + core)[k]

    own_cols = []
    for k in range(3):
        for part, (ref, start) in enumerate(
            ((w_keys_hbm, 0), (w_keys_hbm, 1024), (w_query_hbm, 0), (w_query_hbm, 1024))
        ):
            cols = pl.ds(pl.multiple_of(start + head_of(k, c) * 128, 128), 128)
            own_cols.append(
                pltpu.make_async_copy(
                    ref.at[:, cols],
                    heads.at[k, t, :, 128 * part : 128 * part + 128],
                    hds.at[k, part],
                )
            )
            own_cols[-1].start()
    pairs = (
        (feat_hbm, feat_ref),
        (w_cross_hbm, w_cross_ref),
        (b_cross_hbm, b_cross_ref),
        (b_score_hbm, b_score_ref),
        (ids_hbm, ids_ref),
        (table_hbm, table_ref),
        (segs_hbm, segs_ref),
        (cand_hbm, cand_ref),
        (owners_hbm, owners_ref),
        (w_out_hbm, w_out_ref),
        (w_head_hbm, w_head_ref),
        (b_deep_hbm, b_deep_ref),
        (w_deep_hbm, w_deep_ref),
        (w_score_hbm, w_score_ref),
        (emb_hbm, emb),
    )
    loads = [pltpu.make_async_copy(src, dst, lds.at[n]) for n, (src, dst) in enumerate(pairs)]
    for load in loads:
        load.start()

    def along(k, i, j, rows, send_sem, recv_sem, device):
        ref = heads.at[k, shard(i, j), rows]
        return push(ref, ref, send_sem, recv_sem, device, True)

    full = slice(0, 64)
    y_next = (t, (y + 1 + 2 * c) % 4 * 2 + c)
    p1, p2 = {}, {}

    def to_y(k, i, j):
        if k == 0:
            up = heads.at[0, shard(i, j)]
            push(up, heads.at[3, shard(i, j)], ups.at[0], upr.at[0], y_next, True)

    def spread(k, i):
        for side, step in enumerate((1, 3, 2) if k == 0 else (1, 3)):
            device = (shard(0, step), s)
            p2[k, i, side] = along(k, i, 0, full, p2s.at[0], p2r.at[k, i, side], device)
        to_y(k, i, 0)

    def hop(k):
        for side, step in enumerate((1, 3, 2)):
            device = (shard(step, 0), s)
            p1[k, side] = along(k, 0, 0, full, p1s.at[0], p1r.at[k, side], device)

    def hop_end(k):
        for side in range(3):
            p1[k, side].wait_recv()

    def arrive(i):
        for side, j in enumerate((3, 1, 2)):
            p2[0, i, side].wait_recv()
            to_y(0, i, j)

    def event3(k):
        for i in (0, 1, 3, 2):
            side = 0 if i < 2 else 1
            step = (1, 3)[side]
            p2[k, i, side].wait_recv()
            device = (shard(0, step), s)
            p2[k, i, 2] = along(k, i, 4 - step, full, p2s.at[0], p2r.at[k, i, 2], device)
            p2[k, i, 1 - side].wait_recv()

    def event4(k):
        for i in range(4):
            p2[k, i, 2].wait_recv()

    for copy in own_cols:
        copy.wait()
    pl.semaphore_wait(barrier, len(peers))
    hop(0)
    spread(0, 0)
    hop(1)
    hop(2)

    for load in loads[:12]:
        load.wait()
    feats = feat_ref[...]
    feats32 = feats.astype(F32)
    cross = nn(feats, w_cross_ref[...]) + b_cross_ref[...].astype(F32).reshape(1, 512)
    crossed[...] = (feats32 * cross + feats32).astype(BF)
    ct[...] = flip(crossed[...])
    ft[...] = flip(feats)
    ct_copy = push(ct, ct_sib, scs.at[0], scr.at[0], sibling)
    ft_copy = push(ft, ft_sib, scs.at[1], scr.at[1], sibling)
    scores[...] = jnp.broadcast_to(b_score_ref[...].astype(F32), scores.shape)
    table_pad[...] = jnp.zeros_like(table_pad)
    table_pad[0:16] = table_ref[...]
    loads[14].wait()

    def embed(i):
        rows = slice(i * 256, i * 256 + 256)
        kinds = lax.broadcasted_iota(jnp.int32, (128, 256), 0)
        onehot = flip(kinds == ids_ref[:, rows])
        hist[0, rows, :] = (emb[rows, :].astype(F32) + nn(onehot, table_pad[...])).astype(BF)

    for i in range(4):
        embed(i)
    hist_copy = push(hist.at[0], hist.at[1], sbs.at[0], sbr.at[0], sibling)
    hop_end(0)
    for i in (3, 1, 2):
        spread(0, i)
    b_deep32 = b_deep_ref[...].astype(F32).reshape(1, 4096)

    def forward(j):
        cols = slice(j * 512, j * 512 + 512)
        pre = nn(crossed[...], w_deep_ref[:, cols]) + b_deep32[:, cols]
        sigma = 0.5 + 0.5 * jnp.tanh(0.5 * pre)
        hidden = (pre * sigma).astype(BF)
        slope[j] = sigma * (1.0 + pre * (1.0 - sigma))
        hid_t[cols, :] = hidden.T
        scores[...] += nn(hidden, w_score_ref[cols, :])

    loads[12].wait()
    loads[13].wait()
    for j in range(2):
        forward(j)
    for k in (1, 2):
        hop_end(k)
        for i in range(4):
            spread(k, i)

    where_col = jnp.broadcast_to(cand_ref[...], (128, 256)).astype(F32).T[:, 0:1]
    places = lax.broadcasted_iota(jnp.int32, (256, 1024), 1).astype(F32)
    segs = segs_ref[...].astype(F32)
    chosen = (places == where_col).astype(F32)
    picked[0:256] = nn(chosen.astype(BF), hist[0]).astype(BF)
    seg_col = jnp.sum(chosen * segs, axis=1, keepdims=True)
    mask[0] = jnp.where((segs == seg_col) & (places <= where_col), 1.0, 0.0)
    base[...] = nn(picked[0:256], w_head_ref[...])
    picked_copy = push(picked.at[0:256], picked.at[256:512], sbs.at[1], sbr.at[1], sibling)
    mask_copy = push(mask.at[0], mask.at[1], sbs.at[2], sbr.at[2], sibling)
    arrive(0)
    for j in range(2, 5):
        forward(j)
    arrive(3)
    arrive(1)
    for j in range(5, 8):
        forward(j)
    arrive(2)

    att_done = []

    def attend(k, between=None):
        head = head_of(k, c)
        columns = heads[k].reshape(1024, 512)
        qrows = silu(nn(picked[...], columns[:, 256:512])).astype(BF)
        gate[head] = qrows[:256, :128]
        gate_out[k] = qrows[256:, :128]
        for side in (1, 0):
            kv[side] = silu(nn(hist[side], columns[:, :256])).astype(BF)
        if between is not None:
            between()
        for side in (1, 0):
            half = nt(qrows[256 * side : 256 * side + 256, 128:], kv[side, :, 128:])
            half = half * (0.5 * 128 ** (-0.5))
            weights = ((half + half * jnp.tanh(half)) * mask[side]).astype(BF)
            result = nn(weights, kv[side, :, :128])
            if side == 0:
                mixed[head] = result
            else:
                mixed_out[k] = result
                for n, (src, dst) in enumerate(((mixed_out, mixed), (gate_out, gate))):
                    n += 3 + 2 * k
                    att_done.append(push(src.at[k], dst.at[head], sbs.at[n], sbr.at[n], sibling))

    dest = owners_ref[...]
    kinds = lax.broadcasted_iota(jnp.int32, (16, 256), 0)
    hits = (kinds == dest).astype(F32)
    upper = (
        lax.broadcasted_iota(jnp.int32, (256, 256), 0)
        < lax.broadcasted_iota(jnp.int32, (256, 256), 1)
    ).astype(BF)
    before = nn(hits.astype(BF), upper)
    rank = jnp.sum(before * hits, axis=0, keepdims=True).astype(jnp.int32)
    slot = dest * CAP + rank
    place = (lax.broadcasted_iota(jnp.int32, (512, 256), 0) == slot).astype(BF)
    own_out = nn(w_out_ref[...], w_head_ref[...]).astype(BF)
    own_half[...] = own_out
    mine_rows = pl.ds(pl.multiple_of(32 * c, 32), 32)
    placed = nn(place, scores[...].astype(BF)).astype(BF).reshape(16, CAP, 128)
    place_out[:, :CAP] = placed
    place_out[:, CAP:] = jnp.broadcast_to(own_half[mine_rows, :][None], (16, 32, 128))
    rows_in[t] = place_out[t]
    event3(1)
    for copy in (hist_copy, picked_copy, mask_copy):
        copy.wait_recv()
    attend(0, functools.partial(event3, 2))
    for k in range(1, 16):
        to = (t + k) % 16
        push(place_out.at[to], rows_in.at[t], srs.at[0], srr.at[0], (to, s), True)
    event4(1)
    attend(1)
    whole_of(heads.at[3], ups.at[0], upr.at[0]).wait_recv()
    attend(3)
    whole_of(rows_in.at[0:15], srs.at[0], srr.at[0]).wait_recv()
    out_head[:, mine_rows] = rows_in[:, CAP:]
    every = out_head.at[:, mine_rows]
    oh_sib = push(every, every, ohs.at[0], ohr.at[0], sibling)
    event4(2)
    attend(2)
    for copy in att_done:
        copy.wait_recv()

    centre = jnp.sum(jnp.sum(mixed[...], axis=0), axis=1, keepdims=True) * (1.0 / 1024.0)
    spread_sum = jnp.sum(jnp.square(mixed[...] - centre[None]), axis=0)
    scale_rows = lax.rsqrt(jnp.sum(spread_sum, axis=1, keepdims=True) * (1.0 / 1024.0) + EPS)
    for head in range(8):
        normed = (mixed[head] - centre) * scale_rows
        joined[:, 128 * head : 128 * head + 128] = (normed * gate[head].astype(F32)).astype(BF)
    oh_sib.wait_recv()
    logits = base[...] + nn(joined[...], out_head[...].reshape(1024, 128))

    delta = scores[...] - logits.astype(BF).astype(F32)
    delta16 = delta.astype(BF)
    bscore = jnp.sum(delta, axis=0, keepdims=True)

    def back_chunk(j):
        rows = pl.ds(pl.multiple_of(j * 512, 512), 512)
        dpre = nt(delta16, w_score_ref[rows, :]) * slope[j]
        d_own[j] = dpre.astype(BF)
        bd[j] = jnp.broadcast_to(jnp.sum(dpre, axis=0, keepdims=True), (8, 512))

    d_copies = {}
    for q in (0, 1, 3, 2):
        j = (1 - c) * 4 + q
        back_chunk(j)
        d_copies[q] = push(d_own.at[j], d_sib.at[q], scs.at[2 + q], scr.at[2 + q], sibling)
    for q in (0, 1, 3, 2):
        back_chunk(c * 4 + q)
    def axes_of(u):
        axis = ROUTES[u // 2][0]
        rest = [a for a in range(3) if a != axis]
        return axis, rest

    def piece(u, where, half):
        axis, rest = axes_of(u)
        index = [slice(None)] * 3
        index[axis] = where
        index[rest[0]] = pl.ds(2 * half, 2)
        return (u, *index)

    def stage1_first(u):
        axis, _ = axes_of(u)
        m = pos[axis]
        right, left, opp = (m + 1) % 4, (m + 3) % 4, (m + 2) % 4
        to_right, to_left = at_chip(axis, right, c), at_chip(axis, left, c)
        return (
            push(grads.at[piece(u, opp, 0)], x1.at[u, 0], s1s.at[0], s1r.at[u, 0], to_right, True),
            push(grads.at[piece(u, opp, 1)], x1.at[u, 1], s1s.at[0], s1r.at[u, 1], to_left, True),
        )

    def stage1_second(u):
        axis, _ = axes_of(u)
        m = pos[axis]
        right, left = (m + 1) % 4, (m + 3) % 4
        to_right, to_left = at_chip(axis, right, c), at_chip(axis, left, c)
        return (
            push(grads.at[piece(u, right, 1)], x2.at[u, 0], s1s.at[1], s1r.at[u, 2], to_right, True),
            push(grads.at[piece(u, left, 0)], x2.at[u, 1], s1s.at[1], s1r.at[u, 3], to_left, True),
        )

    def stage1_pass(u, started):
        axis, _ = axes_of(u)
        m = pos[axis]
        right, left = (m + 1) % 4, (m + 3) % 4
        out = []
        for side, (where, device) in enumerate(
            ((right, at_chip(axis, right, c)), (left, at_chip(axis, left, c)))
        ):
            started[side].wait_recv()
            mine = grads[piece(u, where, side)].astype(F32)
            y3[u, side] = (mine + x1[u, side].astype(F32)).astype(BF)
            out.append(
                push(y3.at[u, side], x3.at[u, side], s1s.at[2], s1r.at[u, 4 + side], device, True)
            )
        return out

    def stage1_end(u, started, passed):
        axis, _ = axes_of(u)
        m = pos[axis]
        for copy in (started[2], started[3], passed[0], passed[1]):
            copy.wait_recv()
        for half in range(2):
            total = grads[piece(u, m, half)].astype(F32)
            total += x2[u, 1 - half].astype(F32) + x3[u, half].astype(F32)
            w1[u // 2, u % 2, 2 * half : 2 * half + 2] = total.astype(BF)

    started, passed = {}, {}

    ct_copy.wait_recv()

    def deep_unit(q):
        d_copies[q].wait_recv()
        g = nn(ct[...], d_own[c * 4 + q]) + nn(ct_sib[...], d_sib[q])
        g = g.reshape(64, 8, 512)
        g = jnp.concatenate([g[:, :, :256], g[:, :, 256:]], axis=1)
        grads[1 + q] = g.astype(BF).reshape(4, 4, 4, 16, 256)
        started[1 + q] = stage1_first(1 + q)

    for q in (0, 1, 3):
        deep_unit(q)
    for i in range(8):
        g = nn(hid_t[512 * i : 512 * i + 512, :], delta16).astype(BF).reshape(8, 2, 2, 16, 128)
        for core in range(2):
            gs[core, 8 * i : 8 * i + 8, :, 0:128] = g[:, core, 0]
            gs[core, 8 * i : 8 * i + 8, :, 128:256] = g[:, core, 1]
    gs_copy = push(gs.at[1 - c], gs_sib, scs.at[6], scr.at[6], sibling)
    every_dpre = jnp.concatenate([d_own[j] for j in range(8)], axis=1)
    dcr = nt(every_dpre, w_deep_ref[...]) * feats32
    bcross = jnp.sum(dcr, axis=0, keepdims=True)
    dc[0] = dcr[:, :256].astype(BF)
    dc[1] = dcr[:, 256:].astype(BF)
    dc_copy = push(dc.at[1 - c], dc_sib, scs.at[7], scr.at[7], sibling)
    deep_unit(2)

    gs_copy.wait_recv()
    summed = gs[c].astype(F32) + gs_sib[...].astype(F32)
    grads[0] = summed.astype(BF).reshape(4, 4, 4, 16, 256)
    started[0] = stage1_first(0)

    for u in (1, 2, 4):
        started[u] += stage1_second(u)

    sub = lax.broadcasted_iota(jnp.int32, (16, 128), 0)
    for pair in range(32):
        deep_row = bd[pair // 4, 0:1, (pair % 4) * 128 : (pair % 4) * 128 + 128]
        cross_row = bcross[:, (pair // 8) * 128 : (pair // 8) * 128 + 128]
        tile = jnp.where(sub == 0, deep_row, jnp.where(sub == 1, cross_row, bscore))
        tile = tile.astype(BF)
        for chip in (2 * pair, 2 * pair + 1):
            grads[5, chip // 16, chip // 4 % 4, chip % 4, :, 128:256] = tile
    ft_copy.wait_recv()
    dc_copy.wait_recv()
    g = nn(ft[...], dc[c]) + nn(ft_sib[...], dc_sib[...])
    g = g.reshape(64, 8, 256)
    g = jnp.concatenate([g[:, :, :128], g[:, :, 128:]], axis=1)
    grads[5, :, :, :, :, 0:128] = g.astype(BF).reshape(4, 4, 4, 16, 128)
    started[5] = stage1_first(5)
    for u in (3, 0, 5):
        started[u] += stage1_second(u)
    for u in (1, 2, 4, 3, 0, 5):
        passed[u] = stage1_pass(u, started[u])

    def piece2(u, where):
        axis, second, _ = ROUTES[u // 2]
        rest = [a for a in range(3) if a != axis]
        index = [slice(None)] * 2
        index[rest.index(second)] = where
        return (u // 2, u % 2, *index)

    def stage2_start(u):
        axis = ROUTES[u // 2][1]
        m = pos[axis]
        return [
            push(
                w1.at[piece2(u, (m + step) % 4)],
                v1.at[u, k],
                s2s.at[0],
                s2r.at[u, k],
                at_chip(axis, (m + step) % 4, c),
                True,
            )
            for k, step in enumerate((1, 3, 2))
        ]

    def stage2_end(u, begun):
        total = w1[piece2(u, pos[ROUTES[u // 2][1]])].astype(F32)
        for k, copy in enumerate(begun):
            copy.wait_recv()
            total += v1[u, k].astype(F32)
        w2[u // 2, u % 2] = total.astype(BF)

    def stage3_start(r):
        axis = ROUTES[r][2]
        m = pos[axis]
        last[r, m, c] = w2[r, :, m]
        for k in range(4):
            where = (m + k) % 4
            for other in range(2):
                if k == 0 and other == 0:
                    continue
                core = c if other == 0 else 1 - c
                push(
                    w2.at[r, :, where],
                    last.at[r, m, c],
                    s3s.at[k],
                    s3r.at[k],
                    at_chip(axis, where, core),
                    True,
                )

    def stage3_end(r):
        scale = 1.0 / 32768.0
        for core in range(2):
            total = last[r, 0, core].astype(F32)
            for k in range(1, 4):
                total += last[r, k, core].astype(F32)
            fin[core, 2 * r : 2 * r + 2] = total * scale

    begun = {}
    for u in (1, 2, 4, 3, 0, 5):
        stage1_end(u, started[u], passed[u])
        begun[u] = stage2_start(u)
    for r in range(3):
        for u in (2 * r, 2 * r + 1):
            stage2_end(u, begun[u])
        stage3_start(r)
    o_rows[...] = rows_in[:, :CAP]
    stage3_all = [whole_of(last.at[:, 0, 0], s3s.at[0], s3r.at[0])]
    stage3_all += [whole_of(last.at[:, 0], s3s.at[k], s3r.at[k]) for k in range(1, 4)]
    for copy in stage3_all:
        copy.wait_recv()
    for r in range(3):
        stage3_end(r)

    def own_rows(core, unit, half, cols):
        lower = fin[core, unit, 8 * half : 8 * half + 4, cols]
        higher = fin[core, unit, 8 * half + 4 : 8 * half + 8, cols]
        return jnp.where(c == 0, lower, higher)

    for core in range(2):
        for half in range(2):
            for q in range(4):
                at = core * 2048 + q * 512 + half * 256
                o_deep[:, at : at + 256] = own_rows(core, 1 + q, half, slice(0, 256))
            at = core * 256 + half * 128
            o_cross[:, at : at + 128] = own_rows(core, 5, half, slice(0, 128))
    for half in range(2):
        cols = slice(128 * half, 128 * half + 128)
        o_score[16 * half : 16 * half + 16] = jnp.where(c == 0, fin[0, 0, :, cols], fin[1, 0, :, cols])
    chip = t * 4 + y
    bias = fin[0, 5, 0:8, 128:256] + fin[1, 5, 0:8, 128:256]
    for row, first in enumerate((chip % 2 * 64 + c * 32, chip % 16 * 8 + c * 4, chip * 2 + c)):
        o_bias[row : row + 1] = pltpu.roll(bias, (128 - first) % 128, 1)[row : row + 1]
    sends += stage3_all
    sends.append(whole_of(heads.at[0, 0:9], p1s.at[0], upr.at[0]))
    sends.append(whole_of(heads.at[0:3, 0:12], p2s.at[0], upr.at[0]))
    sends.append(whole_of(heads.at[0], ups.at[0], upr.at[0]))
    sends.append(whole_of(place_out.at[0:15], srs.at[0], srr.at[0]))
    sends.append(whole_of(x1, s1s.at[0], upr.at[0]))
    sends.append(whole_of(x2, s1s.at[1], upr.at[0]))
    sends.append(whole_of(x3, s1s.at[2], upr.at[0]))
    sends.append(whole_of(v1, s2s.at[0], upr.at[0]))
    for copy in sends:
        copy.wait_send()


def results(cross, deep, score, bias, rows, o_cross, o_bcross, o_deep, o_bdeep, o_score, o_bscore, o_rows):
    o_cross[...] = cross[...]
    o_deep[...] = deep[...]
    o_score[...] = score[...]
    o_rows[...] = rows[...]
    o_bdeep[...] = bias[0, 0:32]
    o_bcross[...] = bias[1, 0:4]
    o_bscore[...] = bias[2, 0:1]


def local(
    embeddings,
    action_ids,
    segment_ids,
    cand_pos,
    owners,
    features,
    action_table,
    w_query,
    w_keys,
    w_out,
    w_head,
    w_cross,
    b_cross,
    w_deep,
    b_deep,
    w_score,
    b_score,
):
    dma = pltpu.SemaphoreType.DMA
    vmem = pltpu.VMEM
    whole = pl.BlockSpec(memory_space=pltpu.VMEM)
    stay = pl.BlockSpec(memory_space=pl.ANY)
    g_cross, g_deep, g_score, bias, rows = pl.pallas_call(
        kernel,
        out_shape=(
            jax.ShapeDtypeStruct((4, 512), F32),
            jax.ShapeDtypeStruct((4, 4096), F32),
            jax.ShapeDtypeStruct((32, 128), F32),
            jax.ShapeDtypeStruct((8, 128), F32),
            jax.ShapeDtypeStruct((16, CAP, 128), BF),
        ),
        in_specs=[stay] * 17,
        out_specs=(whole,) * 5,
        scratch_shapes=[
            vmem((1, 1024), jnp.int32),
            vmem((1, 1024), jnp.int32),
            vmem((1, 256), jnp.int32),
            vmem((1, 256), jnp.int32),
            vmem((256, 512), BF),
            vmem((16, 1024), BF),
            vmem((64, 1024), BF),
            vmem((1024, 128), BF),
            vmem((512, 512), BF),
            vmem((512,), BF),
            vmem((4096,), BF),
            vmem((1, 128), BF),
            vmem((1024, 1024), BF),
            vmem((512, 4096), BF),
            vmem((4096, 128), BF),
            vmem((4, 16, 64, 512), BF),
            vmem((16, 64, 128), BF),
            vmem((64, 128), BF),
            vmem((128, 1024), BF),
            vmem((2, 1024, 1024), BF),
            vmem((512, 1024), BF),
            vmem((2, 256, 1024), F32),
            vmem((2, 1024, 256), BF),
            vmem((8, 256, 128), BF),
            vmem((4, 256, 128), BF),
            vmem((8, 256, 128), F32),
            vmem((4, 256, 128), F32),
            vmem((256, 1024), BF),
            vmem((256, 128), F32),
            vmem((256, 512), BF),
            vmem((512, 256), BF),
            vmem((512, 256), BF),
            vmem((512, 256), BF),
            vmem((512, 256), BF),
            vmem((4096, 256), BF),
            vmem((8, 256, 512), F32),
            vmem((256, 128), F32),
            vmem((16, CAP + 32, 128), BF),
            vmem((16, CAP + 32, 128), BF),
            vmem((8, 256, 512), BF),
            vmem((4, 256, 512), BF),
            vmem((2, 64, 16, 256), BF),
            vmem((64, 16, 256), BF),
            vmem((2, 256, 256), BF),
            vmem((256, 256), BF),
            vmem((8, 8, 512), F32),
            vmem((6, 4, 4, 4, 16, 256), BF),
            vmem((6, 2, 2, 4, 16, 256), BF),
            vmem((6, 2, 2, 4, 16, 256), BF),
            vmem((6, 2, 2, 4, 16, 256), BF),
            vmem((6, 2, 2, 4, 16, 256), BF),
            vmem((3, 2, 4, 4, 16, 256), BF),
            vmem((6, 3, 4, 16, 256), BF),
            vmem((3, 2, 4, 16, 256), BF),
            vmem((3, 4, 2, 2, 16, 256), BF),
            vmem((2, 6, 16, 256), F32),
            dma((3,)),
            dma((6, 6)),
            dma((1,)),
            dma((6, 3)),
            dma((4,)),
            dma((4,)),
            dma((8,)),
            dma((8,)),
            dma((1,)),
            dma((1,)),
            dma((15,)),
            dma((3, 4)),
            dma((1,)),
            dma((3, 3)),
            dma((1,)),
            dma((3, 4, 3)),
            dma((1,)),
            dma((1,)),
            dma((11,)),
            dma((11,)),
            dma((1,)),
            dma((1,)),
        ],
        compiler_params=pltpu.CompilerParams(
            collective_id=0, has_side_effects=True, vmem_limit_bytes=56 * 1024 * 1024
        ),
    )(
        embeddings,
        action_ids.reshape(1, -1),
        segment_ids,
        cand_pos.reshape(1, -1),
        owners.reshape(1, -1),
        features,
        action_table,
        w_query,
        w_keys,
        w_out,
        w_head,
        w_cross,
        b_cross,
        w_deep,
        b_deep,
        w_score,
        b_score.reshape(1, -1),
    )
    return pl.pallas_call(
        results,
        out_shape=(
            jax.ShapeDtypeStruct((4, 512), F32),
            jax.ShapeDtypeStruct((4,), F32),
            jax.ShapeDtypeStruct((4, 4096), F32),
            jax.ShapeDtypeStruct((32,), F32),
            jax.ShapeDtypeStruct((32, 128), F32),
            jax.ShapeDtypeStruct((1,), F32),
            jax.ShapeDtypeStruct((512, 128), BF),
        ),
        in_specs=[whole] * 5,
        out_specs=(whole,) * 7,
    )(g_cross, g_deep, g_score, bias, rows.reshape(512, 128))


def solution(mesh):
    both = ("teacher", "student")
    return jax.shard_map(
        local,
        mesh=mesh,
        in_specs=(
            P(both, None),
            P(both),
            P(both, None),
            P(both),
            P(both, None),
            P(both, None),
            P(),
            P("teacher", None),
            P("teacher", None),
            P("teacher", None),
            P(),
            P(),
            P(),
            P(),
            P(),
            P(),
            P(),
        ),
        out_specs=(
            P(both, None),
            P(both),
            P(both, None),
            P(both),
            P(both, None),
            P(both),
            P(both, None),
        ),
        check_vma=False,
    )
```
